32 devices in a mesh: ctx: 16 (over z, x, core), fsdp: 2 (over y).
Axes of the slice: x: 2, y: 2, z: 4, core: 2. Of those that a mesh axis runs over, the one named last changes fastest.
Arguments:
- incoming_sequence: bfloat16 [2, 4096, 768], P('fsdp', 'ctx'), may hold values from -6 to 6
- mixer_scaling_factor: bfloat16 [768], P('fsdp'), may hold values from 0.099609375 to 1.8984375
- asker_lookup_content_maps: bfloat16 [768, 2304], P('fsdp'), may hold values from -0.21875 to 0.21875
- mixer_final_map: bfloat16 [768, 768], P('fsdp'), may hold values from -3.5 to 3.5
- specialist_scaling_factor: bfloat16 [768], P('fsdp'), may hold values from 0.099609375 to 1.8984375
- dispatch_space_map: bfloat16 [768, 16], P('fsdp'), may hold values from -0.0546875 to 0.0546875
- specialist_dispatch_vectors: bfloat16 [16, 16], P('fsdp'), may hold values from -1.5 to 1.5
- specialist_widen_weights_pair: bfloat16 [16, 768, 3072], P('ctx', 'fsdp'), may hold values from -0.21875 to 0.21875
- specialist_shrink_weights_pair: bfloat16 [16, 3072, 768], P('ctx', 'fsdp'), may hold values from -3.5 to 3.5
- document_labels: int32 [2, 4096], P('fsdp', 'ctx'), may hold values from 0 to 7, as said below
- piece_specialist_choice: int32 [2, 4096, 1], P('fsdp', 'ctx'), may hold values from 0 to 15; in each aligned block of 256 rows (0 to 255, 256 to 511, ..., all dimensions but the last counted through in order) at most 32 rows name the same one
- result_cotangent_array: bfloat16 [2, 4096, 768], P('fsdp', 'ctx'), may hold values from -6 to 6
Outputs:
- out: bfloat16 [2, 4096, 768], P('fsdp', 'ctx')
- grad_input: float32 [2, 4096, 768], P('fsdp', 'ctx')
- grad_ln1: float32 [768], P('fsdp')
- grad_qkv: float32 [768, 2304], P('fsdp')
- grad_output_weight: float32 [768, 768], P('fsdp')
- grad_ln2: float32 [768], P('fsdp')
- grad_router: float32 [768, 16], P('fsdp')
- grad_embed: float32 [16, 16], P('fsdp')
- grad_expert_up: float32 [16, 768, 3072], P('ctx', 'fsdp')
- grad_expert_down: float32 [16, 3072, 768], P('ctx', 'fsdp')
The draws below stay inside these ranges and needn't reach their ends.
Inputs may be any that keep to these rules, and one draw needn't show every extreme that they name: `document_labels`: within a sequence the document numbers never fall. In one sequence, chosen by the seed, all tokens form one document; in each other sequence the numbers run through all of 0 to 7. `piece_specialist_choice`: in each aligned block of 256 tokens of a sequence no expert is named by more than 32 tokens, a bound that some block reaches.
All inputs are finite; a program needn't handle non-finite values.
Results may differ from the reference program's by a relative error of at most 0.02.
Values may be sent and summed in bfloat16 or wider, within the bound.
No kernel may reach another device: no remote copies, remote signals or barrier semaphores. Data moves between devices by JAX's collectives and lax.ppermute only.
A program may use at most 256 MiB of HBM per device.

```python
import math
import jax
import jax.numpy as jnp
import numpy as np
from jax import lax

D = 768
H = 12
HD = 64
FF = 3072
ROUTE = 16
TOK_DEV = 256
DOCS = 8
SEQS = 2
LENGTH = 4096
EXPERTS = 16
CAP = 32
N_CTX = 16


def draw_document_labels(key, part):
    key = jax.random.fold_in(key, 11)
    whole_key = jax.random.fold_in(key, 1)
    cut_key = jax.random.fold_in(key, 2)
    single = jax.random.randint(whole_key, (), 0, SEQS)
    positions = jnp.arange(LENGTH, dtype=jnp.int32)
    labels_list = []
    for seq_number in range(SEQS):
        order = jax.random.permutation(jax.random.fold_in(cut_key, seq_number), LENGTH - 1)
        cuts = order[:DOCS - 1].astype(jnp.int32) + 1
        labels = jnp.sum((positions[:, None] >= cuts[None, :]).astype(jnp.int32), axis=1)
        labels = jnp.where(single == seq_number, jnp.zeros_like(labels), labels)
        labels_list.append(labels.astype(jnp.int32))
    return jnp.stack(labels_list, axis=0)


def block_levels(stream_key, extent, cuts, least, top_value):
    factor_of, own = 1.0, jax.random.fold_in(stream_key, 6)
    for axis_at, shards_of in cuts:
        heights = jnp.exp(jax.random.uniform(jax.random.fold_in(own, axis_at), (shards_of,), jnp.float32, least / len(cuts), top_value / len(cuts)))
        factor_of = factor_of * jnp.repeat(heights, extent[axis_at] // shards_of).reshape([-1 if axis == axis_at else 1 for axis in range(len(extent))])
    return factor_of


def assign_block(stream_key, own, number, rows, number_of, top, limit, skew):
    sequence = jax.random.permutation(stream_key, number_of)
    crowded, ordinary = shares(number_of, rows * top, limit, skew, True), shares(number_of, rows * top, limit, skew, False)
    places = jnp.arange(number_of)

    def named(lengths, turn):
        used = int((lengths > 0).sum())
        fixed = max(1, used // 4)
        moved = fixed + (places - fixed + turn * (used - fixed)) % max(1, number_of - fixed)
        return jnp.zeros((number_of,), jnp.int32).at[sequence[jnp.where(places < fixed, places, moved)]].set(jnp.asarray(lengths, jnp.int32))

    lengths = jnp.where(number % 4 == 0, named(crowded, number // 4), named(ordinary, number - number // 4 - 1))
    mixed = jax.random.permutation(jax.random.fold_in(own, 3), number_of)
    donor, receiver = mixed[0:number_of // 2 * 2:2], mixed[1:number_of // 2 * 2:2]
    room = jnp.minimum(lengths[donor] - 1, limit - lengths[receiver]) // 2
    room = jnp.where((donor == sequence[0]) | (receiver == sequence[0]) | (lengths[receiver] == 0), 0, jnp.maximum(room, 0))
    moved = jax.random.randint(jax.random.fold_in(own, 4), (number_of // 2,), 0, 1 << 20) % (room + 1)
    lengths = lengths.at[donor].add(-moved).at[receiver].add(moved)
    items = jnp.searchsorted(jnp.cumsum(lengths), jnp.arange(rows * top), side="right").astype(jnp.int32)
    listing = items.reshape(top, rows).T
    listing = listing[jax.random.permutation(jax.random.fold_in(own, 1), rows)]
    turn = jax.random.randint(jax.random.fold_in(own, 2), (rows, 1), 0, top)
    return jnp.take_along_axis(listing, (jnp.arange(top)[None, :] + turn) % top, axis=1)


def shares(amount, total, most, slope, full):
    loads = [(1 << 20) // math.isqrt(standing ** slope) + 1 for standing in range(1, amount + 1)]
    largest = most if full else min(most, max(-(-total // amount), total * loads[0] // sum(loads)))
    least = 1 if total - largest >= amount - 1 else 0
    given, spare = [largest] + [least] * (amount - 1), total - largest - least * (amount - 1)
    while spare > 0:
        candidates = [i for i in range(1, amount) if given[i] < largest] or [i for i in range(1, amount) if given[i] < most]
        whole, remaining = sum([loads[i] for i in candidates]), spare
        for i in candidates:
            more = min(most - given[i], max(1, remaining * loads[i] // whole), spare)
            given[i] = given[i] + more
            spare = spare - more
    return np.array(given)


def centred(stream_key, shape, width, bound, shards=(), held_as=jnp.bfloat16):
    entries = width * jax.random.normal(stream_key, shape, jnp.float32)
    if shards:
        entries = entries * block_levels(stream_key, shape, shards, -0.22, 0.18)
    return jnp.clip(entries, -bound, bound).astype(held_as)


def setup_inputs(seed: int = 0) -> dict:
    arg_keys = jax.random.split(jax.random.key(seed), 13)
    incoming_sequence = centred(arg_keys[0], (SEQS, LENGTH, D), 1.0, 6.0, ((0, 2), (1, 16)))
    mixer_scaling_factor = jnp.clip(1.0 + 0.18 * jax.random.normal(arg_keys[1], (D,), jnp.float32), 0.099609375, 1.8984375).astype(jnp.bfloat16)
    asker_lookup_content_maps = centred(arg_keys[2], (D, 3 * D), D ** -0.5, 0.21875, ((0, 2),))
    mixer_final_map = centred(arg_keys[3], (D, D), (max(1, D // 256)) ** -0.5, 3.5, ((0, 2),))
    specialist_scaling_factor = jnp.clip(1.0 + 0.18 * jax.random.normal(arg_keys[4], (D,), jnp.float32), 0.099609375, 1.8984375).astype(jnp.bfloat16)
    dispatch_space_map = centred(arg_keys[5], (D, ROUTE), (ROUTE * D) ** -0.5, 0.0546875, ((0, 2),))
    specialist_dispatch_vectors = centred(arg_keys[6], (ROUTE, EXPERTS), 0.25, 1.5, ((0, 2),))
    specialist_widen_weights_pair = centred(arg_keys[7], (EXPERTS, D, FF), D ** -0.5, 0.21875, ((0, 16), (1, 2)))
    specialist_shrink_weights_pair = centred(arg_keys[8], (EXPERTS, FF, D), (2.0 * EXPERTS * FF ** -0.5), 3.5, ((0, 16), (1, 2)))
    document_labels = draw_document_labels(jax.random.fold_in(arg_keys[12], 71), 0)
    piece_specialist_choice_keys = jax.random.split(jax.random.fold_in(arg_keys[10], 1), SEQS * LENGTH // TOK_DEV)
    piece_specialist_choice_turns = jax.random.permutation(jax.random.fold_in(arg_keys[10], 3), SEQS * LENGTH // TOK_DEV)
    piece_specialist_choice = jax.vmap(lambda own, number: assign_block(jax.random.fold_in(arg_keys[10], 2), own, number, TOK_DEV, EXPERTS, 1, CAP, 2))(piece_specialist_choice_keys, piece_specialist_choice_turns).reshape((SEQS, LENGTH, 1))
    result_cotangent_array = centred(arg_keys[11], (SEQS, LENGTH, D), 1.0, 6.0, ((0, 2), (1, 16)))
    return {"incoming_sequence": incoming_sequence, "mixer_scaling_factor": mixer_scaling_factor, "asker_lookup_content_maps": asker_lookup_content_maps, "mixer_final_map": mixer_final_map, "specialist_scaling_factor": specialist_scaling_factor, "dispatch_space_map": dispatch_space_map, "specialist_dispatch_vectors": specialist_dispatch_vectors, "specialist_widen_weights_pair": specialist_widen_weights_pair, "specialist_shrink_weights_pair": specialist_shrink_weights_pair, "document_labels": document_labels, "piece_specialist_choice": piece_specialist_choice, "result_cotangent_array": result_cotangent_array}


@jax.custom_vjp
def low(v):
    return lax.optimization_barrier(v.astype(jnp.bfloat16)).astype(jnp.float32)

@jax.custom_vjp
def low_back(v):
    return v

def low_keep(v):
    return (low(v), None)

def low_pass(kept, grad):
    return (grad,)

def back_keep(v):
    return (v, None)

def back_low(kept, grad):
    return (low(grad),)
low.defvjp(low_keep, low_pass)
low_back.defvjp(back_keep, back_low)
EPSILON = 1e-05
FLOOR = 0.5
ROUTER_HEAT = 0.5
MATMUL_ACCURACY = lax.Precision.HIGHEST
ROOT_HALF = 0.7071067811865476

def layer_norm(values, gain):
    center = values - lax.optimization_barrier(jnp.mean(values, axis=-1, keepdims=True))
    spread = lax.optimization_barrier(jnp.mean(center * center, axis=-1, keepdims=True))
    return center * lax.rsqrt(spread + EPSILON) * gain

def gelu_value(values):
    return 0.5 * values * (1.0 + lax.erf(values * ROOT_HALF))

def route_gate(normed, router, embed_cols, chosen):
    project = jnp.einsum('...d,dr->...r', normed, router, precision=MATMUL_ACCURACY)
    unit_row_vectors = project / jnp.maximum(jnp.sqrt(lax.optimization_barrier(jnp.sum(project * project, axis=-1, keepdims=True))), FLOOR)
    unit_columns = embed_cols / jnp.maximum(jnp.sqrt(lax.optimization_barrier(jnp.sum(embed_cols * embed_cols, axis=0, keepdims=True))), FLOOR)
    router_scores = jnp.einsum('...d,dx->...x', unit_row_vectors, unit_columns, precision=MATMUL_ACCURACY) / ROUTER_HEAT
    shifted = router_scores - lax.optimization_barrier(jnp.max(router_scores, axis=-1, keepdims=True))
    raised = jnp.exp(shifted)
    probs = raised / lax.optimization_barrier(jnp.sum(raised, axis=-1, keepdims=True))
    return lax.optimization_barrier(jnp.sum(probs * chosen, axis=-1))

def attend(queries, key_heads, value_heads, document_labels):
    seq_len = key_heads.shape[1]
    block_rows = math.gcd(seq_len, 512)
    score_scale = 1.0 / math.sqrt(HD)

    def one_block(block_index):
        row_start = block_index * block_rows
        query_rows = lax.dynamic_slice_in_dim(queries, row_start, block_rows, 1)
        query_segs = lax.dynamic_slice_in_dim(document_labels, row_start, block_rows, 1)
        scores = low_back(jnp.einsum('sqhd,skhd->shqk', query_rows, key_heads, precision=MATMUL_ACCURACY) * score_scale)
        allowed = document_labels[:, None, None, :] == query_segs[:, None, :, None]
        masked = jnp.where(allowed, scores, -1e+30)
        raised = jnp.where(allowed, jnp.exp(masked - lax.optimization_barrier(jnp.max(masked, axis=-1, keepdims=True))), 0.0)
        weights = low(raised / lax.optimization_barrier(jnp.sum(raised, axis=-1, keepdims=True)))
        return jnp.einsum('shqk,skhd->sqhd', weights, value_heads, precision=MATMUL_ACCURACY)
    blocks = lax.map(jax.checkpoint(one_block), jnp.arange(seq_len // block_rows, dtype=jnp.int32))
    return jnp.moveaxis(blocks, 0, 1).reshape(queries.shape)

def experts_apply(routed, slot_index, specialist_widen_weights_pair, specialist_shrink_weights_pair):
    slot_total = SEQS * N_CTX * CAP
    buffer = jnp.zeros((EXPERTS * slot_total, D), jnp.float32).at[slot_index].set(routed)
    buffer = buffer.reshape(EXPERTS, slot_total, D)

    def one_expert(packed):
        block_inputs, weight_up, weight_down = packed
        pre_act = low_back(jnp.dot(block_inputs, weight_up, precision=MATMUL_ACCURACY, preferred_element_type=jnp.float32))
        hidden = low(gelu_value(pre_act))
        return low(low_back(jnp.dot(hidden, weight_down, precision=MATMUL_ACCURACY, preferred_element_type=jnp.float32)))
    made = lax.map(jax.checkpoint(one_expert), (buffer, specialist_widen_weights_pair, specialist_shrink_weights_pair))
    return made.reshape(EXPERTS * slot_total, D)[slot_index]

def forward(block_inputs, gain_in, weight_qkv, weight_out, gain_mid, router, embed_cols, specialist_widen_weights_pair, specialist_shrink_weights_pair, document_labels, slot_index, chosen):
    normed_input = low(layer_norm(block_inputs, gain_in))
    joined_heads = low(low_back(jnp.einsum('cyn,nq->cyq', normed_input, weight_qkv, precision=MATMUL_ACCURACY)))
    heads_shape = (SEQS, LENGTH, H, HD)
    queries = joined_heads[..., :D].reshape(heads_shape)
    key_heads = joined_heads[..., D:2 * D].reshape(heads_shape)
    value_heads = joined_heads[..., 2 * D:].reshape(heads_shape)
    context_rows = low(low_back(attend(queries, key_heads, value_heads, document_labels).reshape(SEQS, LENGTH, D)))
    residual_stream = block_inputs + low_back(jnp.einsum('cyn,nq->cyq', context_rows, weight_out, precision=MATMUL_ACCURACY))
    normed_mid = low(layer_norm(residual_stream, gain_mid))
    gate = route_gate(normed_mid, router, embed_cols, chosen)
    routed = low_back(normed_mid).reshape(SEQS * LENGTH, D)
    expert_rows = experts_apply(routed, slot_index, specialist_widen_weights_pair, specialist_shrink_weights_pair).reshape(SEQS, LENGTH, D)
    return residual_stream + gate[..., None] * expert_rows

def reference(incoming_sequence, mixer_scaling_factor, asker_lookup_content_maps, mixer_final_map, specialist_scaling_factor, dispatch_space_map, specialist_dispatch_vectors, specialist_widen_weights_pair, specialist_shrink_weights_pair, document_labels, piece_specialist_choice, result_cotangent_array):
    picked = piece_specialist_choice[..., 0]
    one_hot = (picked[..., None] == jnp.arange(EXPERTS, dtype=jnp.int32)).astype(jnp.int32)
    blocked = one_hot.reshape(SEQS, N_CTX, TOK_DEV, EXPERTS)
    slot_rank = lax.optimization_barrier(jnp.sum(jnp.cumsum(blocked, axis=2) * blocked, axis=-1)) - 1
    seq_ids = jnp.arange(SEQS, dtype=jnp.int32)[:, None, None]
    device_numbering = jnp.arange(N_CTX, dtype=jnp.int32)[None, :, None]
    slot_index = (picked.reshape(SEQS, N_CTX, TOK_DEV) * (SEQS * N_CTX * CAP) + seq_ids * (N_CTX * CAP) + device_numbering * CAP + slot_rank).reshape(-1).astype(jnp.int32)
    chosen = one_hot.astype(jnp.float32)
    real_numbers_list = (incoming_sequence.astype(jnp.float32), mixer_scaling_factor.astype(jnp.float32), asker_lookup_content_maps.astype(jnp.float32), mixer_final_map.astype(jnp.float32), specialist_scaling_factor.astype(jnp.float32), dispatch_space_map.astype(jnp.float32), specialist_dispatch_vectors.astype(jnp.float32), specialist_widen_weights_pair.astype(jnp.float32), specialist_shrink_weights_pair.astype(jnp.float32))

    def closed(block_inputs, gain_in, weight_qkv, weight_out, gain_mid, router, embed_cols, weight_up, weight_down):
        return forward(block_inputs, gain_in, weight_qkv, weight_out, gain_mid, router, embed_cols, weight_up, weight_down, document_labels, slot_index, chosen)
    result, pullback = jax.vjp(closed, *real_numbers_list)
    grads = pullback(result_cotangent_array.astype(jnp.float32))
    return (result.astype(jnp.bfloat16), grads[0], grads[1], grads[2], grads[3], grads[4], grads[5], grads[6], grads[7], grads[8])
```

```python
import functools
import math

import jax
import jax.numpy as jnp
from jax import lax
from jax.experimental import pallas as pl
from jax.experimental.pallas import tpu as pltpu
from jax.sharding import Mesh, PartitionSpec as P

HD = 64
DOCS = 8
AUX = 16
GROUPS = 4
EPSILON = 1e-05
FLOOR = 0.5
ROUTER_HEAT = 0.5
HIGHEST = lax.Precision.HIGHEST
ROOT_HALF = 0.7071067811865476
ROOT_TWO_PI = 2.5066282746310002
NEG_LARGE = -1e30
LOG2E = 1.4426950408889634
VMEM_BYTES = 48 * 1024 * 1024
BF16 = jnp.bfloat16
F32 = jnp.float32


def dot32(left, right, dims):
    return lax.dot_general(left, right, (dims, ((), ())), preferred_element_type=F32)


def forward_kernel(scale2, last, q_ref, oh_ref, k_ref, v_ref, mk_ref, *rest):
    if last:
        top_in, acc_in, out_ref, lse_ref, top_sc, acc_sc = rest
    else:
        top_out, acc_out, top_sc, acc_sc = rest
    step = pl.program_id(1)
    width = k_ref.shape[-1]
    block = min(512, width)
    pad = jnp.zeros((128 - HD - AUX, q_ref.shape[-1]), BF16)
    query = jnp.concatenate([q_ref[...], oh_ref[...], pad], axis=0)

    @pl.when(step == 0)
    def _():
        if last:
            top_sc[...] = top_in[0]
            acc_sc[...] = acc_in[0]
        else:
            top_sc[...] = jnp.full_like(top_sc, NEG_LARGE)
            acc_sc[...] = jnp.zeros_like(acc_sc)

    top, acc = top_sc[...], acc_sc[...]
    for at in range(0, width, block):
        cut = slice(at, at + block)
        aux = mk_ref[0, :, cut]
        keys = jnp.concatenate([k_ref[0, :, cut], aux, pad[:, :block]], axis=0).T
        scores = jnp.dot(keys, query, preferred_element_type=F32)
        new_top = jnp.maximum(top, jnp.max(scores, axis=0, keepdims=True))
        probs = jnp.exp2((scores - new_top) * scale2).astype(BF16)
        decay = jnp.exp2((top - new_top) * scale2)
        values = jnp.concatenate([v_ref[0, :, cut], aux], axis=0)
        acc = acc * decay + jnp.dot(values, probs, preferred_element_type=F32)
        top = new_top
    top_sc[...], acc_sc[...] = top, acc

    @pl.when(step == pl.num_programs(1) - 1)
    def _():
        if last:
            total = acc[HD + DOCS : HD + DOCS + 1]
            out_ref[0] = acc[:HD] / total
            lse_ref[0] = top + jnp.log2(total) / scale2
        else:
            top_out[0] = top
            acc_out[0] = acc


def attend(query_t, onehot, pieces, carry, scale2, heads):
    count, _, width = pieces.shape
    rows = query_t.shape[1]
    last = carry is not None
    q_spec = pl.BlockSpec((HD, rows), lambda h, j: (h, 0))
    top_spec = pl.BlockSpec((1, 1, rows), lambda h, j: (h, 0, 0))
    acc_spec = pl.BlockSpec((1, HD + AUX, rows), lambda h, j: (h, 0, 0))
    in_specs = [
        q_spec,
        pl.BlockSpec((AUX, rows), lambda h, j: (0, 0)),
        pl.BlockSpec((1, HD, width), lambda h, j: (j, h, 0)),
        pl.BlockSpec((1, HD, width), lambda h, j: (j, heads + h, 0)),
        pl.BlockSpec((1, AUX, width), lambda h, j: (j, 2 * heads * HD // AUX, 0)),
    ]
    top_shape = jax.ShapeDtypeStruct((heads, 1, rows), F32)
    if last:
        in_specs += [top_spec, acc_spec]
        out_specs = [pl.BlockSpec((1, HD, rows), lambda h, j: (h, 0, 0)), top_spec]
        out_shape = [jax.ShapeDtypeStruct((heads, HD, rows), F32), top_shape]
    else:
        out_specs = [top_spec, acc_spec]
        out_shape = [top_shape, jax.ShapeDtypeStruct((heads, HD + AUX, rows), F32)]
    pairs = heads * rows * count * width
    return pl.pallas_call(
        functools.partial(forward_kernel, scale2, last),
        grid=(heads, count),
        in_specs=in_specs,
        out_specs=out_specs,
        out_shape=out_shape,
        scratch_shapes=[pltpu.VMEM((1, rows), F32), pltpu.VMEM((HD + AUX, rows), F32)],
        compiler_params=pltpu.CompilerParams(vmem_limit_bytes=VMEM_BYTES),
        cost_estimate=pl.CostEstimate(
            flops=16 * pairs * HD, bytes_accessed=4 * count * width * HD * heads, transcendentals=pairs
        ),
    )(query_t, onehot, pieces, pieces, pieces, *(carry or ()))


def split3(value):
    high = value.astype(BF16)
    rest = value - high.astype(F32)
    mid = rest.astype(BF16)
    return high, mid, (rest - mid.astype(F32)).astype(BF16)


def backward_kernel(
    scale2, q_ref, oh_ref, g_ref, o_ref, lse_ref, k_ref, v_ref, mk_ref, dq_ref, dkv_ref, qa_sc, ga_sc, nat_sc, dq_sc
):
    step = pl.program_id(0)
    width = k_ref.shape[-1]
    block = min(256, width)
    rows = q_ref.shape[-1]
    pad = jnp.zeros((128 - HD - AUX, rows), BF16)

    @pl.when(step == 0)
    def _():
        query, grad = q_ref[...], g_ref[...]
        delta = jnp.sum(grad.astype(F32) * o_ref[0], axis=0, keepdims=True)
        place = lax.broadcasted_iota(jnp.int32, (AUX, rows), 0)

        def aux_rows(start, value):
            out = start
            for at, piece in enumerate(split3(-value)):
                out = jnp.where(place == DOCS + at, piece.astype(F32), out)
            return out.astype(BF16)

        qa_sc[...] = jnp.concatenate([query, aux_rows(oh_ref[...].astype(F32), lse_ref[0]), pad], axis=0)
        ga_sc[...] = jnp.concatenate([grad, aux_rows(jnp.zeros((AUX, rows), F32), delta), pad], axis=0)
        nat_sc[...] = jnp.concatenate([grad, query], axis=0).T
        dq_sc[...] = jnp.zeros_like(dq_sc)

    natural = nat_sc[...]
    for at in range(0, width, block):
        cut = slice(at, at + block)
        aux = mk_ref[0, :, cut]
        keys_t = k_ref[0, :, cut]
        keys = jnp.concatenate([keys_t, aux, pad[:, :block]], axis=0).T
        values = jnp.concatenate([v_ref[0, :, cut], aux, pad[:, :block]], axis=0).T
        probs = jnp.exp2(jnp.dot(keys, qa_sc[...], preferred_element_type=F32) * scale2)
        slopes = jnp.dot(values, ga_sc[...], preferred_element_type=F32)
        grad_scores = (probs * slopes).astype(BF16)
        from_probs = jnp.dot(probs.astype(BF16), natural, preferred_element_type=F32)
        from_scores = jnp.dot(grad_scores, natural, preferred_element_type=F32) * (1.0 / math.sqrt(HD))
        lane = lax.broadcasted_iota(jnp.int32, from_probs.shape, 1)
        dkv_ref[0, :, cut] = jnp.where(lane < HD, from_probs, from_scores).T.astype(BF16)
        dq_sc[...] += jnp.dot(keys_t, grad_scores, preferred_element_type=F32)

    @pl.when(step == pl.num_programs(0) - 1)
    def _():
        dq_ref[...] = (dq_sc[...] * (1.0 / math.sqrt(HD))).astype(BF16)


def attend_back(head, query_t, onehot, grad_t, out_heads, lse, pieces, scale2, heads):
    count, _, width = pieces.shape
    rows = query_t.shape[1]
    pairs = rows * count * width
    return pl.pallas_call(
        functools.partial(backward_kernel, scale2),
        grid=(count,),
        in_specs=[
            pl.BlockSpec((HD, rows), lambda j: (head, 0)),
            pl.BlockSpec((AUX, rows), lambda j: (0, 0)),
            pl.BlockSpec((HD, rows), lambda j: (head, 0)),
            pl.BlockSpec((1, HD, rows), lambda j: (head, 0, 0)),
            pl.BlockSpec((1, 1, rows), lambda j: (head, 0, 0)),
            pl.BlockSpec((1, HD, width), lambda j: (j, head, 0)),
            pl.BlockSpec((1, HD, width), lambda j: (j, heads + head, 0)),
            pl.BlockSpec((1, AUX, width), lambda j: (j, 2 * heads * HD // AUX, 0)),
        ],
        out_specs=[
            pl.BlockSpec((HD, rows), lambda j: (0, 0)),
            pl.BlockSpec((1, 2 * HD, width), lambda j: (j, 0, 0)),
        ],
        out_shape=[
            jax.ShapeDtypeStruct((HD, rows), BF16),
            jax.ShapeDtypeStruct((count, 2 * HD, width), BF16),
        ],
        scratch_shapes=[
            pltpu.VMEM((128, rows), BF16),
            pltpu.VMEM((128, rows), BF16),
            pltpu.VMEM((rows, 128), BF16),
            pltpu.VMEM((HD, rows), F32),
        ],
        compiler_params=pltpu.CompilerParams(vmem_limit_bytes=VMEM_BYTES),
        cost_estimate=pl.CostEstimate(
            flops=40 * pairs * HD, bytes_accessed=8 * count * width * HD, transcendentals=pairs
        ),
    )(query_t, onehot, grad_t, out_heads, lse, pieces, pieces, pieces)


def norm_parts(values):
    center = values - jnp.mean(values, axis=-1, keepdims=True)
    scale = lax.rsqrt(jnp.mean(center * center, axis=-1, keepdims=True) + EPSILON)
    return center * scale, scale


def norm_back(unit, scale, scaled_grad):
    along = jnp.mean(scaled_grad * unit, axis=-1, keepdims=True)
    return scale * (scaled_grad - jnp.mean(scaled_grad, axis=-1, keepdims=True) - unit * along)


def unit_of(vectors, axis):
    size = jnp.sqrt(jnp.sum(vectors * vectors, axis=axis, keepdims=True))
    share = jnp.where(size > FLOOR, 1.0, jnp.where(size == FLOOR, 0.5, 0.0))
    inverse = 1.0 / jnp.maximum(size, FLOOR)
    return vectors * inverse, inverse, share


def unit_back(unit, inverse, share, grad, axis):
    return inverse * (grad - share * unit * jnp.sum(unit * grad, axis=axis, keepdims=True))


def shift(value, axis, size, by):
    return lax.ppermute(value, axis, [(at, (at + by) % size) for at in range(size)])


def flip(value, axis, size, bit):
    return lax.ppermute(value, axis, [(at, at ^ bit) for at in range(size)])


def after(value, *others):
    return lax.optimization_barrier((value, *others))[0]


def line_gather(value, axis, size):
    upward, downward, from_low, from_high = value, value, [], []
    for hop in range(size - 1):
        upward = lax.ppermute(upward, axis, [(at, at + 1) for at in range(hop, size - 1)])
        downward = lax.ppermute(downward, axis, [(at, at - 1) for at in range(size - 1 - hop, 0, -1)])
        from_low.append(upward)
        from_high.append(downward)
    return [value] + [from_low[k] + from_high[size - 2 - k] for k in range(size - 1)]


def roll_blocks(blocks, start):
    return lax.dynamic_slice_in_dim(jnp.concatenate([blocks, blocks], axis=0), start, blocks.shape[0], 0)


def pair_order(own, other, at):
    return jnp.where(at == 0, jnp.concatenate([own, other], 0), jnp.concatenate([other, own], 0))


def body(
    ctx_count,
    fsdp_count,
    incoming_sequence,
    mixer_scaling_factor,
    asker_lookup_content_maps,
    mixer_final_map,
    specialist_scaling_factor,
    dispatch_space_map,
    specialist_dispatch_vectors,
    specialist_widen_weights_pair,
    specialist_shrink_weights_pair,
    document_labels,
    piece_specialist_choice,
    result_cotangent_array,
):
    row_count = incoming_sequence.shape[1]
    width = incoming_sequence.shape[2]
    head_count = width // HD
    heads = head_count // GROUPS
    group_width = heads * HD
    ring = ctx_count // GROUPS
    bits = ring.bit_length() - 1
    scale2 = LOG2E / math.sqrt(HD)
    z_at = lax.axis_index("z")
    r_at = lax.axis_index("r")
    f_at = lax.axis_index("fsdp")
    core = r_at & 1
    expert_at = z_at * ring + r_at
    share = width // fsdp_count
    capacity = max(2, 2 * row_count // ctx_count)
    slots = ctx_count * capacity

    def swap(value):
        return flip(value, "fsdp", fsdp_count, 1)

    def across(value, bit):
        return flip(value, "r", ring, bit)

    def exchange_slots(rows):
        return lax.all_to_all(
            rows.reshape(ctx_count, capacity, -1), ("z", "r"), split_axis=0, concat_axis=0, tiled=True
        ).reshape(slots, -1)

    def other_half(piece):
        part = piece.shape[0] // 2
        got = swap(lax.dynamic_slice_in_dim(piece, core * part, part, 0))
        return pair_order(got, across(got, 1), core)

    x_own = incoming_sequence[0]
    label_rows = jnp.zeros((16, width), BF16).at[0, :row_count].set(document_labels[0].astype(BF16))
    blocks = line_gather(jnp.concatenate([x_own, label_rows], axis=0), "z", GROUPS)
    x_all = jnp.concatenate([piece[:row_count] for piece in blocks], axis=0)
    labels = jnp.concatenate([piece[row_count, :row_count] for piece in blocks], axis=0)

    gains_own = jnp.stack([mixer_scaling_factor, specialist_scaling_factor])
    gains_other = swap(gains_own)
    gains = jnp.where(
        f_at == 0,
        jnp.concatenate([gains_own, gains_other], 1),
        jnp.concatenate([gains_other, gains_own], 1),
    ).astype(F32)
    gain_in, gain_mid = gains[0], gains[1]

    maps = asker_lookup_content_maps.reshape(share, 3, GROUPS, group_width)
    maps_own = lax.dynamic_index_in_dim(maps, z_at, 2, keepdims=False).reshape(share, 3 * group_width)
    maps_other = swap(maps_own)
    maps_group = pair_order(maps_own, maps_other, f_at)
    router = pair_order(dispatch_space_map, swap(dispatch_space_map), f_at)
    embed = pair_order(specialist_dispatch_vectors, swap(specialist_dispatch_vectors), f_at).astype(F32)
    final_other = other_half(after(mixer_final_map, maps_other))
    final_map = pair_order(mixer_final_map, final_other, f_at)
    widen = specialist_widen_weights_pair[0]
    shrink_own = specialist_shrink_weights_pair[0]
    half_ff = shrink_own.shape[0]

    def swap_columns(value):
        return jnp.where(
            f_at == 0, value, jnp.concatenate([value[:, half_ff:], value[:, :half_ff]], axis=1)
        )

    widen_own = swap_columns(widen)
    widen_sent = jnp.concatenate([widen_own[:, half_ff:], widen_own[:, :half_ff]], axis=1)
    widen_other = swap(after(widen_sent, final_other))
    shrink_other = swap(after(shrink_own, widen_other))
    maps_rest = other_half(after(asker_lookup_content_maps, shrink_other))
    maps_full = pair_order(asker_lookup_content_maps, maps_rest, f_at)

    unit_all, _ = norm_parts(x_all.astype(F32))
    normed_low = (unit_all * gain_in).astype(BF16)
    joined_t = dot32(maps_group, normed_low, (((0,), (1,)))).astype(BF16)
    query_t = joined_t[:group_width]
    rows = x_all.shape[0]
    aux_at = jnp.arange(AUX, dtype=jnp.int32)[:, None]
    same = labels.astype(jnp.int32)[None, :] == aux_at
    onehot = same.astype(BF16)
    key_aux = jnp.where(
        aux_at < DOCS, jnp.where(same, 0.0, NEG_LARGE), jnp.where(aux_at < DOCS + 3, 1.0, 0.0)
    ).astype(BF16)
    own_piece = jnp.concatenate([joined_t[group_width:], key_aux], axis=0)[None]
    near = jnp.concatenate([own_piece, across(own_piece, 1)], axis=0)
    evens = own_piece
    for bit in range(bits - 1, 0, -1):
        got = across(evens, 1 << bit)
        evens = jnp.stack([evens, got], axis=1).reshape(-1, *own_piece.shape[1:]) if bit == 1 else jnp.concatenate([evens, got], axis=0)
    far = jnp.stack([evens[1:], across(evens[1:], 1)], axis=1).reshape(-1, *own_piece.shape[1:])

    carry = attend(query_t, onehot, near, None, scale2, heads)
    out_heads, lse = attend(query_t, onehot, far, carry, scale2, heads)
    out_low = out_heads.astype(BF16).reshape(group_width, GROUPS, row_count)
    context_parts = [
        out_low[:, k] if k == 0 else shift(out_low[:, k], "z", GROUPS, -k) for k in range(GROUPS)
    ]
    context_t = roll_blocks(jnp.stack(context_parts), (GROUPS - z_at) % GROUPS).reshape(width, row_count)

    x32 = x_own.astype(F32)
    residual = x32 + dot32(context_t, final_map, (((0,), (0,))))
    unit_mid, scale_mid = norm_parts(residual)
    mid_low = (unit_mid * gain_mid).astype(BF16)
    picked = piece_specialist_choice[0, :, 0]
    hits = (picked[:, None] == jnp.arange(ctx_count, dtype=jnp.int32)[None, :]).astype(jnp.int32)
    slot_rank = jnp.sum(jnp.cumsum(hits, axis=0) * hits, axis=1) - 1
    slot_index = picked * capacity + slot_rank
    place = (jnp.arange(slots, dtype=jnp.int32)[:, None] == slot_index[None, :]).astype(BF16)
    cotangent = result_cotangent_array[0]

    def to_slots(values):
        return jnp.dot(place, values, preferred_element_type=F32).astype(BF16)

    def from_slots(values):
        return dot32(place, values, (((0,), (0,))))

    grad_slots = exchange_slots(to_slots(cotangent))
    arrived = exchange_slots(to_slots(mid_low))

    project = jnp.dot(arrived, router, preferred_element_type=F32)
    unit_rows, inverse_rows, share_rows = unit_of(project, -1)
    unit_columns, inverse_columns, share_columns = unit_of(embed, 0)
    logits = jnp.dot(unit_rows, unit_columns, precision=HIGHEST) / ROUTER_HEAT
    raised = jnp.exp(logits - jnp.max(logits, axis=-1, keepdims=True))
    chances = raised / jnp.sum(raised, axis=-1, keepdims=True)
    mine = (jnp.arange(ctx_count, dtype=jnp.int32) == expert_at).astype(F32)[None, :]
    gate = jnp.sum(chances * mine, axis=-1, keepdims=True)

    first, second = arrived[:, :share], arrived[:, share:]
    rows_own = jnp.where(f_at == 0, first, second)
    rows_other = jnp.where(f_at == 0, second, first)
    pre_act = jnp.dot(rows_own, widen_own, preferred_element_type=F32) + jnp.dot(
        rows_other, widen_other, preferred_element_type=F32
    )
    bell = 0.5 * (1.0 + lax.erf(pre_act * ROOT_HALF))
    hidden = (pre_act * bell).astype(BF16)
    slope = bell + pre_act * jnp.exp(-0.5 * pre_act * pre_act) / ROOT_TWO_PI
    made = (
        jnp.dot(hidden[:, :half_ff], shrink_own, preferred_element_type=F32)
        + jnp.dot(hidden[:, half_ff:], shrink_other, preferred_element_type=F32)
    ).astype(BF16)
    made32, grad32 = made.astype(F32), grad_slots.astype(F32)
    scaled_rows = exchange_slots((gate * made32).astype(BF16))
    grad_made = (gate * grad32).astype(BF16)
    grad_gate = jnp.sum(grad32 * made32, axis=-1, keepdims=True)
    grad_hidden = jnp.concatenate(
        [dot32(grad_made, shrink_own, (((1,), (1,)))), dot32(grad_made, shrink_other, (((1,), (1,))))], axis=1
    )
    grad_pre = (grad_hidden * slope).astype(BF16)
    back_own = dot32(grad_pre, widen_own, (((1,), (1,))))
    back_other = dot32(grad_pre, widen_other, (((1,), (1,))))
    grad_inputs = jnp.where(
        f_at == 0,
        jnp.concatenate([back_own, back_other], axis=1),
        jnp.concatenate([back_other, back_own], axis=1),
    ).astype(BF16)

    grad_logits = grad_gate * gate * (mine - chances) / ROUTER_HEAT
    grad_unit = lax.dot_general(
        grad_logits, unit_columns, (((1,), (1,)), ((), ())), precision=HIGHEST
    )
    grad_project = unit_back(unit_rows, inverse_rows, share_rows, grad_unit, -1)
    grad_columns = lax.dot_general(
        unit_rows, grad_logits, (((0,), (0,)), ((), ())), precision=HIGHEST
    )
    grad_embed_own = unit_back(unit_columns, inverse_columns, share_columns, grad_columns, 0)
    grad_router_own = lax.dot_general(
        grad_project, arrived.astype(F32), (((0,), (0,)), ((), ())), precision=HIGHEST
    )
    grad_route_in = lax.dot_general(
        grad_project, router.astype(F32), (((1,), (1,)), ((), ())), precision=HIGHEST
    )
    grad_back = exchange_slots((grad_inputs.astype(F32) + grad_route_in).astype(BF16))

    grad_widen_other = swap(dot32(rows_other, grad_pre, (((0,), (0,)))).astype(BF16))
    grad_widen_own = dot32(rows_own, grad_pre, (((0,), (0,))))
    grad_shrink_other = swap(
        after(dot32(hidden[:, half_ff:], grad_made, (((0,), (0,)))).astype(BF16), grad_widen_other)
    )
    grad_shrink_own = dot32(hidden[:, :half_ff], grad_made, (((0,), (0,))))

    out = residual + from_slots(scaled_rows)
    grad_mid = from_slots(grad_back)
    grad_residual = cotangent.astype(F32) + norm_back(unit_mid, scale_mid, grad_mid * gain_mid)
    grad_gain_mid = jnp.sum(grad_mid * unit_mid, axis=0)
    grad_res_low = grad_residual.astype(BF16)
    grad_context_t = dot32(final_map, grad_res_low, (((1,), (1,)))).astype(BF16)
    grad_blocks = roll_blocks(grad_context_t.reshape(GROUPS, group_width, row_count), z_at)
    grad_t = jnp.concatenate(
        [grad_blocks[k] if k == 0 else shift(grad_blocks[k], "z", GROUPS, k) for k in range(GROUPS)], axis=1
    )

    pieces = jnp.concatenate([near, far], axis=0)
    grad_query, grad_value, grad_key = [], [], []
    for head in range(heads):
        grad_q, grad_kv = attend_back(head, query_t, onehot, grad_t, out_heads, lse, pieces, scale2, heads)
        for bit in range(bits):
            halves = grad_kv.reshape(-1, 2, *grad_kv.shape[1:])
            moved = across(halves[:, 1], 1 << bit)
            grad_kv = (halves[:, 0].astype(F32) + moved.astype(F32)).astype(BF16)
        grad_query.append(grad_q)
        grad_value.append(grad_kv[0, :HD])
        grad_key.append(grad_kv[0, HD:])
    grad_joined_t = jnp.concatenate(grad_query + grad_key + grad_value, axis=0)

    def halve(value):
        value = value.reshape(2, *([2] * bits), -1, value.shape[-1])
        for bit in range(bits):
            own_bit = (r_at >> bit) & 1
            sent = lax.dynamic_index_in_dim(value, 1 - own_bit, 1, keepdims=False)
            kept = lax.dynamic_index_in_dim(value, own_bit, 1, keepdims=False)
            value = (kept.astype(F32) + across(sent, 1 << bit).astype(F32)).astype(BF16)
        sent = lax.dynamic_index_in_dim(value, 1 - f_at, 0, keepdims=False)
        kept = lax.dynamic_index_in_dim(value, f_at, 0, keepdims=False)
        return kept.astype(F32) + swap(sent).astype(F32)

    def double(value):
        for bit in range(bits - 1, -1, -1):
            own_bit = (r_at >> bit) & 1
            value = pair_order(value, across(value, 1 << bit), own_bit)
        return value

    grad_final_part = halve(dot32(context_t, grad_res_low, (((1,), (0,)))).astype(BF16))
    for bit in (1, 2):
        grad_final_part = grad_final_part + flip(grad_final_part, "z", GROUPS, bit)
    grad_final = double(grad_final_part.astype(BF16)).astype(F32)

    grad_maps_part = halve(
        dot32(normed_low, grad_joined_t, (((0,), (1,)))).astype(BF16)
    ).astype(BF16)
    grad_maps_groups = roll_blocks(
        jnp.stack([grad_maps_part if k == 0 else shift(grad_maps_part, "z", GROUPS, k) for k in range(GROUPS)][::-1]),
        (GROUPS - 1 - z_at) % GROUPS,
    )
    part_rows = grad_maps_part.shape[0]
    grad_maps = (
        double(
            jnp.transpose(grad_maps_groups.reshape(GROUPS, part_rows, 3, group_width), (1, 2, 0, 3)).reshape(
                part_rows, 3 * width
            )
        )
    ).astype(F32)
    grad_ln1 = jnp.sum(grad_maps * asker_lookup_content_maps.astype(F32), axis=1) / mixer_scaling_factor.astype(F32)

    small = jnp.concatenate(
        [
            grad_router_own,
            jnp.pad(grad_embed_own, ((0, 0), (0, width - grad_embed_own.shape[1]))),
            jnp.pad(grad_gain_mid[None], ((0, 7), (0, 0))),
        ],
        axis=0,
    )
    for bit in range(bits):
        small = small + across(small, 1 << bit)
    small = small + swap(small)
    for bit in (1, 2):
        small = small + flip(small, "z", GROUPS, bit)
    route = grad_router_own.shape[0]
    own_columns = lax.dynamic_slice_in_dim(small, f_at * share, share, 1)
    grad_router = own_columns[:route].T
    grad_ln2 = own_columns[2 * route]
    embed_share = route // fsdp_count
    grad_embed = lax.dynamic_slice_in_dim(
        small[route : 2 * route, : grad_embed_own.shape[1]], f_at * embed_share, embed_share, 0
    )

    joined_blocks = grad_joined_t.reshape(3 * group_width, GROUPS, row_count)
    joined_parts = [
        joined_blocks[:, k] if k == 0 else shift(joined_blocks[:, k], "z", GROUPS, -k) for k in range(GROUPS)
    ]
    joined_own = roll_blocks(jnp.stack(joined_parts), (GROUPS - z_at) % GROUPS)
    joined_own = jnp.transpose(
        joined_own.reshape(GROUPS, 3, group_width, row_count), (1, 0, 2, 3)
    ).reshape(3 * width, row_count)
    grad_normed_in = dot32(joined_own, maps_full, (((0,), (1,))))
    unit_in, scale_in = norm_parts(x32)
    grad_input = grad_residual + norm_back(unit_in, scale_in, grad_normed_in * gain_in)

    turned = jnp.concatenate([grad_widen_other[:, half_ff:], grad_widen_other[:, :half_ff]], axis=1)
    grad_up = swap_columns(grad_widen_own + turned.astype(F32))
    grad_down = grad_shrink_own + grad_shrink_other.astype(F32)
    return (
        out[None].astype(BF16),
        grad_input[None],
        grad_ln1,
        grad_maps,
        grad_final,
        grad_ln2,
        grad_router,
        grad_embed,
        grad_up[None],
        grad_down[None],
    )


def solution(mesh):
    ctx_count, fsdp_count = mesh.shape["ctx"], mesh.shape["fsdp"]
    inner = Mesh(mesh.devices.reshape(GROUPS, ctx_count // GROUPS, fsdp_count), ("z", "r", "fsdp"))
    ctx = ("z", "r")
    tokens = P("fsdp", ctx, None)
    expert = P(ctx, "fsdp", None)
    halves, halves2 = P("fsdp"), P("fsdp", None)
    return jax.shard_map(
        functools.partial(body, ctx_count, fsdp_count),
        mesh=inner,
        in_specs=(
            tokens, halves, halves2, halves2, halves, halves2, halves2, expert, expert,
            P("fsdp", ctx), tokens, tokens,
        ),
        out_specs=(
            tokens, tokens, halves, halves2, halves2, halves, halves2, halves2, expert, expert,
        ),
        check_vma=False,
    )
```

```python
import functools
import math

import jax
import jax.numpy as jnp
from jax import lax
from jax.experimental import pallas as pl
from jax.experimental.pallas import tpu as pltpu
from jax.sharding import Mesh, PartitionSpec as P

HD = 64
SMALL = 64
DOCS = 8
AUX = 16
GROUPS = 4
EPSILON = 1e-05
FLOOR = 0.5
ROUTER_HEAT = 0.5
HIGHEST = lax.Precision.HIGHEST
ROOT_HALF = 0.7071067811865476
ROOT_TWO_PI = 2.5066282746310002
NEG_LARGE = -1e30
LOG2E = 1.4426950408889634
VMEM_BYTES = 62 * 1024 * 1024
BF16 = jnp.bfloat16
F32 = jnp.float32


def dot32(left, right, dims):
    return lax.dot_general(left, right, (dims, ((), ())), preferred_element_type=F32)


def dot_high(left, right):
    return lax.dot_general(left, right, (((0,), (0,)), ((), ())), precision=HIGHEST)


def early_kernel(group_width, info, maps_ref, extra_ref, own_ref, sent_ref):
    width = GROUPS * group_width
    for group in range(GROUPS):

        @pl.when(info[0] == group)
        def _():
            begins = [part * width + group * group_width for part in range(3)]
            pieces = [maps_ref[:, begin : begin + group_width] for begin in begins]
            own_ref[...] = jnp.concatenate([*pieces, extra_ref[...]], axis=1)

    half = sent_ref.shape[0]
    sent_ref[...] = own_ref[pl.ds(pl.multiple_of(info[1] * half, 16), half)]


def early_rows(info, maps, extra, group_width):
    rows = maps.shape[0]
    columns = 3 * group_width + extra.shape[1]
    shapes = [(rows, columns), (rows // 2, columns)]
    return pl.pallas_call(
        functools.partial(early_kernel, group_width),
        grid_spec=pltpu.PrefetchScalarGridSpec(
            num_scalar_prefetch=1,
            grid=(1,),
            in_specs=[pl.BlockSpec(value.shape, lambda j, info: (0, 0)) for value in (maps, extra)],
            out_specs=[pl.BlockSpec(shape, lambda j, info: (0, 0)) for shape in shapes],
        ),
        out_shape=[jax.ShapeDtypeStruct(shape, BF16) for shape in shapes],
        compiler_params=pltpu.CompilerParams(vmem_limit_bytes=VMEM_BYTES),
    )(info.astype(jnp.int32), maps, extra)


def forward_kernel(scale2, first, last, q_ref, oh_ref, k_ref, v_ref, mk_ref, *rest):
    if not first:
        top_in, acc_in, *rest = rest
    if last:
        out_ref, low_ref, lse_ref, top_sc, acc_sc = rest
    else:
        top_out, acc_out, top_sc, acc_sc = rest
    step = pl.program_id(1)
    width = k_ref.shape[-1]
    block = min(1024, width)
    pad = jnp.zeros((128 - HD - AUX, q_ref.shape[-1]), BF16)
    query = jnp.concatenate([q_ref[...], oh_ref[...], pad], axis=0)

    @pl.when(step == 0)
    def _():
        if first:
            top_sc[...] = jnp.full_like(top_sc, NEG_LARGE)
            acc_sc[...] = jnp.zeros_like(acc_sc)
        else:
            top_sc[...] = top_in[0]
            acc_sc[...] = acc_in[0]

    top, acc = top_sc[...], acc_sc[...]
    for at in range(0, width, block):
        cut = slice(at, at + block)
        aux = mk_ref[0, :, cut]
        keys = jnp.concatenate([k_ref[0, :, cut], aux, pad[:, :block]], axis=0).T
        scores = jnp.dot(keys, query, preferred_element_type=F32)
        new_top = jnp.maximum(top, jnp.max(scores, axis=0, keepdims=True))
        probs = jnp.exp2((scores - new_top) * scale2).astype(BF16)
        decay = jnp.exp2((top - new_top) * scale2)
        values = jnp.concatenate([v_ref[0, :, cut], aux], axis=0)
        acc = acc * decay + jnp.dot(values, probs, preferred_element_type=F32)
        top = new_top
    top_sc[...], acc_sc[...] = top, acc

    @pl.when(step == pl.num_programs(1) - 1)
    def _():
        if last:
            total = acc[HD + DOCS : HD + DOCS + 1]
            result = acc[:HD] / total
            out_ref[0] = result
            cut = low_ref.shape[-1]
            for at in range(low_ref.shape[0]):
                low_ref[at] = result[:, at * cut : (at + 1) * cut].astype(BF16)
            lse_ref[0] = top + jnp.log2(total) / scale2
        else:
            top_out[0] = top
            acc_out[0] = acc


def attend(query_t, onehot, pieces, carry, last, scale2, heads):
    count, _, width = pieces.shape
    rows = query_t.shape[1]
    cut = rows // GROUPS
    top_spec = pl.BlockSpec((1, 1, rows), lambda h, j: (h, 0, 0))
    acc_spec = pl.BlockSpec((1, HD + AUX, rows), lambda h, j: (h, 0, 0))
    in_specs = [
        pl.BlockSpec((HD, rows), lambda h, j: (h, 0)),
        pl.BlockSpec((AUX, rows), lambda h, j: (0, 0)),
        pl.BlockSpec((1, HD, width), lambda h, j: (j, h, 0)),
        pl.BlockSpec((1, HD, width), lambda h, j: (j, heads + h, 0)),
        pl.BlockSpec((1, AUX, width), lambda h, j: (j, 2 * heads * HD // AUX, 0)),
    ]
    if carry is not None:
        in_specs += [top_spec, acc_spec]
    top_shape = jax.ShapeDtypeStruct((heads, 1, rows), F32)
    if last:
        out_specs = [
            pl.BlockSpec((1, HD, rows), lambda h, j: (h, 0, 0)),
            pl.BlockSpec((GROUPS, HD, cut), lambda h, j: (0, h, 0)),
            top_spec,
        ]
        out_shape = [
            jax.ShapeDtypeStruct((heads, HD, rows), F32),
            jax.ShapeDtypeStruct((GROUPS, heads * HD, cut), BF16),
            top_shape,
        ]
    else:
        out_specs = [top_spec, acc_spec]
        out_shape = [top_shape, jax.ShapeDtypeStruct((heads, HD + AUX, rows), F32)]
    return pl.pallas_call(
        functools.partial(forward_kernel, scale2, carry is None, last),
        grid=(heads, count),
        in_specs=in_specs,
        out_specs=out_specs,
        out_shape=out_shape,
        scratch_shapes=[pltpu.VMEM((1, rows), F32), pltpu.VMEM((HD + AUX, rows), F32)],
        compiler_params=pltpu.CompilerParams(vmem_limit_bytes=VMEM_BYTES),
        cost_estimate=pl.CostEstimate(
            flops=34 * heads * rows * count * width * HD, bytes_accessed=0, transcendentals=0
        ),
    )(query_t, onehot, pieces, pieces, pieces, *(carry or ()))


def split3(value):
    high = value.astype(BF16)
    rest = value - high.astype(F32)
    mid = rest.astype(BF16)
    return high, mid, (rest - mid.astype(F32)).astype(BF16)


def backward_kernel(scale2, first, last, q_ref, oh_ref, g_ref, o_ref, lse_ref, k_ref, v_ref, mk_ref, *rest):
    if not first:
        carry_ref, *rest = rest
    else:
        delta_ref, *rest = rest
    dq_ref, dkv_ref, qa_sc, ga_sc, nat_sc, dq_sc = rest
    step = pl.program_id(1)
    width = k_ref.shape[-1]
    block = width // GROUPS
    rows = q_ref.shape[-1]
    scale = 1.0 / math.sqrt(HD)
    pad = jnp.zeros((128 - HD - AUX, rows), BF16)

    @pl.when(step == 0)
    def _():
        query = q_ref[...]
        grad = jnp.concatenate([g_ref[at] for at in range(g_ref.shape[0])], axis=1)
        if first:
            delta = jnp.sum(grad.astype(F32) * o_ref[0], axis=0, keepdims=True)
            delta_ref[0] = delta
        else:
            delta = o_ref[0]
        place = lax.broadcasted_iota(jnp.int32, (AUX, rows), 0)

        def aux_rows(start, value):
            out = start
            for at, piece in enumerate(split3(-value)):
                out = jnp.where(place == DOCS + at, piece.astype(F32), out)
            return out.astype(BF16)

        qa_sc[...] = jnp.concatenate([query, aux_rows(oh_ref[...].astype(F32), lse_ref[0]), pad], axis=0)
        ga_sc[...] = jnp.concatenate([grad, aux_rows(jnp.zeros((AUX, rows), F32), delta), pad], axis=0)
        nat_sc[...] = jnp.concatenate([grad, query], axis=0).T
        if first:
            dq_sc[...] = jnp.zeros_like(dq_sc)
        else:
            dq_sc[...] = carry_ref[0]

    natural = nat_sc[...]
    for at in range(0, width, block):
        cut = slice(at, at + block)
        aux = mk_ref[0, :, cut]
        keys_t = k_ref[0, :, cut]
        keys = jnp.concatenate([keys_t, aux, pad[:, :block]], axis=0).T
        values = jnp.concatenate([v_ref[0, :, cut], aux, pad[:, :block]], axis=0).T
        probs = jnp.exp2(jnp.dot(keys, qa_sc[...], preferred_element_type=F32) * scale2)
        slopes = jnp.dot(values, ga_sc[...], preferred_element_type=F32)
        grad_scores = (probs * slopes).astype(BF16)
        from_probs = jnp.dot(probs.astype(BF16), natural, preferred_element_type=F32)
        from_scores = jnp.dot(grad_scores, natural, preferred_element_type=F32) * scale
        lane = lax.broadcasted_iota(jnp.int32, from_probs.shape, 1)
        both = jnp.where(lane < HD, from_probs, from_scores).T.astype(BF16)
        dkv_ref[0, at // block, 0] = both[HD:]
        dkv_ref[0, at // block, 1] = both[:HD]
        dq_sc[...] += jnp.dot(keys_t, grad_scores, preferred_element_type=F32)

    @pl.when(step == pl.num_programs(1) - 1)
    def _():
        if last:
            cut = dq_ref.shape[-1]
            for at in range(dq_ref.shape[0]):
                dq_ref[at] = (dq_sc[:, at * cut : (at + 1) * cut] * scale).astype(BF16)
        else:
            dq_ref[0] = dq_sc[...]


def attend_back(query_t, onehot, grad_t, out_heads, lse, pieces, carry, last, scale2, heads):
    count, _, width = pieces.shape
    rows = query_t.shape[1]
    cut = rows // GROUPS
    block = width // GROUPS
    blocks = width // block
    sum_spec = pl.BlockSpec((1, HD, rows), lambda h, j: (h, 0, 0))
    cut_spec = pl.BlockSpec((GROUPS, HD, cut), lambda h, j: (0, h, 0))
    row_spec = pl.BlockSpec((1, 1, rows), lambda h, j: (h, 0, 0))
    in_specs = [
        pl.BlockSpec((HD, rows), lambda h, j: (h, 0)),
        pl.BlockSpec((AUX, rows), lambda h, j: (0, 0)),
        cut_spec,
        sum_spec if carry is None else row_spec,
        row_spec,
        pl.BlockSpec((1, HD, width), lambda h, j: (j, h, 0)),
        pl.BlockSpec((1, HD, width), lambda h, j: (j, heads + h, 0)),
        pl.BlockSpec((1, AUX, width), lambda h, j: (j, 2 * heads * HD // AUX, 0)),
    ]
    if carry is not None:
        in_specs += [sum_spec]
    dq_shape = (GROUPS, heads * HD, cut) if last else (heads, HD, rows)
    return pl.pallas_call(
        functools.partial(backward_kernel, scale2, carry is None, last),
        grid=(heads, count),
        in_specs=in_specs,
        out_specs=([row_spec] if carry is None else [])
        + [
            cut_spec if last else sum_spec,
            pl.BlockSpec((1, blocks, 2, HD, block), lambda h, j: (j, 0, 0, h, 0)),
        ],
        out_shape=([jax.ShapeDtypeStruct((heads, 1, rows), F32)] if carry is None else [])
        + [
            jax.ShapeDtypeStruct(dq_shape, BF16 if last else F32),
            jax.ShapeDtypeStruct((count, blocks, 2, heads * HD, block), BF16),
        ],
        scratch_shapes=[
            pltpu.VMEM((128, rows), BF16),
            pltpu.VMEM((128, rows), BF16),
            pltpu.VMEM((rows, 128), BF16),
            pltpu.VMEM((HD, rows), F32),
        ],
        compiler_params=pltpu.CompilerParams(vmem_limit_bytes=VMEM_BYTES),
        cost_estimate=pl.CostEstimate(
            flops=47 * heads * rows * count * width * HD, bytes_accessed=0, transcendentals=0
        ),
    )(query_t, onehot, grad_t, out_heads, lse, pieces, pieces, pieces, *([] if carry is None else [carry]))


def route_parts(rows, router, columns, expert, expert_count):
    project = jnp.dot(rows, router, preferred_element_type=F32)
    size = jnp.sqrt(jnp.sum(project * project, axis=-1, keepdims=True))
    along = jnp.where(size > FLOOR, 1.0, jnp.where(size == FLOOR, 0.5, 0.0))
    inverse = 1.0 / jnp.maximum(size, FLOOR)
    unit = project * inverse
    logits = jnp.dot(unit, columns, precision=HIGHEST, preferred_element_type=F32) / ROUTER_HEAT
    lane = lax.broadcasted_iota(jnp.int32, logits.shape, 1)
    logits = jnp.where(lane < expert_count, logits, NEG_LARGE)
    raised = jnp.exp(logits - jnp.max(logits, axis=-1, keepdims=True))
    chances = raised / jnp.sum(raised, axis=-1, keepdims=True)
    mine = (lane == expert).astype(F32)
    gate = jnp.sum(chances * mine, axis=-1, keepdims=True)
    return unit, inverse, along, chances, mine, gate


def expert_kernel(first, expert_count, downs, info, x_ref, g_ref, uo_ref, ux0_ref, ux1_ref, *rest):
    down_refs, (router_ref, columns_ref, *rest) = rest[:downs], rest[downs:]
    if first:
        hidden_ref, gp_ref, gm_ref, made_ref, gin_ref, up_sc = rest
    else:
        gm_ref, made_in, gin_in, _, *rest = rest
        hidden_ref, gp_ref, scaled_ref, back_ref, dproj_ref, dlogit_ref, unit_ref, up_sc, made_ref, gin_ref = rest
    step = pl.program_id(0)
    share = uo_ref.shape[0]

    @pl.when(step == 0)
    def _():
        if first:
            gate = route_parts(x_ref[...], router_ref[...], columns_ref[...], info[1], expert_count)[-1]
            gm_ref[...] = (gate * g_ref[...].astype(F32)).astype(BF16)
            made_ref[...] = jnp.zeros_like(made_ref)
            gin_ref[...] = jnp.zeros_like(gin_ref)
        else:
            made_ref[...] = made_in[...]
            gin_ref[...] = gin_in[...]

    up_sc[pl.ds(pl.multiple_of(info[0] * share, 128), share)] = uo_ref[...]
    up_sc[pl.ds(pl.multiple_of((1 - info[0]) * share, 128), share)] = jnp.where(
        step == 0, ux0_ref[...], ux1_ref[...]
    )
    up = up_sc[...]
    if downs == 1:
        down = down_refs[0][...]
    else:
        lower, upper = (jnp.where(step == 0, down_refs[at][...], down_refs[2 + at][...]) for at in range(2))
        down = jnp.concatenate([lower, upper], axis=0)
    pre_act = jnp.dot(x_ref[...], up, preferred_element_type=F32)
    bell = 0.5 * (1.0 + lax.erf(pre_act * ROOT_HALF))
    hidden = (pre_act * bell).astype(BF16)
    hidden_ref[...] = hidden
    made_ref[...] += jnp.dot(hidden, down, preferred_element_type=F32)
    slope = bell + pre_act * (jnp.exp(-0.5 * pre_act * pre_act) * (1.0 / ROOT_TWO_PI))
    grad_hidden = dot32(gm_ref[...], down, (((1,), (1,))))
    grad_pre = (grad_hidden * slope).astype(BF16)
    gp_ref[...] = grad_pre
    gin_ref[...] += dot32(grad_pre, up, (((1,), (1,))))

    if not first:

        @pl.when(step == pl.num_programs(0) - 1)
        def _():
            router, columns = router_ref[...], columns_ref[...]
            unit, inverse, along, chances, mine, gate = route_parts(
                x_ref[...], router, columns, info[1], expert_count
            )
            made = made_ref[...].astype(BF16).astype(F32)
            scaled_ref[...] = (gate * made).astype(BF16)
            grad_gate = jnp.sum(g_ref[...].astype(F32) * made, axis=-1, keepdims=True)
            dlogit = grad_gate * gate * (mine - chances) / ROUTER_HEAT
            dunit = lax.dot_general(
                dlogit, columns, (((1,), (1,)), ((), ())), precision=HIGHEST, preferred_element_type=F32
            )
            dproj = inverse * (dunit - along * unit * jnp.sum(unit * dunit, axis=-1, keepdims=True))
            high = dproj.astype(BF16)
            low = (dproj - high.astype(F32)).astype(BF16)
            back = dot32(high, router, (((1,), (1,)))) + dot32(low, router, (((1,), (1,))))
            back_ref[...] = (gin_ref[...].astype(BF16).astype(F32) + back).astype(BF16)
            dproj_ref[...], dlogit_ref[...], unit_ref[...] = dproj, dlogit, unit


def run_expert(info, rows, grads, widen, widen_other, shrink, routing, carry, expert_count):
    slots, width = rows.shape
    share, units = widen.shape
    block = units // 4
    first = carry is None
    whole = pl.BlockSpec((slots, width), lambda j, info: (0, 0))
    cols = pl.BlockSpec((slots, block), lambda j, info: (0, j))
    cols_at = pl.BlockSpec((slots, block), lambda j, info: (0, 2 * info[2] + j))
    small = pl.BlockSpec((slots, 128), lambda j, info: (0, 0))
    half = jax.ShapeDtypeStruct((slots, units // 2), BF16)
    part = jax.ShapeDtypeStruct((slots, units), BF16)
    low = jax.ShapeDtypeStruct((slots, width), BF16)
    full = jax.ShapeDtypeStruct((slots, width), F32)
    narrow = jax.ShapeDtypeStruct((slots, 128), F32)
    in_specs = [
        whole,
        whole,
        pl.BlockSpec((share, block), lambda j, info: (0, 2 * info[2] + j)),
        *[pl.BlockSpec((share, block), lambda j, info: (0, 0)) for _ in widen_other],
    ]
    if len(shrink) == 1:
        in_specs.append(pl.BlockSpec((block, width), lambda j, info: (j, 0)))
    else:
        in_specs += [pl.BlockSpec((block // 2, width), lambda j, info: (0, 0)) for _ in shrink]
    in_specs += [pl.BlockSpec(value.shape, lambda j, info: (0, 0)) for value in routing]
    operands = [rows, grads, widen, *widen_other, *shrink, *routing]
    scratch = [pltpu.VMEM((width, block), BF16)]
    aliases = {}
    if first:
        out_specs = [cols, cols_at, whole, whole, whole]
        out_shape = [half, part, low, full, full]
    else:
        grad_pre, grad_made, made, grad_inputs = carry
        in_specs += [whole, whole, whole, pl.BlockSpec(memory_space=pl.ANY)]
        operands += [grad_made, made, grad_inputs, grad_pre]
        aliases = {len(operands): 1}
        out_specs = [cols, cols_at, whole, whole, small, small, small]
        out_shape = [half, part, low, low, narrow, narrow, narrow]
        scratch += [pltpu.VMEM((slots, width), F32), pltpu.VMEM((slots, width), F32)]
    return pl.pallas_call(
        functools.partial(expert_kernel, first, expert_count, len(shrink)),
        grid_spec=pltpu.PrefetchScalarGridSpec(
            num_scalar_prefetch=1, grid=(2,), in_specs=in_specs, out_specs=out_specs, scratch_shapes=scratch
        ),
        out_shape=out_shape,
        input_output_aliases=aliases,
        compiler_params=pltpu.CompilerParams(vmem_limit_bytes=VMEM_BYTES),
        cost_estimate=pl.CostEstimate(flops=12 * slots * width * units, bytes_accessed=0, transcendentals=0),
    )(info.astype(jnp.int32), *operands)


def gather_kernel(info, dq_ref, own_ref, got_ref, far0_ref, far1_ref, x_ref, w_ref, f0, f1, f2, f3, small_ref, *rest):
    kept_ref, sent_ref, *part_refs, acc_sc, all_sc = rest
    step = pl.program_id(0)
    group_width = dq_ref.shape[1]
    far = jnp.where(step < GROUPS // 2, far0_ref[0, 0].astype(F32), far1_ref[0, 0].astype(F32))
    grad_kv = (own_ref[0, 0].astype(F32) + got_ref[0, 0].astype(F32) + far).astype(BF16)
    joined = jnp.concatenate([dq_ref[0], grad_kv[0], grad_kv[1]], axis=0)
    product = jnp.dot(joined, x_ref[...], preferred_element_type=F32)

    @pl.when(step == 0)
    def _():
        acc_sc[...] = product

    @pl.when(step > 0)
    def _():
        acc_sc[...] += product

    through = dot32(joined.T, w_ref[...], (((1,), (1,)))).astype(BF16)
    for at in range(GROUPS):

        @pl.when(step == at)
        def _():
            part_refs[at][...] = through

    @pl.when(step == pl.num_programs(0) - 1)
    def _():
        all_sc[: 3 * group_width] = acc_sc[...].astype(BF16)
        total = f0[...].astype(F32) + f1[...].astype(F32) + f2[...].astype(F32) + f3[...].astype(F32)
        all_sc[3 * group_width : 4 * group_width] = total.astype(BF16)
        all_sc[4 * group_width :] = small_ref[...]
        half = kept_ref.shape[0]
        kept_ref[...] = all_sc[pl.ds(pl.multiple_of(info[0] * half, 16), half)]
        sent_ref[...] = all_sc[pl.ds(pl.multiple_of((1 - info[0]) * half, 16), half)]


def gather_grads(core, grad_query, near_own, near_got, far, far_last, normed, maps, finals, small):
    group_width, cut = grad_query.shape[1:]
    width = normed.shape[1]
    total = 4 * group_width + small.shape[0]
    half = GROUPS // 2

    def fixed(shape):
        return pl.BlockSpec(shape, lambda j, info: (0,) * len(shape))

    piece = (1, 1, 2, group_width, cut)
    part = jax.ShapeDtypeStruct((cut, width), BF16)
    return pl.pallas_call(
        gather_kernel,
        grid_spec=pltpu.PrefetchScalarGridSpec(
            num_scalar_prefetch=1,
            grid=(GROUPS,),
            in_specs=[
                pl.BlockSpec((1, group_width, cut), lambda j, info: (j, 0, 0)),
                pl.BlockSpec(piece, lambda j, info: (0, j, 0, 0, 0)),
                pl.BlockSpec(piece, lambda j, info: (0, j, 0, 0, 0)),
                pl.BlockSpec(piece, lambda j, info: (0, jnp.minimum(j, half - 1), 0, 0, 0)),
                pl.BlockSpec(piece, lambda j, info: (0, jnp.maximum(j - half, 0), 0, 0, 0)),
                pl.BlockSpec((cut, width), lambda j, info: (j, 0)),
                fixed(maps.shape),
                *[fixed(value.shape) for value in finals],
                fixed(small.shape),
            ],
            out_specs=[fixed((total // 2, width))] * 2 + [fixed((cut, width))] * GROUPS,
            scratch_shapes=[pltpu.VMEM((3 * group_width, width), F32), pltpu.VMEM((total, width), BF16)],
        ),
        out_shape=[jax.ShapeDtypeStruct((total // 2, width), BF16)] * 2 + [part] * GROUPS,
        compiler_params=pltpu.CompilerParams(vmem_limit_bytes=VMEM_BYTES),
        cost_estimate=pl.CostEstimate(flops=24 * group_width * GROUPS * cut * width, bytes_accessed=0, transcendentals=0),
    )(core[None].astype(jnp.int32), grad_query, near_own, near_got, far, far_last, normed, maps, *finals, small)


def finish_kernel(group_width, info, v_ref, w_ref, maps_ref, final_ref, small_ref, sum_ref):
    def columns(pair, begin):
        rows = pl.ds(begin, group_width)
        halves = [v_ref[lax.rem(2 * pair + k + GROUPS - info[0], GROUPS), rows] for k in range(2)]
        return jnp.concatenate(halves, axis=0).astype(F32).T

    total = 0.0
    for part in range(3):
        for pair in range(GROUPS // 2):
            value = columns(pair, part * group_width)
            at = (part * GROUPS + 2 * pair) * group_width
            cut = slice(at, at + 2 * group_width)
            maps_ref[:, cut] = value
            total = total + jnp.sum(value * w_ref[:, cut].astype(F32), axis=1, keepdims=True)
    sum_ref[...] = total
    for pair in range(GROUPS // 2):
        at = 2 * pair * group_width
        final_ref[:, at : at + 2 * group_width] = columns(pair, 3 * group_width)
    small_ref[...] = sum(v_ref[k, 4 * group_width :].astype(F32) for k in range(GROUPS))


def finish_shared(groups, weights, z_at, group_width):
    rows, columns = weights.shape
    shapes = [(rows, columns), (rows, GROUPS * group_width), (SMALL, rows), (rows, 1)]
    return pl.pallas_call(
        functools.partial(finish_kernel, group_width),
        grid_spec=pltpu.PrefetchScalarGridSpec(
            num_scalar_prefetch=1,
            grid=(1,),
            in_specs=[
                pl.BlockSpec(groups.shape, lambda j, info: (0, 0, 0)),
                pl.BlockSpec(weights.shape, lambda j, info: (0, 0)),
            ],
            out_specs=[pl.BlockSpec(shape, lambda j, info: (0, 0)) for shape in shapes],
        ),
        out_shape=[jax.ShapeDtypeStruct(shape, F32) for shape in shapes],
        compiler_params=pltpu.CompilerParams(vmem_limit_bytes=VMEM_BYTES),
    )(z_at[None].astype(jnp.int32), groups, weights)


def norm_parts(values):
    center = values - jnp.mean(values, axis=-1, keepdims=True)
    scale = lax.rsqrt(jnp.mean(center * center, axis=-1, keepdims=True) + EPSILON)
    return center * scale, scale


def norm_back(unit, scale, scaled_grad):
    along = jnp.mean(scaled_grad * unit, axis=-1, keepdims=True)
    return scale * (scaled_grad - jnp.mean(scaled_grad, axis=-1, keepdims=True) - unit * along)


def unit_of(vectors, axis):
    size = jnp.sqrt(jnp.sum(vectors * vectors, axis=axis, keepdims=True))
    share = jnp.where(size > FLOOR, 1.0, jnp.where(size == FLOOR, 0.5, 0.0))
    inverse = 1.0 / jnp.maximum(size, FLOOR)
    return vectors * inverse, inverse, share


def unit_back(unit, inverse, share, grad, axis):
    return inverse * (grad - share * unit * jnp.sum(unit * grad, axis=axis, keepdims=True))


def shift(value, axis, size, by):
    return lax.ppermute(value, axis, [(at, (at + by) % size) for at in range(size)])


def flip(value, axis, size, bit):
    return lax.ppermute(value, axis, [(at, at ^ bit) for at in range(size)])


def after(value, *others):
    return lax.optimization_barrier((value, *others))[0]


def line_gather(value, axis, size, tied):
    upward, downward, from_low, from_high = value, value, [], []
    for hop in range(size - 1):
        upward = tied(hop, upward)
        upward = lax.ppermute(upward, axis, [(at, at + 1) for at in range(hop, size - 1)])
        downward = lax.ppermute(downward, axis, [(at, at - 1) for at in range(size - 1 - hop, 0, -1)])
        from_low.append(upward)
        from_high.append(downward)
    return [value] + [from_low[k] + from_high[size - 2 - k] for k in range(size - 1)]


def roll_blocks(blocks, start):
    return lax.dynamic_slice_in_dim(jnp.concatenate([blocks, blocks], axis=0), start, blocks.shape[0], 0)


def pair_order(own, other, at):
    return jnp.where(at == 0, jnp.concatenate([own, other], 0), jnp.concatenate([other, own], 0))


def body(
    ctx_count,
    fsdp_count,
    incoming_sequence,
    mixer_scaling_factor,
    asker_lookup_content_maps,
    mixer_final_map,
    specialist_scaling_factor,
    dispatch_space_map,
    specialist_dispatch_vectors,
    specialist_widen_weights_pair,
    specialist_shrink_weights_pair,
    document_labels,
    piece_specialist_choice,
    result_cotangent_array,
):
    row_count = incoming_sequence.shape[1]
    width = incoming_sequence.shape[2]
    head_count = width // HD
    heads = head_count // GROUPS
    group_width = heads * HD
    ring = ctx_count // GROUPS
    bits = ring.bit_length() - 1
    scale2 = LOG2E / math.sqrt(HD)
    z_at = lax.axis_index("z")
    r_at = lax.axis_index("r")
    f_at = lax.axis_index("fsdp")
    core = r_at & 1
    expert_at = z_at * ring + r_at
    share = width // fsdp_count
    capacity = max(2, 2 * row_count // ctx_count)
    slots = ctx_count * capacity

    def swap(value):
        return flip(value, "fsdp", fsdp_count, 1)

    def across(value, bit):
        return flip(value, "r", ring, bit)

    def exchange_slots(rows):
        return lax.all_to_all(
            rows.reshape(ctx_count, capacity, -1), ("z", "r"), split_axis=0, concat_axis=0, tiled=True
        ).reshape(slots, -1)

    def both_cores(got):
        return pair_order(got, across(got, 1), core)

    def halve(value, axis, flag, send):
        half = value.shape[axis] // 2
        kept = lax.dynamic_slice_in_dim(value, flag * half, half, axis)
        sent = lax.dynamic_slice_in_dim(value, (1 - flag) * half, half, axis)
        return (kept.astype(F32) + send(sent).astype(F32)).astype(BF16)

    def by_fsdp(own, other, axis):
        return jnp.where(
            f_at == 0,
            jnp.concatenate([own, other], axis=axis),
            jnp.concatenate([other, own], axis=axis),
        )

    route, experts = specialist_dispatch_vectors.shape[0] * fsdp_count, specialist_dispatch_vectors.shape[1]
    embed_share = route // fsdp_count
    extras = [
        mixer_scaling_factor[:, None],
        specialist_scaling_factor[:, None],
        dispatch_space_map,
        jnp.pad(specialist_dispatch_vectors, ((0, share - embed_share), (0, 0))),
    ]
    edges = [0, 3 * group_width]
    for value in extras:
        edges.append(edges[-1] + value.shape[1])
    extras.append(jnp.zeros((share, -edges[-1] % 128), BF16))
    early_own, early_sent = early_rows(
        jnp.stack([z_at, core]), asker_lookup_content_maps, jnp.concatenate(extras, axis=1), group_width
    )
    half = share // 2
    final_sent = lax.dynamic_slice_in_dim(mixer_final_map, core * half, half, 0)

    widen = specialist_widen_weights_pair[0]
    shrink_own = specialist_shrink_weights_pair[0]
    half_ff = shrink_own.shape[0]
    part_ff = half_ff // 2
    small_ff = half_ff // 4
    early_pieces = []

    def send_widen(which, at, *others):
        begin = (which * 2 + at) * part_ff
        return swap(lax.dynamic_slice_in_dim(after(widen, *others), begin, part_ff, 1))

    def tie(value, pieces, at):
        value, pieces[at] = lax.optimization_barrier((value, pieces[at]))
        return value

    def hop_tie(hop, value):
        if hop == 1:
            value, *sent = lax.optimization_barrier((value, early_sent, final_sent))
            early_pieces.extend([swap(piece) for piece in sent])
        return value

    x_own = incoming_sequence[0]
    label_rows = jnp.zeros((16, width), BF16).at[0, :row_count].set(document_labels[0].astype(BF16))
    blocks = line_gather(jnp.concatenate([x_own, label_rows], axis=0), "z", GROUPS, hop_tie)
    x_all = jnp.concatenate([piece[:row_count] for piece in blocks], axis=0)
    labels = jnp.concatenate([piece[row_count, :row_count] for piece in blocks], axis=0)

    widen_near = [send_widen(1 - f_at, at, *early_pieces) for at in range(2)]
    widen_far = [send_widen(f_at, at, *early_pieces) for at in range(2)]
    shrink_other = [swap(shrink_own[at * small_ff : (at + 1) * small_ff]) for at in range(4)]
    early_full = pair_order(early_own, both_cores(early_pieces[0]), f_at)
    maps_group, gain_in, gain_mid, router, embed = (
        early_full[:, begin:end] for begin, end in zip(edges[:-1], edges[1:])
    )
    gain_in, gain_mid = gain_in[:, 0].astype(F32), gain_mid[:, 0].astype(F32)
    embed = embed.reshape(fsdp_count, share, experts)[:, :embed_share].reshape(route, experts).astype(F32)
    final_map = roll_blocks(
        pair_order(mixer_final_map, both_cores(early_pieces[1]), f_at).reshape(GROUPS, group_width, width), z_at
    ).reshape(width, width)

    picked = piece_specialist_choice[0, :, 0]
    hits = (picked[:, None] == jnp.arange(ctx_count, dtype=jnp.int32)[None, :]).astype(jnp.int32)
    slot_rank = jnp.sum(jnp.cumsum(hits, axis=0) * hits, axis=1) - 1
    slot_index = picked * capacity + slot_rank
    place = (jnp.arange(slots, dtype=jnp.int32)[:, None] == slot_index[None, :]).astype(BF16)
    cotangent = result_cotangent_array[0]

    def to_slots(values):
        return jnp.dot(place, values, preferred_element_type=F32).astype(BF16)

    x_all = tie(x_all, widen_near, 0)
    x_all, final_map, grad_rows = lax.optimization_barrier((x_all, final_map, to_slots(cotangent)))
    unit_all, _ = norm_parts(x_all.astype(F32))
    normed_low = (unit_all * gain_in).astype(BF16)
    joined_t = dot32(maps_group, normed_low, (((0,), (1,)))).astype(BF16)
    aux_at = jnp.arange(AUX, dtype=jnp.int32)[:, None]
    same = labels.astype(jnp.int32)[None, :] == aux_at
    onehot = same.astype(BF16)
    key_aux = jnp.where(
        aux_at < DOCS, jnp.where(same, 0.0, NEG_LARGE), jnp.where(aux_at < DOCS + 3, 1.0, 0.0)
    ).astype(BF16)
    own_piece = jnp.concatenate([joined_t[group_width:], key_aux], axis=0)[None]
    even = own_piece
    for bit in range(bits - 1, 0, -1):
        even = jnp.stack([even, across(even, 1 << bit)], axis=1).reshape(-1, *own_piece.shape[1:])
    even = even[1:]
    peer_piece = across(own_piece, 1)
    carry = attend(joined_t, onehot, own_piece, None, False, scale2, heads)
    carry = attend(joined_t, onehot, peer_piece, carry, False, scale2, heads)
    even = tie(tie(after(even, carry[0]), widen_near, 1), widen_far, 0)
    odd = across(even, 1)
    carry = attend(joined_t, onehot, even, carry, False, scale2, heads)
    out_heads, out_low, lse = attend(joined_t, onehot, odd, carry, True, scale2, heads)
    out_low = tie(out_low, widen_far, 1)
    context_t = jnp.concatenate(
        [out_low[0]] + [shift(out_low[k], "z", GROUPS, -k) for k in range(1, GROUPS)], axis=0
    )

    context_t = tie(context_t, shrink_other, 0)
    x32 = x_own.astype(F32)
    residual = x32 + dot32(context_t, final_map, (((0,), (0,))))
    unit_mid, scale_mid = norm_parts(residual)
    mid_low = (unit_mid * gain_mid).astype(BF16)
    def from_slots(values):
        return dot32(place, values, (((0,), (0,))))

    grad_slots = exchange_slots(after(grad_rows, peer_piece))
    sent_rows, grad_slots = lax.optimization_barrier((to_slots(mid_low), grad_slots))
    arrived = exchange_slots(sent_rows)

    unit_columns, inverse_columns, share_columns = unit_of(embed, 0)
    routing = (
        jnp.pad(router, ((0, 0), (0, 128 - route))),
        jnp.pad(unit_columns, ((0, 128 - route), (0, 128 - experts))),
    )

    hidden_own, *partial = run_expert(
        jnp.stack([f_at, expert_at, f_at]), arrived, grad_slots, widen, widen_near, [shrink_own], routing, None, experts
    )
    grad_made = partial[1]
    hidden_other, grad_pre, scaled, sent_back, dproj, dlogit, unit_rows = run_expert(
        jnp.stack([f_at, expert_at, 1 - f_at]), arrived, grad_slots, widen, widen_far, shrink_other, routing, partial,
        experts,
    )
    grad_back = exchange_slots(sent_back)

    arrived, hidden_own, hidden_other, grad_made, _ = lax.optimization_barrier(
        (arrived, hidden_own, hidden_other, grad_made, sent_back)
    )
    first, second = arrived[:, :share], arrived[:, share:]
    rows_own = jnp.where(f_at == 0, first, second)
    rows_other = jnp.where(f_at == 0, second, first)
    widen_back = swap(dot32(rows_other, grad_pre, (((0,), (0,)))).astype(BF16))
    shrink_back = [
        dot32(hidden_other[:, at * part_ff : (at + 1) * part_ff], grad_made, (((0,), (0,)))).astype(BF16)
        for at in range(2)
    ]
    grad_router_own = dot_high(dproj, arrived.astype(F32))[:route]
    grad_columns = dot_high(unit_rows, dlogit)[:route, :experts]
    grad_embed_own = unit_back(unit_columns, inverse_columns, share_columns, grad_columns, 0)
    grad_back, grad_embed_own, grad_router_own, *shrink_back = lax.optimization_barrier(
        (grad_back, grad_embed_own, grad_router_own, *shrink_back)
    )
    shrink_back[0] = swap(shrink_back[0])

    grad_mid = from_slots(grad_back)
    grad_residual = cotangent.astype(F32) + norm_back(unit_mid, scale_mid, grad_mid * gain_mid)
    grad_gain_mid = jnp.sum(grad_mid * unit_mid, axis=0)
    grad_res_low = grad_residual.astype(BF16)
    grad_context = dot32(final_map, grad_res_low, (((1,), (1,)))).astype(BF16).reshape(
        GROUPS, group_width, row_count
    )
    grad_parts = [grad_context[0]] + [shift(grad_context[k], "z", GROUPS, k) for k in range(1, GROUPS)]
    grad_t = jnp.stack(grad_parts)

    context_rows = roll_blocks(
        context_t.reshape(GROUPS, group_width, row_count), (GROUPS - z_at) % GROUPS
    ).reshape(width, row_count)
    grad_final_own = dot32(after(grad_res_low, grad_parts[1]), context_rows, (((0,), (1,)))).astype(BF16)
    grad_final_own = roll_blocks(grad_final_own.reshape(GROUPS, width // GROUPS, width), z_at)
    embed_rows = jnp.pad(
        grad_embed_own.reshape(fsdp_count, embed_share, experts), ((0, 0), (0, 0), (0, share - experts))
    )
    small = jnp.concatenate(
        [
            grad_router_own,
            jnp.concatenate([embed_rows[at] for at in range(fsdp_count)], axis=1),
            grad_gain_mid[None],
            jnp.zeros((SMALL - route - embed_share - 1, width), F32),
        ],
        axis=0,
    ).astype(BF16)

    def back(piece, running, last=False, ties=()):
        tied = lax.optimization_barrier((grad_t, *ties))
        rows = out_heads if running is None else delta
        result = attend_back(joined_t, onehot, tied[0], rows, lse, piece, running, last, scale2, heads)
        return (*result, *tied[1:])

    scaled_back = exchange_slots(after(scaled, grad_parts[1]))
    final_parts = [shift(grad_final_own[k], "z", GROUPS, k) for k in range(1, GROUPS)]
    delta, running, far_odd = back(odd, None)
    running, far_even = back(even, running)
    far = (far_even.astype(F32) + across(far_odd, 1).astype(F32)).astype(BF16)
    far = jnp.concatenate([jnp.zeros_like(far[:1]), far], axis=0)
    cut = far.shape[1] // 2

    def add_far(value):
        for bit in range(1, bits):
            halves = value.reshape(-1, 2, *value.shape[1:])
            value = (halves[:, 0].astype(F32) + across(halves[:, 1], 1 << bit).astype(F32)).astype(BF16)
        return value

    far, far_last = far[:, :cut], far[:, cut:]
    running, near_peer, far, far_last, final_parts[0] = back(
        peer_piece, running, ties=(far, far_last, final_parts[0])
    )
    far = add_far(far)
    far_last = add_far(after(far_last, running))
    grad_query, near_own, far, widen_back, final_parts[1] = back(
        own_piece, running, True, ties=(far, widen_back, final_parts[1])
    )
    grad_query, shrink_back[0], scaled_back = lax.optimization_barrier((grad_query, shrink_back[0], scaled_back))

    kept, sent, *grad_parts = gather_grads(
        core, grad_query, near_own, across(near_peer, 1), far, far_last, normed_low, maps_group,
        [grad_final_own[0], *final_parts], small,
    )
    grad_maps_part = (kept.astype(F32) + across(sent, 1).astype(F32)).astype(BF16)
    first_part = shift(grad_parts[1], "z", GROUPS, -1)
    for bit in range(1, bits):
        grad_maps_part = halve(grad_maps_part, 0, (r_at >> bit) & 1, lambda v: across(v, 1 << bit))
    second_part = shift(grad_parts[2], "z", GROUPS, -2)
    scaled_back, _ = lax.optimization_barrier((scaled_back, grad_maps_part))
    out = residual + from_slots(scaled_back)
    grad_maps_part = halve(grad_maps_part, 1, f_at, swap)
    grad_maps_part, first_part, second_part = lax.optimization_barrier((grad_maps_part, first_part, second_part))
    grad_maps = jnp.stack(
        [grad_maps_part] + [shift(grad_maps_part, "z", GROUPS, -k) for k in range(1, GROUPS)]
    )
    third_part = shift(after(grad_parts[3], grad_maps), "z", GROUPS, -3)
    shrink_back[1] = swap(after(shrink_back[1], grad_maps_part))


    def double(value, axis):
        for bit in range(bits - 1, -1, -1):
            got = across(value, 1 << bit)
            value = jnp.where(
                (r_at >> bit) & 1 == 0,
                jnp.concatenate([value, got], axis=axis),
                jnp.concatenate([got, value], axis=axis),
            )
        return value

    grad_maps, grad_final, small, grad_ln1 = finish_shared(
        double(grad_maps, 1), asker_lookup_content_maps, z_at, group_width
    )
    grad_ln1 = grad_ln1[:, 0] / mixer_scaling_factor.astype(F32)
    grad_router, grad_embed, grad_ln2 = small[:route].T, small[route : route + embed_share, :experts], small[route + embed_share]

    grad_normed_in = sum(part.astype(F32) for part in (grad_parts[0], first_part, second_part, third_part))
    unit_in, scale_in = norm_parts(x32)
    grad_input = grad_residual + norm_back(unit_in, scale_in, grad_normed_in * gain_in)

    grad_up = dot32(rows_own, grad_pre, (((0,), (0,)))) + after(widen_back, grad_maps_part).astype(F32)
    grad_down = dot32(hidden_own, grad_made, (((0,), (0,)))) + jnp.concatenate(
        shrink_back, axis=0
    ).astype(F32)
    return (
        out[None].astype(BF16),
        grad_input[None],
        grad_ln1,
        grad_maps,
        grad_final,
        grad_ln2,
        grad_router,
        grad_embed,
        grad_up[None],
        grad_down[None],
    )


def solution(mesh):
    ctx_count, fsdp_count = mesh.shape["ctx"], mesh.shape["fsdp"]
    inner = Mesh(mesh.devices.reshape(GROUPS, ctx_count // GROUPS, fsdp_count), ("z", "r", "fsdp"))
    ctx = ("z", "r")
    tokens = P("fsdp", ctx, None)
    expert = P(ctx, "fsdp", None)
    halves, halves2 = P("fsdp"), P("fsdp", None)
    return jax.shard_map(
        functools.partial(body, ctx_count, fsdp_count),
        mesh=inner,
        in_specs=(
            tokens, halves, halves2, halves2, halves, halves2, halves2, expert, expert,
            P("fsdp", ctx), tokens, tokens,
        ),
        out_specs=(
            tokens, tokens, halves, halves2, halves2, halves, halves2, halves2, expert, expert,
        ),
        check_vma=False,
    )
```

```python
import functools
import math

import jax
import jax.numpy as jnp
from jax import lax
from jax.experimental import pallas as pl
from jax.experimental.pallas import tpu as pltpu
from jax.sharding import Mesh, PartitionSpec as P

HD = 64
SMALL = 64
DOCS = 8
AUX = 16
GROUPS = 4
EPSILON = 1e-05
FLOOR = 0.5
ROUTER_HEAT = 0.5
HIGHEST = lax.Precision.HIGHEST
ROOT_HALF = 0.7071067811865476
ROOT_TWO_PI = 2.5066282746310002
NEG_LARGE = -1e30
LOG2E = 1.4426950408889634
VMEM_BYTES = 62 * 1024 * 1024
VMEM_SHARED = 48 * 1024 * 1024
BF16 = jnp.bfloat16
F32 = jnp.float32


def dot32(left, right, dims):
    return lax.dot_general(left, right, (dims, ((), ())), preferred_element_type=F32)


def dot_high(left, right):
    return lax.dot_general(left, right, (((0,), (0,)), ((), ())), precision=HIGHEST)


def early_kernel(group_width, info, maps_ref, extra_ref, own_ref, sent_ref):
    width = GROUPS * group_width
    for group in range(GROUPS):

        @pl.when(info[0] == group)
        def _():
            begins = [part * width + group * group_width for part in range(3)]
            pieces = [maps_ref[:, begin : begin + group_width] for begin in begins]
            own_ref[...] = jnp.concatenate([*pieces, extra_ref[...]], axis=1)

    half = sent_ref.shape[0]
    sent_ref[...] = own_ref[pl.ds(pl.multiple_of(info[1] * half, 16), half)]


def early_rows(info, maps, extra, group_width):
    rows = maps.shape[0]
    columns = 3 * group_width + extra.shape[1]
    shapes = [(rows, columns), (rows // 2, columns)]
    return pl.pallas_call(
        functools.partial(early_kernel, group_width),
        grid_spec=pltpu.PrefetchScalarGridSpec(
            num_scalar_prefetch=1,
            grid=(1,),
            in_specs=[pl.BlockSpec(value.shape, lambda j, info: (0, 0)) for value in (maps, extra)],
            out_specs=[pl.BlockSpec(shape, lambda j, info: (0, 0)) for shape in shapes],
        ),
        out_shape=[jax.ShapeDtypeStruct(shape, BF16) for shape in shapes],
        compiler_params=pltpu.CompilerParams(vmem_limit_bytes=VMEM_BYTES),
    )(info.astype(jnp.int32), maps, extra)


def forward_kernel(scale2, first, last, q_ref, oh_ref, k_ref, v_ref, mk_ref, *rest):
    if not first:
        top_in, acc_in, *rest = rest
    if last:
        out_ref, *low_refs, lse_ref, top_sc, acc_sc = rest
    else:
        top_out, acc_out, top_sc, acc_sc = rest
    step = pl.program_id(1)
    width = k_ref.shape[-1]
    block = min(1024, width)
    pad = jnp.zeros((128 - HD - AUX, q_ref.shape[-1]), BF16)
    query = jnp.concatenate([q_ref[...], oh_ref[...], pad], axis=0)

    @pl.when(step == 0)
    def _():
        if first:
            top_sc[...] = jnp.full_like(top_sc, NEG_LARGE)
            acc_sc[...] = jnp.zeros_like(acc_sc)
        else:
            top_sc[...] = top_in[0]
            acc_sc[...] = acc_in[0]

    top, acc = top_sc[...], acc_sc[...]
    for at in range(0, width, block):
        cut = slice(at, at + block)
        aux = mk_ref[0, :, cut]
        keys = jnp.concatenate([k_ref[0, :, cut], aux, pad[:, :block]], axis=0).T
        scores = jnp.dot(keys, query, preferred_element_type=F32)
        new_top = jnp.maximum(top, jnp.max(scores, axis=0, keepdims=True))
        probs = jnp.exp2((scores - new_top) * scale2).astype(BF16)
        decay = jnp.exp2((top - new_top) * scale2)
        values = jnp.concatenate([v_ref[0, :, cut], aux], axis=0)
        acc = acc * decay + jnp.dot(values, probs, preferred_element_type=F32)
        top = new_top
    top_sc[...], acc_sc[...] = top, acc

    @pl.when(step == pl.num_programs(1) - 1)
    def _():
        if last:
            total = acc[HD + DOCS : HD + DOCS + 1]
            result = acc[:HD] / total
            out_ref[0] = result
            cut = low_refs[0].shape[-1]
            for at, low_ref in enumerate(low_refs):
                low_ref[...] = result[:, at * cut : (at + 1) * cut].astype(BF16)
            lse_ref[0] = top + jnp.log2(total) / scale2
        else:
            top_out[0] = top
            acc_out[0] = acc


def attend(query_t, onehot, pieces, carry, last, scale2, heads):
    count, _, width = pieces.shape
    rows = query_t.shape[1]
    cut = rows // GROUPS
    top_spec = pl.BlockSpec((1, 1, rows), lambda h, j: (h, 0, 0))
    acc_spec = pl.BlockSpec((1, HD + AUX, rows), lambda h, j: (h, 0, 0))
    in_specs = [
        pl.BlockSpec((HD, rows), lambda h, j: (h, 0)),
        pl.BlockSpec((AUX, rows), lambda h, j: (0, 0)),
        pl.BlockSpec((1, HD, width), lambda h, j: (j, h, 0)),
        pl.BlockSpec((1, HD, width), lambda h, j: (j, heads + h, 0)),
        pl.BlockSpec((1, AUX, width), lambda h, j: (j, 2 * heads * HD // AUX, 0)),
    ]
    if carry is not None:
        in_specs += [top_spec, acc_spec]
    top_shape = jax.ShapeDtypeStruct((heads, 1, rows), F32)
    if last:
        out_specs = [
            pl.BlockSpec((1, HD, rows), lambda h, j: (h, 0, 0)),
            *[pl.BlockSpec((HD, cut), lambda h, j: (h, 0))] * GROUPS,
            top_spec,
        ]
        out_shape = [
            jax.ShapeDtypeStruct((heads, HD, rows), F32),
            *[jax.ShapeDtypeStruct((heads * HD, cut), BF16)] * GROUPS,
            top_shape,
        ]
    else:
        out_specs = [top_spec, acc_spec]
        out_shape = [top_shape, jax.ShapeDtypeStruct((heads, HD + AUX, rows), F32)]
    return pl.pallas_call(
        functools.partial(forward_kernel, scale2, carry is None, last),
        grid=(heads, count),
        in_specs=in_specs,
        out_specs=out_specs,
        out_shape=out_shape,
        scratch_shapes=[pltpu.VMEM((1, rows), F32), pltpu.VMEM((HD + AUX, rows), F32)],
        compiler_params=pltpu.CompilerParams(vmem_limit_bytes=VMEM_SHARED),
        cost_estimate=pl.CostEstimate(
            flops=34 * heads * rows * count * width * HD, bytes_accessed=0, transcendentals=0
        ),
    )(query_t, onehot, pieces, pieces, pieces, *(carry or ()))


def split3(value):
    high = value.astype(BF16)
    rest = value - high.astype(F32)
    mid = rest.astype(BF16)
    return high, mid, (rest - mid.astype(F32)).astype(BF16)


def backward_kernel(scale2, first, last, q_ref, oh_ref, g_ref, o_ref, lse_ref, k_ref, v_ref, mk_ref, *rest):
    if not first:
        carry_ref, *rest = rest
    else:
        delta_ref, *rest = rest
    dq_ref, dkv_ref, qa_sc, ga_sc, nat_sc, dq_sc = rest
    step = pl.program_id(1)
    width = k_ref.shape[-1]
    block = width // GROUPS
    rows = q_ref.shape[-1]
    scale = 1.0 / math.sqrt(HD)
    pad = jnp.zeros((128 - HD - AUX, rows), BF16)

    @pl.when(step == 0)
    def _():
        query = q_ref[...]
        grad = jnp.concatenate([g_ref[at] for at in range(g_ref.shape[0])], axis=1)
        if first:
            delta = jnp.sum(grad.astype(F32) * o_ref[0], axis=0, keepdims=True)
            delta_ref[0] = delta
        else:
            delta = o_ref[0]
        place = lax.broadcasted_iota(jnp.int32, (AUX, rows), 0)

        def aux_rows(start, value):
            out = start
            for at, piece in enumerate(split3(-value)):
                out = jnp.where(place == DOCS + at, piece.astype(F32), out)
            return out.astype(BF16)

        qa_sc[...] = jnp.concatenate([query, aux_rows(oh_ref[...].astype(F32), lse_ref[0]), pad], axis=0)
        ga_sc[...] = jnp.concatenate([grad, aux_rows(jnp.zeros((AUX, rows), F32), delta), pad], axis=0)
        nat_sc[...] = jnp.concatenate([grad, query], axis=0).T
        if first:
            dq_sc[...] = jnp.zeros_like(dq_sc)
        else:
            dq_sc[...] = carry_ref[0]

    natural = nat_sc[...]
    for at in range(0, width, block):
        cut = slice(at, at + block)
        aux = mk_ref[0, :, cut]
        keys_t = k_ref[0, :, cut]
        keys = jnp.concatenate([keys_t, aux, pad[:, :block]], axis=0).T
        values = jnp.concatenate([v_ref[0, :, cut], aux, pad[:, :block]], axis=0).T
        probs = jnp.exp2(jnp.dot(keys, qa_sc[...], preferred_element_type=F32) * scale2)
        slopes = jnp.dot(values, ga_sc[...], preferred_element_type=F32)
        grad_scores = (probs * slopes).astype(BF16)
        from_probs = jnp.dot(probs.astype(BF16), natural, preferred_element_type=F32)
        from_scores = jnp.dot(grad_scores, natural, preferred_element_type=F32) * scale
        lane = lax.broadcasted_iota(jnp.int32, from_probs.shape, 1)
        both = jnp.where(lane < HD, from_probs, from_scores).T.astype(BF16)
        dkv_ref[0, at // block, 0] = both[HD:]
        dkv_ref[0, at // block, 1] = both[:HD]
        dq_sc[...] += jnp.dot(keys_t, grad_scores, preferred_element_type=F32)

    @pl.when(step == pl.num_programs(1) - 1)
    def _():
        if last:
            cut = dq_ref.shape[-1]
            for at in range(dq_ref.shape[0]):
                dq_ref[at] = (dq_sc[:, at * cut : (at + 1) * cut] * scale).astype(BF16)
        else:
            dq_ref[0] = dq_sc[...]


def attend_back(query_t, onehot, grad_t, out_heads, lse, pieces, carry, last, scale2, heads):
    count, _, width = pieces.shape
    rows = query_t.shape[1]
    cut = rows // GROUPS
    block = width // GROUPS
    blocks = width // block
    sum_spec = pl.BlockSpec((1, HD, rows), lambda h, j: (h, 0, 0))
    cut_spec = pl.BlockSpec((GROUPS, HD, cut), lambda h, j: (0, h, 0))
    row_spec = pl.BlockSpec((1, 1, rows), lambda h, j: (h, 0, 0))
    in_specs = [
        pl.BlockSpec((HD, rows), lambda h, j: (h, 0)),
        pl.BlockSpec((AUX, rows), lambda h, j: (0, 0)),
        cut_spec,
        sum_spec if carry is None else row_spec,
        row_spec,
        pl.BlockSpec((1, HD, width), lambda h, j: (j, h, 0)),
        pl.BlockSpec((1, HD, width), lambda h, j: (j, heads + h, 0)),
        pl.BlockSpec((1, AUX, width), lambda h, j: (j, 2 * heads * HD // AUX, 0)),
    ]
    if carry is not None:
        in_specs += [sum_spec]
    dq_shape = (GROUPS, heads * HD, cut) if last else (heads, HD, rows)
    return pl.pallas_call(
        functools.partial(backward_kernel, scale2, carry is None, last),
        grid=(heads, count),
        in_specs=in_specs,
        out_specs=([row_spec] if carry is None else [])
        + [
            cut_spec if last else sum_spec,
            pl.BlockSpec((1, blocks, 2, HD, block), lambda h, j: (j, 0, 0, h, 0)),
        ],
        out_shape=([jax.ShapeDtypeStruct((heads, 1, rows), F32)] if carry is None else [])
        + [
            jax.ShapeDtypeStruct(dq_shape, BF16 if last else F32),
            jax.ShapeDtypeStruct((count, blocks, 2, heads * HD, block), BF16),
        ],
        scratch_shapes=[
            pltpu.VMEM((128, rows), BF16),
            pltpu.VMEM((128, rows), BF16),
            pltpu.VMEM((rows, 128), BF16),
            pltpu.VMEM((HD, rows), F32),
        ],
        compiler_params=pltpu.CompilerParams(vmem_limit_bytes=VMEM_SHARED),
        cost_estimate=pl.CostEstimate(
            flops=15 * heads * rows * count * width * HD, bytes_accessed=0, transcendentals=0
        ),
    )(query_t, onehot, grad_t, out_heads, lse, pieces, pieces, pieces, *([] if carry is None else [carry]))


def route_parts(rows, router, columns, expert, expert_count):
    project = jnp.dot(rows, router, preferred_element_type=F32)
    size = jnp.sqrt(jnp.sum(project * project, axis=-1, keepdims=True))
    along = jnp.where(size > FLOOR, 1.0, jnp.where(size == FLOOR, 0.5, 0.0))
    inverse = 1.0 / jnp.maximum(size, FLOOR)
    unit = project * inverse
    logits = jnp.dot(unit, columns, precision=HIGHEST, preferred_element_type=F32) / ROUTER_HEAT
    lane = lax.broadcasted_iota(jnp.int32, logits.shape, 1)
    logits = jnp.where(lane < expert_count, logits, NEG_LARGE)
    raised = jnp.exp(logits - jnp.max(logits, axis=-1, keepdims=True))
    chances = raised / jnp.sum(raised, axis=-1, keepdims=True)
    mine = (lane == expert).astype(F32)
    gate = jnp.sum(chances * mine, axis=-1, keepdims=True)
    return unit, inverse, along, chances, mine, gate


def expert_kernel(first, expert_count, begin, info, x_ref, g_ref, uo_ref, so_ref, router_ref, columns_ref, *rest):
    steps = 3 if first else 1
    ux_refs, rest = rest[:steps], rest[steps:]
    sx_refs, rest = rest[:2], rest[2:]
    if first:
        own_ref, hidden_ref, gp_ref, gw_ref, gm_ref, made_ref, gin_ref, up_sc, down_sc, turned_sc = rest
    else:
        gm_ref, made_in, gin_in, _, _, *rest = rest
        hidden_ref, gp_ref, gw_ref, scaled_ref, back_ref, routed_ref, columns_out, *rest = rest
        up_sc, down_sc, turned_sc, made_ref, gin_ref = rest
    step = pl.program_id(0)
    share, block = uo_ref.shape

    @pl.when(step == 0)
    def _():
        cut = pl.ds(pl.multiple_of((1 - info[0]) * share, 128), share)
        turned_sc[...] = x_ref[:, cut].T
        if first:
            gate = route_parts(x_ref[...], router_ref[...], columns_ref[...], info[1], expert_count)[-1]
            gm_ref[...] = (gate * g_ref[...].astype(F32)).astype(BF16)
            made_ref[...] = jnp.zeros_like(made_ref)
            gin_ref[...] = jnp.zeros_like(gin_ref)
        else:
            made_ref[...] = made_in[...]
            gin_ref[...] = gin_in[...]

    up_sc[pl.ds(pl.multiple_of(info[0] * share, 128), share)] = uo_ref[...]
    other = pl.ds(pl.multiple_of((1 - info[0]) * share, 128), share)
    for now in range(steps):

        @pl.when(step == now)
        def _():
            up_sc[other] = ux_refs[now][...]
            if begin + now < 2:
                down_sc[...] = so_ref[...]
            else:
                down_sc[: block // 2] = sx_refs[0][...]
                down_sc[block // 2 :] = sx_refs[1][...]

    up, down = up_sc[...], down_sc[...]
    pre_act = jnp.dot(x_ref[...], up, preferred_element_type=F32)
    bell = 0.5 * (1.0 + lax.erf(pre_act * ROOT_HALF))
    hidden = (pre_act * bell).astype(BF16)
    if first:

        @pl.when(step < 2)
        def _():
            own_ref[...] = hidden

    hidden_ref[...] = hidden
    made_ref[...] += jnp.dot(hidden, down, preferred_element_type=F32)
    slope = bell + pre_act * (jnp.exp(-0.5 * pre_act * pre_act) * (1.0 / ROOT_TWO_PI))
    grad_hidden = dot32(gm_ref[...], down, (((1,), (1,))))
    grad_pre = (grad_hidden * slope).astype(BF16)
    gp_ref[...] = grad_pre
    gw_ref[...] = jnp.dot(turned_sc[...], grad_pre, preferred_element_type=F32).astype(BF16)
    gin_ref[...] += dot32(grad_pre, up, (((1,), (1,))))

    if not first:
        router, columns = router_ref[...], columns_ref[...]
        unit, inverse, along, chances, mine, gate = route_parts(x_ref[...], router, columns, info[1], expert_count)
        made = made_ref[...].astype(BF16).astype(F32)
        scaled_ref[...] = (gate * made).astype(BF16)
        grad_gate = jnp.sum(g_ref[...].astype(F32) * made, axis=-1, keepdims=True)
        dlogit = grad_gate * gate * (mine - chances) / ROUTER_HEAT
        dunit = lax.dot_general(
            dlogit, columns, (((1,), (1,)), ((), ())), precision=HIGHEST, preferred_element_type=F32
        )
        dproj = inverse * (dunit - along * unit * jnp.sum(unit * dunit, axis=-1, keepdims=True))
        high = dproj.astype(BF16)
        low = (dproj - high.astype(F32)).astype(BF16)
        back = dot32(high, router, (((1,), (1,)))) + dot32(low, router, (((1,), (1,))))
        back_ref[...] = (gin_ref[...].astype(BF16).astype(F32) + back).astype(BF16)
        rows = x_ref[...]
        routed_ref[...] = jnp.dot(high.astype(F32).T.astype(BF16), rows, preferred_element_type=F32) + jnp.dot(
            low.astype(F32).T.astype(BF16), rows, preferred_element_type=F32
        )
        columns_out[...] = jnp.dot(unit.T, dlogit, precision=HIGHEST, preferred_element_type=F32)


def run_expert(info, rows, grads, widen, widen_other, shrink, shrink_other, routing, carry, expert_count):
    slots, width = rows.shape
    share, units = widen.shape
    block = units // 4
    first = carry is None
    begin = 0 if first else 3

    def at(j, info):
        return lax.rem(2 * info[0] + begin + j, 4)

    whole = pl.BlockSpec((slots, width), lambda j, info: (0, 0))
    quarter = pl.BlockSpec((slots, block), lambda j, info: (0, 0))
    part = jax.ShapeDtypeStruct((slots, units), BF16)
    part_spec = pl.BlockSpec((slots, block), lambda j, info: (0, at(j, info)))
    low = jax.ShapeDtypeStruct((slots, width), BF16)
    full = jax.ShapeDtypeStruct((slots, width), F32)
    fixed = [*routing, *widen_other, *shrink_other]
    in_specs = [
        whole,
        whole,
        pl.BlockSpec((share, block), lambda j, info: (0, at(j, info))),
        pl.BlockSpec((block, width), lambda j, info: (jnp.minimum(j, 1), 0)),
        *[pl.BlockSpec(value.shape, lambda j, info: (0, 0)) for value in fixed],
    ]
    operands = [rows, grads, widen, shrink, *fixed]
    scratch = [pltpu.VMEM((width, block), BF16), pltpu.VMEM((block, width), BF16), pltpu.VMEM((share, slots), BF16)]
    sent = jax.ShapeDtypeStruct((share, units), BF16)
    sent_spec = pl.BlockSpec((share, block), lambda j, info: (0, at(j, info)))
    aliases = {}
    if first:
        own = jax.ShapeDtypeStruct((slots, 2 * block), BF16)
        out_specs = [
            pl.BlockSpec((slots, block), lambda j, info: (0, jnp.minimum(j, 1))), quarter, part_spec, sent_spec,
            whole, whole, whole,
        ]
        out_shape = [own, jax.ShapeDtypeStruct((slots, block), BF16), part, sent, low, full, full]
    else:
        grad_pre, widen_sent, grad_made, made, grad_inputs = carry
        in_specs += [whole, whole, whole] + [pl.BlockSpec(memory_space=pl.ANY)] * 2
        operands += [grad_made, made, grad_inputs, grad_pre, widen_sent]
        aliases = {len(operands) - 1: 1, len(operands): 2}
        tops = [jax.ShapeDtypeStruct((128, width), F32), jax.ShapeDtypeStruct((128, 128), F32)]
        out_specs = [quarter, part_spec, sent_spec, whole, whole]
        out_specs += [pl.BlockSpec(v.shape, lambda j, info: (0, 0)) for v in tops]
        out_shape = [jax.ShapeDtypeStruct((slots, block), BF16), part, sent, low, low, *tops]
        scratch += [pltpu.VMEM((slots, width), F32), pltpu.VMEM((slots, width), F32)]
    return pl.pallas_call(
        functools.partial(expert_kernel, first, expert_count, begin),
        grid_spec=pltpu.PrefetchScalarGridSpec(
            num_scalar_prefetch=1,
            grid=(3 if first else 1,),
            in_specs=in_specs,
            out_specs=out_specs,
            scratch_shapes=scratch,
        ),
        out_shape=out_shape,
        input_output_aliases=aliases,
        compiler_params=pltpu.CompilerParams(vmem_limit_bytes=VMEM_BYTES),
        cost_estimate=pl.CostEstimate(
            flops=(9 if first else 3) * slots * width * units, bytes_accessed=0, transcendentals=0
        ),
    )(info.astype(jnp.int32), *operands)


def final_kernel(info, g_ref, c_ref, kept_ref, sent_ref, all_sc):
    all_sc[...] = dot32(g_ref[...].T, c_ref[...], (((1,), (1,)))).astype(BF16)
    count, half = kept_ref.shape[:2]
    for at in range(count):
        for ref, core in ((kept_ref, info[0]), (sent_ref, 1 - info[0])):
            ref[at] = all_sc[pl.ds(pl.multiple_of((2 * at + core) * half, 16), half)]


def final_grads(core, grads, context):
    width = grads.shape[1]
    shape = (GROUPS, width // GROUPS // 2, context.shape[0])
    return pl.pallas_call(
        final_kernel,
        grid_spec=pltpu.PrefetchScalarGridSpec(
            num_scalar_prefetch=1,
            grid=(1,),
            in_specs=[pl.BlockSpec(value.shape, lambda j, info: (0, 0)) for value in (grads, context)],
            out_specs=[pl.BlockSpec(shape, lambda j, info: (0, 0, 0))] * 2,
            scratch_shapes=[pltpu.VMEM((width, context.shape[0]), BF16)],
        ),
        out_shape=[jax.ShapeDtypeStruct(shape, BF16)] * 2,
        compiler_params=pltpu.CompilerParams(vmem_limit_bytes=VMEM_BYTES),
    )(core[None].astype(jnp.int32), grads, context)


def gather_kernel(dq_ref, own_ref, got_ref, far0_ref, far1_ref, w_ref, joined_ref, *part_refs):
    step = pl.program_id(0)
    far = jnp.where(step < GROUPS // 2, far0_ref[0, 0].astype(F32), far1_ref[0, 0].astype(F32))
    grad_kv = (own_ref[0, 0].astype(F32) + got_ref[0, 0].astype(F32) + far).astype(BF16)
    joined = jnp.concatenate([dq_ref[0], grad_kv[0], grad_kv[1]], axis=0)
    joined_ref[0] = joined
    through = dot32(joined.T, w_ref[...], (((1,), (1,)))).astype(BF16)
    for at in range(GROUPS):

        @pl.when(step == at)
        def _():
            part_refs[at][...] = through


def gather_grads(grad_query, near_own, near_got, far, far_last, maps):
    group_width, cut = grad_query.shape[1:]
    width = maps.shape[0]
    half = GROUPS // 2
    piece = (1, 1, 2, group_width, cut)
    joined = (GROUPS, 3 * group_width, cut)
    return pl.pallas_call(
        gather_kernel,
        grid=(GROUPS,),
        in_specs=[
            pl.BlockSpec((1, group_width, cut), lambda j: (j, 0, 0)),
            pl.BlockSpec(piece, lambda j: (0, j, 0, 0, 0)),
            pl.BlockSpec(piece, lambda j: (0, j, 0, 0, 0)),
            pl.BlockSpec(piece, lambda j: (0, jnp.minimum(j, half - 1), 0, 0, 0)),
            pl.BlockSpec(piece, lambda j: (0, jnp.maximum(j - half, 0), 0, 0, 0)),
            pl.BlockSpec(maps.shape, lambda j: (0, 0)),
        ],
        out_specs=[pl.BlockSpec((1, *joined[1:]), lambda j: (j, 0, 0))]
        + [pl.BlockSpec((cut, width), lambda j: (0, 0))] * GROUPS,
        out_shape=[jax.ShapeDtypeStruct(joined, BF16)] + [jax.ShapeDtypeStruct((cut, width), BF16)] * GROUPS,
        compiler_params=pltpu.CompilerParams(vmem_limit_bytes=VMEM_BYTES),
        cost_estimate=pl.CostEstimate(flops=12 * group_width * GROUPS * cut * width, bytes_accessed=0, transcendentals=0),
    )(grad_query, near_own, near_got, far, far_last, maps)


def product_kernel(row, info, joined_ref, x_ref, small_ref, gain_ref, kept_ref, sent_ref, acc_sc, all_sc):
    step = pl.program_id(0)
    product = jnp.dot(joined_ref[0], x_ref[...], preferred_element_type=F32)

    @pl.when(step == 0)
    def _():
        acc_sc[...] = product

    @pl.when(step > 0)
    def _():
        acc_sc[...] += product

    @pl.when(step == pl.num_programs(0) - 1)
    def _():
        rows = acc_sc.shape[0]
        all_sc[:rows] = acc_sc[...].astype(BF16)
        place = lax.broadcasted_iota(jnp.int32, small_ref.shape, 0)
        all_sc[rows:] = jnp.where(place == row, gain_ref[...], small_ref[...].astype(F32)).astype(BF16)
        half = kept_ref.shape[0]
        kept_ref[...] = all_sc[pl.ds(pl.multiple_of(info[0] * half, 16), half)]
        sent_ref[...] = all_sc[pl.ds(pl.multiple_of((1 - info[0]) * half, 16), half)]


def maps_product(core, joined, normed, small, gain_grad, row):
    count, rows, cut = joined.shape
    width = normed.shape[1]
    total = rows + small.shape[0]
    return pl.pallas_call(
        functools.partial(product_kernel, row),
        grid_spec=pltpu.PrefetchScalarGridSpec(
            num_scalar_prefetch=1,
            grid=(count,),
            in_specs=[
                pl.BlockSpec((1, rows, cut), lambda j, info: (j, 0, 0)),
                pl.BlockSpec((cut, width), lambda j, info: (j, 0)),
                pl.BlockSpec(small.shape, lambda j, info: (0, 0)),
                pl.BlockSpec((1, width), lambda j, info: (0, 0)),
            ],
            out_specs=[pl.BlockSpec((total // 2, width), lambda j, info: (0, 0))] * 2,
            scratch_shapes=[pltpu.VMEM((rows, width), F32), pltpu.VMEM((total, width), BF16)],
        ),
        out_shape=[jax.ShapeDtypeStruct((total // 2, width), BF16)] * 2,
        compiler_params=pltpu.CompilerParams(vmem_limit_bytes=VMEM_BYTES),
        cost_estimate=pl.CostEstimate(flops=4 * rows * count * cut * width, bytes_accessed=0, transcendentals=0),
    )(core[None].astype(jnp.int32), joined, normed, small, gain_grad[None])


def finish_kernel(
    group_width, info, own_ref, got_ref, w_ref, gain_ref, maps_ref, final_ref, router_ref, embed_ref, ln1_ref, ln2_ref,
    v_ref,
):
    final_half = group_width // 2
    part = own_ref.shape[1]
    half = 2 * part - final_half
    for ref, core in ((own_ref, info[1]), (got_ref, 1 - info[1])):
        low_rows = pl.ds(pl.multiple_of(core * half, 16), part)
        high_rows = pl.ds(pl.multiple_of(core * half + part, 16), half - part)
        final_rows = pl.ds(pl.multiple_of(2 * half + core * final_half, 16), final_half)
        for k in range(GROUPS):
            v_ref[k, low_rows] = ref[k + GROUPS * info[2]]
            high = ref[k + GROUPS * (1 - info[2])]
            v_ref[k, high_rows] = high[: half - part]
            v_ref[k, final_rows] = high[half - part :]

    def columns(pair, begin):
        rows = pl.ds(begin, group_width)
        halves = [v_ref[lax.rem(2 * pair + k + GROUPS - info[0], GROUPS), rows] for k in range(2)]
        return jnp.concatenate(halves, axis=0).astype(F32).T

    total = 0.0
    for part in range(3):
        for pair in range(GROUPS // 2):
            value = columns(pair, part * group_width)
            at = (part * GROUPS + 2 * pair) * group_width
            cut = slice(at, at + 2 * group_width)
            maps_ref[:, cut] = value
            total = total + jnp.sum(value * w_ref[:, cut].astype(F32), axis=1, keepdims=True)
    for pair in range(GROUPS // 2):
        at = 2 * pair * group_width
        final_ref[:, at : at + 2 * group_width] = columns(pair, 2 * half)
    small = sum(v_ref[k, 3 * group_width : 2 * half].astype(F32) for k in range(GROUPS))
    route, embed = router_ref.shape[0], embed_ref.shape[0]
    rows = small.shape[1]
    router_ref[...] = small[:route]
    embed_ref[...] = small[route : route + embed, : embed_ref.shape[1]]
    ln2_ref[...] = small[route + embed]
    ln1_ref[...] = (jnp.broadcast_to(total, (rows, 128)).T[:1] / gain_ref[...].astype(F32))[0]


def finish_shared(own, got, weights, gain, info, group_width, route, embed_shape):
    rows, columns = weights.shape
    shapes = [(rows, columns), (rows, GROUPS * group_width), (route, rows), embed_shape, (rows,), (rows,)]
    return pl.pallas_call(
        functools.partial(finish_kernel, group_width),
        grid_spec=pltpu.PrefetchScalarGridSpec(
            num_scalar_prefetch=1,
            grid=(1,),
            in_specs=[
                pl.BlockSpec(own.shape, lambda j, info: (0, 0, 0)),
                pl.BlockSpec(got.shape, lambda j, info: (0, 0, 0)),
                pl.BlockSpec(weights.shape, lambda j, info: (0, 0)),
                pl.BlockSpec((1, rows), lambda j, info: (0, 0)),
            ],
            out_specs=[pl.BlockSpec(shape, lambda j, info, rank=len(shape): (0,) * rank) for shape in shapes],
            scratch_shapes=[pltpu.VMEM((GROUPS, 4 * own.shape[1], rows), BF16)],
        ),
        out_shape=[jax.ShapeDtypeStruct(shape, F32) for shape in shapes],
        compiler_params=pltpu.CompilerParams(vmem_limit_bytes=VMEM_BYTES),
    )(info.astype(jnp.int32), own, got, weights, gain[None])


def norm_parts(values):
    center = values - jnp.mean(values, axis=-1, keepdims=True)
    scale = lax.rsqrt(jnp.mean(center * center, axis=-1, keepdims=True) + EPSILON)
    return center * scale, scale


def norm_back(unit, scale, scaled_grad):
    along = jnp.mean(scaled_grad * unit, axis=-1, keepdims=True)
    return scale * (scaled_grad - jnp.mean(scaled_grad, axis=-1, keepdims=True) - unit * along)


def unit_of(vectors, axis):
    size = jnp.sqrt(jnp.sum(vectors * vectors, axis=axis, keepdims=True))
    share = jnp.where(size > FLOOR, 1.0, jnp.where(size == FLOOR, 0.5, 0.0))
    inverse = 1.0 / jnp.maximum(size, FLOOR)
    return vectors * inverse, inverse, share


def unit_back(unit, inverse, share, grad, axis):
    return inverse * (grad - share * unit * jnp.sum(unit * grad, axis=axis, keepdims=True))


def shift(value, axis, size, by):
    return lax.ppermute(value, axis, [(at, (at + by) % size) for at in range(size)])


def flip(value, axis, size, bit):
    return lax.ppermute(value, axis, [(at, at ^ bit) for at in range(size)])


def after(value, *others):
    return lax.optimization_barrier((value, *others))[0]


def line_gather(value, axis, size, tied):
    upward, downward, from_low, from_high = value, value, [], []
    for hop in range(size - 1):
        upward = tied(hop, upward)
        upward = lax.ppermute(upward, axis, [(at, at + 1) for at in range(hop, size - 1)])
        downward = lax.ppermute(downward, axis, [(at, at - 1) for at in range(size - 1 - hop, 0, -1)])
        from_low.append(upward)
        from_high.append(downward)
    return [value] + [from_low[k] + from_high[size - 2 - k] for k in range(size - 1)]


def roll_blocks(blocks, start):
    return lax.dynamic_slice_in_dim(jnp.concatenate([blocks, blocks], axis=0), start, blocks.shape[0], 0)


def pair_order(own, other, at):
    return jnp.where(at == 0, jnp.concatenate([own, other], 0), jnp.concatenate([other, own], 0))


def body(
    ctx_count,
    fsdp_count,
    incoming_sequence,
    mixer_scaling_factor,
    asker_lookup_content_maps,
    mixer_final_map,
    specialist_scaling_factor,
    dispatch_space_map,
    specialist_dispatch_vectors,
    specialist_widen_weights_pair,
    specialist_shrink_weights_pair,
    document_labels,
    piece_specialist_choice,
    result_cotangent_array,
):
    row_count = incoming_sequence.shape[1]
    width = incoming_sequence.shape[2]
    head_count = width // HD
    heads = head_count // GROUPS
    group_width = heads * HD
    ring = ctx_count // GROUPS
    bits = ring.bit_length() - 1
    scale2 = LOG2E / math.sqrt(HD)
    z_at = lax.axis_index("z")
    r_at = lax.axis_index("r")
    f_at = lax.axis_index("fsdp")
    core = r_at & 1
    expert_at = z_at * ring + r_at
    share = width // fsdp_count
    capacity = max(2, 2 * row_count // ctx_count)
    slots = ctx_count * capacity

    def swap(value):
        return flip(value, "fsdp", fsdp_count, 1)

    def across(value, bit):
        return flip(value, "r", ring, bit)

    def exchange_slots(rows):
        return lax.all_to_all(
            rows.reshape(ctx_count, capacity, -1), ("z", "r"), split_axis=0, concat_axis=0, tiled=True
        ).reshape(slots, -1)

    def both_cores(got):
        return pair_order(got, across(got, 1), core)

    def halve(value, axis, flag, send):
        half = value.shape[axis] // 2
        kept = lax.dynamic_slice_in_dim(value, flag * half, half, axis)
        sent = lax.dynamic_slice_in_dim(value, (1 - flag) * half, half, axis)
        return (kept.astype(F32) + send(sent).astype(F32)).astype(BF16)

    def by_fsdp(own, other, axis):
        return jnp.where(
            f_at == 0,
            jnp.concatenate([own, other], axis=axis),
            jnp.concatenate([other, own], axis=axis),
        )

    route, experts = specialist_dispatch_vectors.shape[0] * fsdp_count, specialist_dispatch_vectors.shape[1]
    embed_share = route // fsdp_count
    extras = [
        mixer_scaling_factor[:, None],
        specialist_scaling_factor[:, None],
        dispatch_space_map,
        jnp.pad(specialist_dispatch_vectors, ((0, share - embed_share), (0, 0))),
    ]
    edges = [0, 3 * group_width]
    for value in extras:
        edges.append(edges[-1] + value.shape[1])
    extras.append(jnp.zeros((share, -edges[-1] % 128), BF16))
    early_own, early_sent = early_rows(
        jnp.stack([z_at, core]), asker_lookup_content_maps, jnp.concatenate(extras, axis=1), group_width
    )
    half = share // 2
    final_sent = lax.dynamic_slice_in_dim(mixer_final_map, core * half, half, 0)

    widen = specialist_widen_weights_pair[0]
    shrink_own = specialist_shrink_weights_pair[0]
    half_ff = shrink_own.shape[0]
    part_ff = half_ff // 2
    eighth = half_ff // 4
    early_pieces = []

    def send_widen(which, at, *others):
        begin = (which * 2 + at) * part_ff
        return swap(lax.dynamic_slice_in_dim(after(widen, *others), begin, part_ff, 1))

    def tie(value, pieces, at):
        value, pieces[at] = lax.optimization_barrier((value, pieces[at]))
        return value

    def hop_tie(hop, value):
        if hop == 1:
            value, *sent = lax.optimization_barrier((value, early_sent, final_sent))
            early_pieces.extend([swap(piece) for piece in sent])
        return value

    x_own = incoming_sequence[0]
    label_rows = jnp.zeros((16, width), BF16).at[0, :row_count].set(document_labels[0].astype(BF16))
    blocks = line_gather(jnp.concatenate([x_own, label_rows], axis=0), "z", GROUPS, hop_tie)
    x_all = jnp.concatenate([piece[:row_count] for piece in blocks], axis=0)
    labels = jnp.concatenate([piece[row_count, :row_count] for piece in blocks], axis=0)

    widen_near = [send_widen(1 - f_at, at, *early_pieces) for at in range(2)]
    widen_far = [send_widen(f_at, at, *early_pieces) for at in range(2)]
    early_full = pair_order(early_own, both_cores(early_pieces[0]), f_at)
    maps_group, gain_in, gain_mid, router, embed = (
        early_full[:, begin:end] for begin, end in zip(edges[:-1], edges[1:])
    )
    gain_in, gain_mid = gain_in[:, 0].astype(F32), gain_mid[:, 0].astype(F32)
    embed = embed.reshape(fsdp_count, share, experts)[:, :embed_share].reshape(route, experts).astype(F32)
    final_map = roll_blocks(
        pair_order(mixer_final_map, both_cores(early_pieces[1]), f_at).reshape(GROUPS, group_width, width), z_at
    ).reshape(width, width)

    picked = piece_specialist_choice[0, :, 0]
    hits = (picked[:, None] == jnp.arange(ctx_count, dtype=jnp.int32)[None, :]).astype(jnp.int32)
    slot_rank = jnp.sum(jnp.cumsum(hits, axis=0) * hits, axis=1) - 1
    slot_index = picked * capacity + slot_rank
    place = (jnp.arange(slots, dtype=jnp.int32)[:, None] == slot_index[None, :]).astype(BF16)
    cotangent = result_cotangent_array[0]

    def to_slots(values):
        return jnp.dot(place, values, preferred_element_type=F32).astype(BF16)

    x_all = tie(x_all, widen_near, 0)
    x_all, final_map, grad_rows = lax.optimization_barrier((x_all, final_map, to_slots(cotangent)))
    unit_all, _ = norm_parts(x_all.astype(F32))
    normed_low = (unit_all * gain_in).astype(BF16)
    joined_t = dot32(maps_group, normed_low, (((0,), (1,)))).astype(BF16)
    aux_at = jnp.arange(AUX, dtype=jnp.int32)[:, None]
    same = labels.astype(jnp.int32)[None, :] == aux_at
    onehot = same.astype(BF16)
    key_aux = jnp.where(
        aux_at < DOCS, jnp.where(same, 0.0, NEG_LARGE), jnp.where(aux_at < DOCS + 3, 1.0, 0.0)
    ).astype(BF16)
    own_piece = jnp.concatenate([joined_t[group_width:], key_aux], axis=0)[None]
    even = own_piece
    for bit in range(bits - 1, 0, -1):
        even = jnp.stack([even, across(even, 1 << bit)], axis=1).reshape(-1, *own_piece.shape[1:])
    even = even[1:]
    peer_piece, *shrink_sent = lax.optimization_barrier(
        (across(own_piece, 1), *[after(shrink_own, own_piece)[at * eighth : (at + 1) * eighth] for at in range(4)])
    )
    shrink_other = [swap(piece) for piece in shrink_sent]
    carry = attend(joined_t, onehot, own_piece, None, False, scale2, heads)
    carry = attend(joined_t, onehot, peer_piece, carry, False, scale2, heads)
    even = tie(tie(after(even, carry[0]), widen_near, 1), widen_far, 0)
    odd = across(even, 1)
    carry = attend(joined_t, onehot, even, carry, False, scale2, heads)
    out_heads, *out_low, lse = attend(joined_t, onehot, odd, carry, True, scale2, heads)
    context_t = jnp.concatenate(
        [out_low[0]] + [shift(out_low[k], "z", GROUPS, -k) for k in range(1, GROUPS)], axis=0
    )

    context_t = tie(tie(tie(context_t, widen_far, 1), shrink_other, 0), shrink_other, 1)
    x32 = x_own.astype(F32)
    residual = x32 + dot32(context_t, final_map, (((0,), (0,))))
    unit_mid, scale_mid = norm_parts(residual)
    mid_low = (unit_mid * gain_mid).astype(BF16)
    def from_slots(values):
        return dot32(place, values, (((0,), (0,))))

    grad_slots = exchange_slots(after(grad_rows, peer_piece))
    sent_rows, grad_slots = lax.optimization_barrier((to_slots(mid_low), grad_slots))
    arrived = exchange_slots(sent_rows)

    unit_columns, inverse_columns, share_columns = unit_of(embed, 0)
    routing = (
        jnp.pad(router, ((0, 0), (0, 128 - route))),
        jnp.pad(unit_columns, ((0, 128 - route), (0, 128 - experts))),
    )

    expert_info = jnp.stack([f_at, expert_at])
    hidden_own, hidden_third, *carry = run_expert(
        expert_info, arrived, grad_slots, widen, [*widen_near, widen_far[0]], shrink_own, shrink_other[:2], routing, None,
        experts,
    )
    grad_made = carry[2]
    hidden_last, grad_pre, widen_sent, scaled, sent_back, routed_grad, columns_grad = run_expert(
        expert_info, arrived, grad_slots, widen, [widen_far[1]], shrink_own, shrink_other[2:], routing, carry, experts
    )
    grad_back = exchange_slots(sent_back)

    arrived, hidden_own, hidden_third, hidden_last, grad_made, _ = lax.optimization_barrier(
        (arrived, hidden_own, hidden_third, hidden_last, grad_made, sent_back)
    )
    first, second = arrived[:, :share], arrived[:, share:]
    rows_own = jnp.where(f_at == 0, first, second)
    widen_back = swap(widen_sent)
    shrink_back = [
        dot32(value, grad_made, (((0,), (0,)))).astype(BF16)
        for value in (hidden_third, hidden_last)
    ]
    grad_router_own, grad_columns = routed_grad[:route], columns_grad[:route, :experts]
    grad_embed_own = unit_back(unit_columns, inverse_columns, share_columns, grad_columns, 0)
    embed_rows = jnp.pad(
        grad_embed_own.reshape(fsdp_count, embed_share, experts), ((0, 0), (0, 0), (0, share - experts))
    )
    small = jnp.concatenate(
        [
            grad_router_own,
            jnp.concatenate([embed_rows[at] for at in range(fsdp_count)], axis=1),
            jnp.zeros((SMALL - route - embed_share, width), F32),
        ],
        axis=0,
    ).astype(BF16)
    grad_back, small, *shrink_back = lax.optimization_barrier((grad_back, small, *shrink_back))
    shrink_back[0] = swap(shrink_back[0])

    grad_mid = from_slots(grad_back)
    grad_residual = cotangent.astype(F32) + norm_back(unit_mid, scale_mid, grad_mid * gain_mid)
    grad_gain_mid = jnp.sum(grad_mid * unit_mid, axis=0)
    grad_res_low = grad_residual.astype(BF16)
    grad_context = dot32(final_map, grad_res_low, (((1,), (1,)))).astype(BF16).reshape(
        GROUPS, group_width, row_count
    )
    grad_parts = [grad_context[0]] + [shift(grad_context[k], "z", GROUPS, k) for k in range(1, GROUPS)]
    grad_t = jnp.stack(grad_parts)

    context_rows = roll_blocks(
        context_t.reshape(GROUPS, group_width, row_count), (GROUPS - z_at) % GROUPS
    ).reshape(width, row_count)
    def back(piece, running, last=False, ties=()):
        tied = lax.optimization_barrier((grad_t, *ties))
        rows = out_heads if running is None else delta
        result = attend_back(joined_t, onehot, tied[0], rows, lse, piece, running, last, scale2, heads)
        return (*result, *tied[1:])

    scaled_back = exchange_slots(after(scaled, *grad_parts[1:]))
    delta, running, far_odd = back(odd, None)
    final_kept, final_sent = final_grads(core, after(grad_res_low, running), context_rows)
    final_got = across(final_sent, 1)
    running, far_even, final_got = back(even, running, ties=(final_got,))
    finals = (final_kept.astype(F32) + final_got.astype(F32)).astype(BF16)
    finals = lax.all_to_all(finals, "z", split_axis=0, concat_axis=0, tiled=True)
    far_got = across(far_odd, 1)
    cut = far_even.shape[1] // 2

    def far_sum(part):
        return (far_even[:, part].astype(F32) + far_got[:, part].astype(F32)).astype(BF16)

    def add_far(value):
        if bits == 2:
            return across(value, 2)
        value = jnp.concatenate([jnp.zeros_like(value[:1]), value], axis=0)
        for bit in range(1, bits):
            halves = value.reshape(-1, 2, *value.shape[1:])
            value = (halves[:, 0].astype(F32) + across(halves[:, 1], 1 << bit).astype(F32)).astype(BF16)
        return value

    far, far_last = far_sum(slice(0, cut)), far_sum(slice(cut, None))
    running, near_peer, far, far_last = back(peer_piece, running, ties=(far, far_last))
    far = add_far(far)
    far_last = add_far(after(far_last, running))
    grad_query, near_own, far, scaled_back, widen_back = back(
        own_piece, running, True, ties=(far, scaled_back, widen_back)
    )

    joined, *grad_parts = gather_grads(grad_query, near_own, across(near_peer, 1), far, far_last, maps_group)
    second_part = shift(grad_parts[2], "z", GROUPS, -2)
    kept, sent = maps_product(core, joined, normed_low, small, grad_gain_mid, route + embed_share)
    grad_maps_part = (kept.astype(F32) + across(sent, 1).astype(F32)).astype(BF16)
    finals = after(finals, joined)
    final_rows = sum(finals[at].astype(F32) for at in range(GROUPS)).astype(BF16)
    grad_maps_part = jnp.concatenate([grad_maps_part, final_rows], axis=0)
    out = residual + from_slots(after(scaled_back, joined))
    x_at = (r_at >> 1) & 1
    if bits == 2:
        half_rows = grad_maps_part.shape[0] // 2

        def piece(x_bit, f_bit):
            return lax.dynamic_slice(grad_maps_part, (x_bit * half_rows, f_bit * share), (half_rows, share))

        corner = [
            (r * fsdp_count + f, (r ^ 2) * fsdp_count + (1 - f)) for r in range(ring) for f in range(fsdp_count)
        ]
        pieces = [
            piece(x_at, f_at),
            across(piece(1 - x_at, f_at), 2),
            swap(piece(x_at, 1 - f_at)),
            lax.ppermute(piece(1 - x_at, 1 - f_at), ("r", "fsdp"), corner),
        ]
        grad_maps_part = sum(value.astype(F32) for value in pieces).astype(BF16)
    else:
        for bit in range(1, bits):
            grad_maps_part = halve(grad_maps_part, 0, (r_at >> bit) & 1, lambda v: across(v, 1 << bit))
        grad_maps_part = halve(grad_maps_part, 1, f_at, swap)
    grad_maps_part, second_part, shrink_back[0] = lax.optimization_barrier((grad_maps_part, second_part, shrink_back[0]))
    shrink_back[1] = swap(after(shrink_back[1], grad_maps_part))
    groups = [grad_maps_part] + [shift(grad_maps_part, "z", GROUPS, -k) for k in (1, 2, 3)]
    first_part = shift(after(grad_parts[1], *groups), "z", GROUPS, -1)
    third_part = shift(after(grad_parts[3], *groups), "z", GROUPS, -3)
    if bits == 2:
        both = jnp.stack([*groups, *[across(value, 2) for value in groups]])
    else:
        both = jnp.stack(groups)
        for bit in range(bits - 1, 0, -1):
            got = across(both, 1 << bit)
            both = jnp.where(
                (r_at >> bit) & 1 == 0,
                jnp.concatenate([both, got], axis=1),
                jnp.concatenate([got, both], axis=1),
            )
        both = jnp.concatenate(jnp.split(both, 2, axis=1), axis=0)
        x_at = jnp.zeros_like(x_at)
    grad_up = dot32(rows_own, grad_pre, (((0,), (0,)))) + after(widen_back, grad_maps_part).astype(F32)
    both, first_part, grad_up = lax.optimization_barrier((both, first_part, grad_up))
    grad_maps, grad_final, grad_router, grad_embed, grad_ln1, grad_ln2 = finish_shared(
        both, across(both, 1), asker_lookup_content_maps, mixer_scaling_factor, jnp.stack([z_at, core, x_at]),
        group_width, route, (embed_share, experts),
    )
    grad_router = grad_router.T

    hidden_own, third_part = lax.optimization_barrier((hidden_own, third_part))
    grad_down = dot32(hidden_own, grad_made, (((0,), (0,)))) + jnp.concatenate(
        shrink_back, axis=0
    ).astype(F32)
    grad_normed_in = sum(part.astype(F32) for part in (grad_parts[0], first_part, second_part, third_part))
    unit_in, scale_in = norm_parts(after(x_own, joined).astype(F32))
    grad_input = grad_residual + norm_back(unit_in, scale_in, grad_normed_in * gain_in)

    return (
        out[None].astype(BF16),
        grad_input[None],
        grad_ln1,
        grad_maps,
        grad_final,
        grad_ln2,
        grad_router,
        grad_embed,
        grad_up[None],
        grad_down[None],
    )


def solution(mesh):
    ctx_count, fsdp_count = mesh.shape["ctx"], mesh.shape["fsdp"]
    inner = Mesh(mesh.devices.reshape(GROUPS, ctx_count // GROUPS, fsdp_count), ("z", "r", "fsdp"))
    ctx = ("z", "r")
    tokens = P("fsdp", ctx, None)
    expert = P(ctx, "fsdp", None)
    halves, halves2 = P("fsdp"), P("fsdp", None)
    return jax.shard_map(
        functools.partial(body, ctx_count, fsdp_count),
        mesh=inner,
        in_specs=(
            tokens, halves, halves2, halves2, halves, halves2, halves2, expert, expert,
            P("fsdp", ctx), tokens, tokens,
        ),
        out_specs=(
            tokens, tokens, halves, halves2, halves2, halves, halves2, halves2, expert, expert,
        ),
        check_vma=False,
    )
```

```python
import functools
import math

import jax
import jax.numpy as jnp
from jax import lax
from jax.experimental import pallas as pl
from jax.experimental.pallas import tpu as pltpu
from jax.sharding import Mesh, PartitionSpec as P

HD = 64
SMALL = 64
DOCS = 8
AUX = 16
GROUPS = 4
EPSILON = 1e-05
FLOOR = 0.5
ROUTER_HEAT = 0.5
HIGHEST = lax.Precision.HIGHEST
ROOT_HALF = 0.7071067811865476
ROOT_TWO_PI = 2.5066282746310002
NEG_LARGE = -1e30
LOG2E = 1.4426950408889634
VMEM_BYTES = 62 * 1024 * 1024
VMEM_SHARED = 48 * 1024 * 1024
BF16 = jnp.bfloat16
F32 = jnp.float32


def dot32(left, right, dims):
    return lax.dot_general(left, right, (dims, ((), ())), preferred_element_type=F32)


def dot_high(left, right):
    return lax.dot_general(left, right, (((0,), (0,)), ((), ())), precision=HIGHEST)


def early_kernel(group_width, info, maps_ref, extra_ref, own_ref, sent_ref):
    width = GROUPS * group_width
    for group in range(GROUPS):

        @pl.when(info[0] == group)
        def _():
            begins = [part * width + group * group_width for part in range(3)]
            pieces = [maps_ref[:, begin : begin + group_width] for begin in begins]
            own_ref[...] = jnp.concatenate([*pieces, extra_ref[...]], axis=1)

    half = sent_ref.shape[0]
    sent_ref[...] = own_ref[pl.ds(pl.multiple_of(info[1] * half, 16), half)]


def early_rows(info, maps, extra, group_width):
    rows = maps.shape[0]
    columns = 3 * group_width + extra.shape[1]
    shapes = [(rows, columns), (rows // 2, columns)]
    return pl.pallas_call(
        functools.partial(early_kernel, group_width),
        grid_spec=pltpu.PrefetchScalarGridSpec(
            num_scalar_prefetch=1,
            grid=(1,),
            in_specs=[pl.BlockSpec(value.shape, lambda j, info: (0, 0)) for value in (maps, extra)],
            out_specs=[pl.BlockSpec(shape, lambda j, info: (0, 0)) for shape in shapes],
        ),
        out_shape=[jax.ShapeDtypeStruct(shape, BF16) for shape in shapes],
        compiler_params=pltpu.CompilerParams(vmem_limit_bytes=VMEM_BYTES),
    )(info.astype(jnp.int32), maps, extra)


def forward_kernel(scale2, first, last, q_ref, oh_ref, k_ref, v_ref, mk_ref, *rest):
    if not first:
        top_in, acc_in, *rest = rest
    if last:
        out_ref, *low_refs, lse_ref, top_sc, acc_sc = rest
    else:
        top_out, acc_out, top_sc, acc_sc = rest
    step = pl.program_id(1)
    width = k_ref.shape[-1]
    block = min(1024, width)
    pad = jnp.zeros((128 - HD - AUX, q_ref.shape[-1]), BF16)
    query = jnp.concatenate([q_ref[...], oh_ref[...], pad], axis=0)

    @pl.when(step == 0)
    def _():
        if first:
            top_sc[...] = jnp.full_like(top_sc, NEG_LARGE)
            acc_sc[...] = jnp.zeros_like(acc_sc)
        else:
            top_sc[...] = top_in[0]
            acc_sc[...] = acc_in[0]

    top, acc = top_sc[...], acc_sc[...]
    for at in range(0, width, block):
        cut = slice(at, at + block)
        aux = mk_ref[0, :, cut]
        keys = jnp.concatenate([k_ref[0, :, cut], aux, pad[:, :block]], axis=0).T
        scores = jnp.dot(keys, query, preferred_element_type=F32)
        new_top = jnp.maximum(top, jnp.max(scores, axis=0, keepdims=True))
        probs = jnp.exp2((scores - new_top) * scale2).astype(BF16)
        decay = jnp.exp2((top - new_top) * scale2)
        values = jnp.concatenate([v_ref[0, :, cut], aux], axis=0)
        acc = acc * decay + jnp.dot(values, probs, preferred_element_type=F32)
        top = new_top
    top_sc[...], acc_sc[...] = top, acc

    @pl.when(step == pl.num_programs(1) - 1)
    def _():
        if last:
            total = acc[HD + DOCS : HD + DOCS + 1]
            result = acc[:HD] / total
            out_ref[0] = result
            cut = low_refs[0].shape[-1]
            for at, low_ref in enumerate(low_refs):
                low_ref[...] = result[:, at * cut : (at + 1) * cut].astype(BF16)
            lse_ref[0] = top + jnp.log2(total) / scale2
        else:
            top_out[0] = top
            acc_out[0] = acc


def attend(query_t, onehot, pieces, carry, last, scale2, heads):
    count, _, width = pieces.shape
    rows = query_t.shape[1]
    cut = rows // GROUPS
    top_spec = pl.BlockSpec((1, 1, rows), lambda h, j: (h, 0, 0))
    acc_spec = pl.BlockSpec((1, HD + AUX, rows), lambda h, j: (h, 0, 0))
    in_specs = [
        pl.BlockSpec((HD, rows), lambda h, j: (h, 0)),
        pl.BlockSpec((AUX, rows), lambda h, j: (0, 0)),
        pl.BlockSpec((1, HD, width), lambda h, j: (j, h, 0)),
        pl.BlockSpec((1, HD, width), lambda h, j: (j, heads + h, 0)),
        pl.BlockSpec((1, AUX, width), lambda h, j: (j, 2 * heads * HD // AUX, 0)),
    ]
    if carry is not None:
        in_specs += [top_spec, acc_spec]
    top_shape = jax.ShapeDtypeStruct((heads, 1, rows), F32)
    if last:
        out_specs = [
            pl.BlockSpec((1, HD, rows), lambda h, j: (h, 0, 0)),
            *[pl.BlockSpec((HD, cut), lambda h, j: (h, 0))] * GROUPS,
            top_spec,
        ]
        out_shape = [
            jax.ShapeDtypeStruct((heads, HD, rows), F32),
            *[jax.ShapeDtypeStruct((heads * HD, cut), BF16)] * GROUPS,
            top_shape,
        ]
    else:
        out_specs = [top_spec, acc_spec]
        out_shape = [top_shape, jax.ShapeDtypeStruct((heads, HD + AUX, rows), F32)]
    return pl.pallas_call(
        functools.partial(forward_kernel, scale2, carry is None, last),
        grid=(heads, count),
        in_specs=in_specs,
        out_specs=out_specs,
        out_shape=out_shape,
        scratch_shapes=[pltpu.VMEM((1, rows), F32), pltpu.VMEM((HD + AUX, rows), F32)],
        compiler_params=pltpu.CompilerParams(vmem_limit_bytes=VMEM_SHARED),
        cost_estimate=pl.CostEstimate(
            flops=34 * heads * rows * count * width * HD, bytes_accessed=0, transcendentals=0
        ),
    )(query_t, onehot, pieces, pieces, pieces, *(carry or ()))


def split3(value):
    high = value.astype(BF16)
    rest = value - high.astype(F32)
    mid = rest.astype(BF16)
    return high, mid, (rest - mid.astype(F32)).astype(BF16)


def backward_kernel(scale2, first, last, q_ref, oh_ref, g_ref, o_ref, lse_ref, k_ref, v_ref, mk_ref, *rest):
    if not first:
        carry_ref, *rest = rest
    else:
        delta_ref, *rest = rest
    dq_ref, dkv_ref, qa_sc, ga_sc, nat_sc, dq_sc = rest
    step = pl.program_id(1)
    width = k_ref.shape[-1]
    block = width // GROUPS
    rows = q_ref.shape[-1]
    scale = 1.0 / math.sqrt(HD)
    pad = jnp.zeros((128 - HD - AUX, rows), BF16)

    @pl.when(step == 0)
    def _():
        query = q_ref[...]
        grad = jnp.concatenate([g_ref[at] for at in range(g_ref.shape[0])], axis=1)
        if first:
            delta = jnp.sum(grad.astype(F32) * o_ref[0], axis=0, keepdims=True)
            delta_ref[0] = delta
        else:
            delta = o_ref[0]
        place = lax.broadcasted_iota(jnp.int32, (AUX, rows), 0)

        def aux_rows(start, value):
            out = start
            for at, piece in enumerate(split3(-value)):
                out = jnp.where(place == DOCS + at, piece.astype(F32), out)
            return out.astype(BF16)

        qa_sc[...] = jnp.concatenate([query, aux_rows(oh_ref[...].astype(F32), lse_ref[0]), pad], axis=0)
        ga_sc[...] = jnp.concatenate([grad, aux_rows(jnp.zeros((AUX, rows), F32), delta), pad], axis=0)
        nat_sc[...] = jnp.concatenate([grad, query], axis=0).T
        if first:
            dq_sc[...] = jnp.zeros_like(dq_sc)
        else:
            dq_sc[...] = carry_ref[0]

    natural = nat_sc[...]
    for at in range(0, width, block):
        cut = slice(at, at + block)
        aux = mk_ref[0, :, cut]
        keys_t = k_ref[0, :, cut]
        keys = jnp.concatenate([keys_t, aux, pad[:, :block]], axis=0).T
        values = jnp.concatenate([v_ref[0, :, cut], aux, pad[:, :block]], axis=0).T
        probs = jnp.exp2(jnp.dot(keys, qa_sc[...], preferred_element_type=F32) * scale2)
        slopes = jnp.dot(values, ga_sc[...], preferred_element_type=F32)
        grad_scores = (probs * slopes).astype(BF16)
        from_probs = jnp.dot(probs.astype(BF16), natural, preferred_element_type=F32)
        from_scores = jnp.dot(grad_scores, natural, preferred_element_type=F32) * scale
        lane = lax.broadcasted_iota(jnp.int32, from_probs.shape, 1)
        both = jnp.where(lane < HD, from_probs, from_scores).T.astype(BF16)
        dkv_ref[0, at // block, 0] = both[HD:]
        dkv_ref[0, at // block, 1] = both[:HD]
        dq_sc[...] += jnp.dot(keys_t, grad_scores, preferred_element_type=F32)

    @pl.when(step == pl.num_programs(1) - 1)
    def _():
        if last:
            cut = dq_ref.shape[-1]
            for at in range(dq_ref.shape[0]):
                dq_ref[at] = (dq_sc[:, at * cut : (at + 1) * cut] * scale).astype(BF16)
        else:
            dq_ref[0] = dq_sc[...]


def attend_back(query_t, onehot, grad_t, out_heads, lse, pieces, carry, last, scale2, heads):
    count, _, width = pieces.shape
    rows = query_t.shape[1]
    cut = rows // GROUPS
    block = width // GROUPS
    blocks = width // block
    sum_spec = pl.BlockSpec((1, HD, rows), lambda h, j: (h, 0, 0))
    cut_spec = pl.BlockSpec((GROUPS, HD, cut), lambda h, j: (0, h, 0))
    row_spec = pl.BlockSpec((1, 1, rows), lambda h, j: (h, 0, 0))
    in_specs = [
        pl.BlockSpec((HD, rows), lambda h, j: (h, 0)),
        pl.BlockSpec((AUX, rows), lambda h, j: (0, 0)),
        cut_spec,
        sum_spec if carry is None else row_spec,
        row_spec,
        pl.BlockSpec((1, HD, width), lambda h, j: (j, h, 0)),
        pl.BlockSpec((1, HD, width), lambda h, j: (j, heads + h, 0)),
        pl.BlockSpec((1, AUX, width), lambda h, j: (j, 2 * heads * HD // AUX, 0)),
    ]
    if carry is not None:
        in_specs += [sum_spec]
    dq_shape = (GROUPS, heads * HD, cut) if last else (heads, HD, rows)
    return pl.pallas_call(
        functools.partial(backward_kernel, scale2, carry is None, last),
        grid=(heads, count),
        in_specs=in_specs,
        out_specs=([row_spec] if carry is None else [])
        + [
            cut_spec if last else sum_spec,
            pl.BlockSpec((1, blocks, 2, HD, block), lambda h, j: (j, 0, 0, h, 0)),
        ],
        out_shape=([jax.ShapeDtypeStruct((heads, 1, rows), F32)] if carry is None else [])
        + [
            jax.ShapeDtypeStruct(dq_shape, BF16 if last else F32),
            jax.ShapeDtypeStruct((count, blocks, 2, heads * HD, block), BF16),
        ],
        scratch_shapes=[
            pltpu.VMEM((128, rows), BF16),
            pltpu.VMEM((128, rows), BF16),
            pltpu.VMEM((rows, 128), BF16),
            pltpu.VMEM((HD, rows), F32),
        ],
        compiler_params=pltpu.CompilerParams(vmem_limit_bytes=VMEM_SHARED),
        cost_estimate=pl.CostEstimate(
            flops=15 * heads * rows * count * width * HD, bytes_accessed=0, transcendentals=0
        ),
    )(query_t, onehot, grad_t, out_heads, lse, pieces, pieces, pieces, *([] if carry is None else [carry]))


def route_parts(rows, router, columns, expert, expert_count):
    project = jnp.dot(rows, router, preferred_element_type=F32)
    size = jnp.sqrt(jnp.sum(project * project, axis=-1, keepdims=True))
    along = jnp.where(size > FLOOR, 1.0, jnp.where(size == FLOOR, 0.5, 0.0))
    inverse = 1.0 / jnp.maximum(size, FLOOR)
    unit = project * inverse
    logits = jnp.dot(unit, columns, precision=HIGHEST, preferred_element_type=F32) / ROUTER_HEAT
    lane = lax.broadcasted_iota(jnp.int32, logits.shape, 1)
    logits = jnp.where(lane < expert_count, logits, NEG_LARGE)
    raised = jnp.exp(logits - jnp.max(logits, axis=-1, keepdims=True))
    chances = raised / jnp.sum(raised, axis=-1, keepdims=True)
    mine = (lane == expert).astype(F32)
    gate = jnp.sum(chances * mine, axis=-1, keepdims=True)
    return unit, inverse, along, chances, mine, gate


def expert_kernel(first, expert_count, begin, info, x_ref, g_ref, uo_ref, so_ref, router_ref, columns_ref, *rest):
    steps = 3 if first else 1
    if first:
        *ux_refs, sx_ref = rest[: steps + 1]
        rest = rest[steps + 1 :]
    else:
        both_ref, *rest = rest
    if first:
        own_ref, hidden_ref, gp_ref, gw_ref, gm_ref, made_ref, gin_ref, up_sc, down_sc, turned_sc = rest
    else:
        gm_ref, made_in, gin_in, _, _, *rest = rest
        hidden_ref, gp_ref, gw_ref, scaled_ref, back_ref, routed_ref, columns_out, *rest = rest
        up_sc, down_sc, turned_sc, made_ref, gin_ref = rest
    step = pl.program_id(0)
    share, block = uo_ref.shape

    @pl.when(step == 0)
    def _():
        cut = pl.ds(pl.multiple_of((1 - info[0]) * share, 128), share)
        turned_sc[...] = x_ref[:, cut].T
        if first:
            gate = route_parts(x_ref[...], router_ref[...], columns_ref[...], info[1], expert_count)[-1]
            gm_ref[...] = (gate * g_ref[...].astype(F32)).astype(BF16)
            made_ref[...] = jnp.zeros_like(made_ref)
            gin_ref[...] = jnp.zeros_like(gin_ref)
        else:
            made_ref[...] = made_in[...]
            gin_ref[...] = gin_in[...]

    up_sc[pl.ds(pl.multiple_of(info[0] * share, 128), share)] = uo_ref[...]
    other = pl.ds(pl.multiple_of((1 - info[0]) * share, 128), share)
    for now in range(steps):

        @pl.when(step == now)
        def _():
            up_sc[other] = ux_refs[now][...] if first else both_ref[:share]
            if begin + now < 2:
                down_sc[...] = so_ref[...]
            else:
                down_sc[...] = sx_ref[...] if first else both_ref[share:]

    up, down = up_sc[...], down_sc[...]
    piece = x_ref.shape[0] // 2
    for begin_row in (0, piece):
        rows = slice(begin_row, begin_row + piece)
        pre_act = jnp.dot(x_ref[rows], up, preferred_element_type=F32)
        grad_hidden = dot32(gm_ref[rows], down, (((1,), (1,))))
        bell = 0.5 * (1.0 + lax.erf(pre_act * ROOT_HALF))
        hidden = (pre_act * bell).astype(BF16)
        hidden_ref[rows] = hidden
        made_ref[rows] += jnp.dot(hidden, down, preferred_element_type=F32)
        slope = bell + pre_act * (jnp.exp(-0.5 * pre_act * pre_act) * (1.0 / ROOT_TWO_PI))
        grad_pre = (grad_hidden * slope).astype(BF16)
        gp_ref[rows] = grad_pre
        gin_ref[rows] += dot32(grad_pre, up, (((1,), (1,))))
    if first:

        @pl.when(step < 2)
        def _():
            own_ref[...] = hidden_ref[...]

    gw_ref[...] = jnp.dot(turned_sc[...], gp_ref[...], preferred_element_type=F32).astype(BF16)

    if not first:
        router, columns = router_ref[...], columns_ref[...]
        unit, inverse, along, chances, mine, gate = route_parts(x_ref[...], router, columns, info[1], expert_count)
        made = made_ref[...].astype(BF16).astype(F32)
        scaled_ref[...] = (gate * made).astype(BF16)
        grad_gate = jnp.sum(g_ref[...].astype(F32) * made, axis=-1, keepdims=True)
        dlogit = grad_gate * gate * (mine - chances) / ROUTER_HEAT
        dunit = lax.dot_general(
            dlogit, columns, (((1,), (1,)), ((), ())), precision=HIGHEST, preferred_element_type=F32
        )
        dproj = inverse * (dunit - along * unit * jnp.sum(unit * dunit, axis=-1, keepdims=True))
        high = dproj.astype(BF16)
        low = (dproj - high.astype(F32)).astype(BF16)
        back = dot32(high, router, (((1,), (1,)))) + dot32(low, router, (((1,), (1,))))
        back_ref[...] = (gin_ref[...].astype(BF16).astype(F32) + back).astype(BF16)
        rows = x_ref[...]
        routed_ref[...] = jnp.dot(high.astype(F32).T.astype(BF16), rows, preferred_element_type=F32) + jnp.dot(
            low.astype(F32).T.astype(BF16), rows, preferred_element_type=F32
        )
        columns_out[...] = jnp.dot(unit.T, dlogit, precision=HIGHEST, preferred_element_type=F32)


def run_expert(info, rows, grads, widen, shrink, others, routing, carry, expert_count):
    slots, width = rows.shape
    share, units = widen.shape
    block = units // 4
    first = carry is None
    begin = 0 if first else 3

    def at(j, info):
        return lax.rem(2 * info[0] + begin + j, 4)

    whole = pl.BlockSpec((slots, width), lambda j, info: (0, 0))
    quarter = pl.BlockSpec((slots, block), lambda j, info: (0, 0))
    part = jax.ShapeDtypeStruct((slots, units), BF16)
    part_spec = pl.BlockSpec((slots, block), lambda j, info: (0, at(j, info)))
    low = jax.ShapeDtypeStruct((slots, width), BF16)
    full = jax.ShapeDtypeStruct((slots, width), F32)
    fixed = [*routing, *others]
    in_specs = [
        whole,
        whole,
        pl.BlockSpec((share, block), lambda j, info: (0, at(j, info))),
        pl.BlockSpec((block, width), lambda j, info: (jnp.minimum(j, 1), 0)),
        *[pl.BlockSpec(value.shape, lambda j, info: (0, 0)) for value in fixed],
    ]
    operands = [rows, grads, widen, shrink, *fixed]
    scratch = [pltpu.VMEM((width, block), BF16), pltpu.VMEM((block, width), BF16), pltpu.VMEM((share, slots), BF16)]
    sent = jax.ShapeDtypeStruct((share, units), BF16)
    sent_spec = pl.BlockSpec((share, block), lambda j, info: (0, at(j, info)))
    aliases = {}
    if first:
        own = jax.ShapeDtypeStruct((slots, 2 * block), BF16)
        out_specs = [
            pl.BlockSpec((slots, block), lambda j, info: (0, jnp.minimum(j, 1))), quarter, part_spec, sent_spec,
            whole, whole, whole,
        ]
        out_shape = [own, jax.ShapeDtypeStruct((slots, block), BF16), part, sent, low, full, full]
    else:
        grad_pre, widen_sent, grad_made, made, grad_inputs = carry
        in_specs += [whole, whole, whole] + [pl.BlockSpec(memory_space=pl.ANY)] * 2
        operands += [grad_made, made, grad_inputs, grad_pre, widen_sent]
        aliases = {len(operands) - 1: 1, len(operands): 2}
        tops = [jax.ShapeDtypeStruct((128, width), F32), jax.ShapeDtypeStruct((128, 128), F32)]
        out_specs = [quarter, part_spec, sent_spec, whole, whole]
        out_specs += [pl.BlockSpec(v.shape, lambda j, info: (0, 0)) for v in tops]
        out_shape = [jax.ShapeDtypeStruct((slots, block), BF16), part, sent, low, low, *tops]
        scratch += [pltpu.VMEM((slots, width), F32), pltpu.VMEM((slots, width), F32)]
    return pl.pallas_call(
        functools.partial(expert_kernel, first, expert_count, begin),
        grid_spec=pltpu.PrefetchScalarGridSpec(
            num_scalar_prefetch=1,
            grid=(3 if first else 1,),
            in_specs=in_specs,
            out_specs=out_specs,
            scratch_shapes=scratch,
        ),
        out_shape=out_shape,
        input_output_aliases=aliases,
        compiler_params=pltpu.CompilerParams(vmem_limit_bytes=VMEM_BYTES),
        cost_estimate=pl.CostEstimate(
            flops=(9 if first else 3) * slots * width * units, bytes_accessed=0, transcendentals=0
        ),
    )(info.astype(jnp.int32), *operands)


def final_kernel(info, g_ref, c_ref, kept_ref, sent_ref, all_sc):
    all_sc[...] = dot32(g_ref[...].T, c_ref[...], (((1,), (1,)))).astype(BF16)
    count, half = kept_ref.shape[:2]
    for at in range(count):
        for ref, core in ((kept_ref, info[0]), (sent_ref, 1 - info[0])):
            ref[at] = all_sc[pl.ds(pl.multiple_of((2 * at + core) * half, 16), half)]


def final_grads(core, grads, context):
    width = grads.shape[1]
    shape = (GROUPS, width // GROUPS // 2, context.shape[0])
    return pl.pallas_call(
        final_kernel,
        grid_spec=pltpu.PrefetchScalarGridSpec(
            num_scalar_prefetch=1,
            grid=(1,),
            in_specs=[pl.BlockSpec(value.shape, lambda j, info: (0, 0)) for value in (grads, context)],
            out_specs=[pl.BlockSpec(shape, lambda j, info: (0, 0, 0))] * 2,
            scratch_shapes=[pltpu.VMEM((width, context.shape[0]), BF16)],
        ),
        out_shape=[jax.ShapeDtypeStruct(shape, BF16)] * 2,
        compiler_params=pltpu.CompilerParams(vmem_limit_bytes=VMEM_BYTES),
    )(core[None].astype(jnp.int32), grads, context)


def gather_kernel(dq_ref, own_ref, got_ref, far0_ref, far1_ref, w_ref, joined_ref, *part_refs):
    step = pl.program_id(0)
    far = jnp.where(step < GROUPS // 2, far0_ref[0, 0].astype(F32), far1_ref[0, 0].astype(F32))
    grad_kv = (own_ref[0, 0].astype(F32) + got_ref[0, 0].astype(F32) + far).astype(BF16)
    joined = jnp.concatenate([dq_ref[0], grad_kv[0], grad_kv[1]], axis=0)
    joined_ref[0] = joined
    through = dot32(joined.T, w_ref[...], (((1,), (1,)))).astype(BF16)
    for at in range(GROUPS):

        @pl.when(step == at)
        def _():
            part_refs[at][...] = through


def gather_grads(grad_query, near_own, near_got, far, far_last, maps):
    group_width, cut = grad_query.shape[1:]
    width = maps.shape[0]
    half = GROUPS // 2
    piece = (1, 1, 2, group_width, cut)
    joined = (GROUPS, 3 * group_width, cut)
    return pl.pallas_call(
        gather_kernel,
        grid=(GROUPS,),
        in_specs=[
            pl.BlockSpec((1, group_width, cut), lambda j: (j, 0, 0)),
            pl.BlockSpec(piece, lambda j: (0, j, 0, 0, 0)),
            pl.BlockSpec(piece, lambda j: (0, j, 0, 0, 0)),
            pl.BlockSpec(piece, lambda j: (0, jnp.minimum(j, half - 1), 0, 0, 0)),
            pl.BlockSpec(piece, lambda j: (0, jnp.maximum(j - half, 0), 0, 0, 0)),
            pl.BlockSpec(maps.shape, lambda j: (0, 0)),
        ],
        out_specs=[pl.BlockSpec((1, *joined[1:]), lambda j: (j, 0, 0))]
        + [pl.BlockSpec((cut, width), lambda j: (0, 0))] * GROUPS,
        out_shape=[jax.ShapeDtypeStruct(joined, BF16)] + [jax.ShapeDtypeStruct((cut, width), BF16)] * GROUPS,
        compiler_params=pltpu.CompilerParams(vmem_limit_bytes=VMEM_BYTES),
        cost_estimate=pl.CostEstimate(flops=12 * group_width * GROUPS * cut * width, bytes_accessed=0, transcendentals=0),
    )(grad_query, near_own, near_got, far, far_last, maps)


def product_kernel(row, info, joined_ref, x_ref, small_ref, gain_ref, kept_ref, sent_ref, acc_sc, all_sc):
    step = pl.program_id(0)
    product = jnp.dot(joined_ref[0], x_ref[...], preferred_element_type=F32)

    @pl.when(step == 0)
    def _():
        acc_sc[...] = product

    @pl.when(step > 0)
    def _():
        acc_sc[...] += product

    @pl.when(step == pl.num_programs(0) - 1)
    def _():
        rows = acc_sc.shape[0]
        all_sc[:rows] = acc_sc[...].astype(BF16)
        place = lax.broadcasted_iota(jnp.int32, small_ref.shape, 0)
        all_sc[rows:] = jnp.where(place == row, gain_ref[...], small_ref[...].astype(F32)).astype(BF16)
        half = kept_ref.shape[0]
        kept_ref[...] = all_sc[pl.ds(pl.multiple_of(info[0] * half, 16), half)]
        sent_ref[...] = all_sc[pl.ds(pl.multiple_of((1 - info[0]) * half, 16), half)]


def maps_product(core, joined, normed, small, gain_grad, row):
    count, rows, cut = joined.shape
    width = normed.shape[1]
    total = rows + small.shape[0]
    return pl.pallas_call(
        functools.partial(product_kernel, row),
        grid_spec=pltpu.PrefetchScalarGridSpec(
            num_scalar_prefetch=1,
            grid=(count,),
            in_specs=[
                pl.BlockSpec((1, rows, cut), lambda j, info: (j, 0, 0)),
                pl.BlockSpec((cut, width), lambda j, info: (j, 0)),
                pl.BlockSpec(small.shape, lambda j, info: (0, 0)),
                pl.BlockSpec((1, width), lambda j, info: (0, 0)),
            ],
            out_specs=[pl.BlockSpec((total // 2, width), lambda j, info: (0, 0))] * 2,
            scratch_shapes=[pltpu.VMEM((rows, width), F32), pltpu.VMEM((total, width), BF16)],
        ),
        out_shape=[jax.ShapeDtypeStruct((total // 2, width), BF16)] * 2,
        compiler_params=pltpu.CompilerParams(vmem_limit_bytes=VMEM_BYTES),
        cost_estimate=pl.CostEstimate(flops=4 * rows * count * cut * width, bytes_accessed=0, transcendentals=0),
    )(core[None].astype(jnp.int32), joined, normed, small, gain_grad[None])


def finish_kernel(
    group_width, info, own_ref, got_ref, w_ref, gain_ref, maps_ref, final_ref, router_ref, embed_ref, ln1_ref, ln2_ref,
    v_ref,
):
    final_half = group_width // 2
    part = own_ref.shape[1]
    half = 2 * part - final_half
    for ref, core in ((own_ref, info[1]), (got_ref, 1 - info[1])):
        low_rows = pl.ds(pl.multiple_of(core * half, 16), part)
        high_rows = pl.ds(pl.multiple_of(core * half + part, 16), half - part)
        final_rows = pl.ds(pl.multiple_of(2 * half + core * final_half, 16), final_half)
        for k in range(GROUPS):
            v_ref[k, low_rows] = ref[k + GROUPS * info[2]]
            high = ref[k + GROUPS * (1 - info[2])]
            v_ref[k, high_rows] = high[: half - part]
            v_ref[k, final_rows] = high[half - part :]

    def columns(pair, begin):
        rows = pl.ds(begin, group_width)
        halves = [v_ref[lax.rem(2 * pair + k + GROUPS - info[0], GROUPS), rows] for k in range(2)]
        return jnp.concatenate(halves, axis=0).astype(F32).T

    total = 0.0
    for part in range(3):
        for pair in range(GROUPS // 2):
            value = columns(pair, part * group_width)
            at = (part * GROUPS + 2 * pair) * group_width
            cut = slice(at, at + 2 * group_width)
            maps_ref[:, cut] = value
            total = total + jnp.sum(value * w_ref[:, cut].astype(F32), axis=1, keepdims=True)
    for pair in range(GROUPS // 2):
        at = 2 * pair * group_width
        final_ref[:, at : at + 2 * group_width] = columns(pair, 2 * half)
    small = sum(v_ref[k, 3 * group_width : 2 * half].astype(F32) for k in range(GROUPS))
    route, embed = router_ref.shape[0], embed_ref.shape[0]
    rows = small.shape[1]
    router_ref[...] = small[:route]
    embed_ref[...] = small[route : route + embed, : embed_ref.shape[1]]
    ln2_ref[...] = small[route + embed]
    ln1_ref[...] = (jnp.broadcast_to(total, (rows, 128)).T[:1] / gain_ref[...].astype(F32))[0]


def finish_shared(own, got, weights, gain, info, group_width, route, embed_shape):
    rows, columns = weights.shape
    shapes = [(rows, columns), (rows, GROUPS * group_width), (route, rows), embed_shape, (rows,), (rows,)]
    return pl.pallas_call(
        functools.partial(finish_kernel, group_width),
        grid_spec=pltpu.PrefetchScalarGridSpec(
            num_scalar_prefetch=1,
            grid=(1,),
            in_specs=[
                pl.BlockSpec(own.shape, lambda j, info: (0, 0, 0)),
                pl.BlockSpec(got.shape, lambda j, info: (0, 0, 0)),
                pl.BlockSpec(weights.shape, lambda j, info: (0, 0)),
                pl.BlockSpec((1, rows), lambda j, info: (0, 0)),
            ],
            out_specs=[pl.BlockSpec(shape, lambda j, info, rank=len(shape): (0,) * rank) for shape in shapes],
            scratch_shapes=[pltpu.VMEM((GROUPS, 4 * own.shape[1], rows), BF16)],
        ),
        out_shape=[jax.ShapeDtypeStruct(shape, F32) for shape in shapes],
        compiler_params=pltpu.CompilerParams(vmem_limit_bytes=VMEM_SHARED),
    )(info.astype(jnp.int32), own, got, weights, gain[None])


def norm_parts(values):
    center = values - jnp.mean(values, axis=-1, keepdims=True)
    scale = lax.rsqrt(jnp.mean(center * center, axis=-1, keepdims=True) + EPSILON)
    return center * scale, scale


def norm_back(unit, scale, scaled_grad):
    along = jnp.mean(scaled_grad * unit, axis=-1, keepdims=True)
    return scale * (scaled_grad - jnp.mean(scaled_grad, axis=-1, keepdims=True) - unit * along)


def unit_of(vectors, axis):
    size = jnp.sqrt(jnp.sum(vectors * vectors, axis=axis, keepdims=True))
    share = jnp.where(size > FLOOR, 1.0, jnp.where(size == FLOOR, 0.5, 0.0))
    inverse = 1.0 / jnp.maximum(size, FLOOR)
    return vectors * inverse, inverse, share


def unit_back(unit, inverse, share, grad, axis):
    return inverse * (grad - share * unit * jnp.sum(unit * grad, axis=axis, keepdims=True))


def shift(value, axis, size, by):
    return lax.ppermute(value, axis, [(at, (at + by) % size) for at in range(size)])


def flip(value, axis, size, bit):
    return lax.ppermute(value, axis, [(at, at ^ bit) for at in range(size)])


def after(value, *others):
    return lax.optimization_barrier((value, *others))[0]


def line_gather(value, axis, size, tied):
    upward, downward, from_low, from_high = value, value, [], []
    for hop in range(size - 1):
        upward = tied(hop, upward)
        upward = lax.ppermute(upward, axis, [(at, at + 1) for at in range(hop, size - 1)])
        downward = lax.ppermute(downward, axis, [(at, at - 1) for at in range(size - 1 - hop, 0, -1)])
        from_low.append(upward)
        from_high.append(downward)
    return [value] + [from_low[k] + from_high[size - 2 - k] for k in range(size - 1)]


def roll_blocks(blocks, start):
    return lax.dynamic_slice_in_dim(jnp.concatenate([blocks, blocks], axis=0), start, blocks.shape[0], 0)


def pair_order(own, other, at):
    return jnp.where(at == 0, jnp.concatenate([own, other], 0), jnp.concatenate([other, own], 0))


def body(
    ctx_count,
    fsdp_count,
    incoming_sequence,
    mixer_scaling_factor,
    asker_lookup_content_maps,
    mixer_final_map,
    specialist_scaling_factor,
    dispatch_space_map,
    specialist_dispatch_vectors,
    specialist_widen_weights_pair,
    specialist_shrink_weights_pair,
    document_labels,
    piece_specialist_choice,
    result_cotangent_array,
):
    row_count = incoming_sequence.shape[1]
    width = incoming_sequence.shape[2]
    head_count = width // HD
    heads = head_count // GROUPS
    group_width = heads * HD
    ring = ctx_count // GROUPS
    bits = ring.bit_length() - 1
    scale2 = LOG2E / math.sqrt(HD)
    z_at = lax.axis_index("z")
    r_at = lax.axis_index("r")
    f_at = lax.axis_index("fsdp")
    core = r_at & 1
    expert_at = z_at * ring + r_at
    share = width // fsdp_count
    capacity = max(2, 2 * row_count // ctx_count)
    slots = ctx_count * capacity

    def swap(value):
        return flip(value, "fsdp", fsdp_count, 1)

    def across(value, bit):
        return flip(value, "r", ring, bit)

    def exchange_slots(rows):
        return lax.all_to_all(
            rows.reshape(ctx_count, capacity, -1), ("z", "r"), split_axis=0, concat_axis=0, tiled=True
        ).reshape(slots, -1)

    def both_cores(got):
        return pair_order(got, across(got, 1), core)

    def halve(value, axis, flag, send):
        half = value.shape[axis] // 2
        kept = lax.dynamic_slice_in_dim(value, flag * half, half, axis)
        sent = lax.dynamic_slice_in_dim(value, (1 - flag) * half, half, axis)
        return (kept.astype(F32) + send(sent).astype(F32)).astype(BF16)

    def by_fsdp(own, other, axis):
        return jnp.where(
            f_at == 0,
            jnp.concatenate([own, other], axis=axis),
            jnp.concatenate([other, own], axis=axis),
        )

    route, experts = specialist_dispatch_vectors.shape[0] * fsdp_count, specialist_dispatch_vectors.shape[1]
    embed_share = route // fsdp_count
    extras = [
        mixer_scaling_factor[:, None],
        specialist_scaling_factor[:, None],
        dispatch_space_map,
        jnp.pad(specialist_dispatch_vectors, ((0, share - embed_share), (0, 0))),
    ]
    edges = [0, 3 * group_width]
    for value in extras:
        edges.append(edges[-1] + value.shape[1])
    extras.append(jnp.zeros((share, -edges[-1] % 128), BF16))
    early_own, early_sent = early_rows(
        jnp.stack([z_at, core]), asker_lookup_content_maps, jnp.concatenate(extras, axis=1), group_width
    )
    half = share // 2
    final_sent = lax.dynamic_slice_in_dim(mixer_final_map, core * half, half, 0)

    widen = specialist_widen_weights_pair[0]
    shrink_own = specialist_shrink_weights_pair[0]
    half_ff = shrink_own.shape[0]
    part_ff = half_ff // 2
    eighth = half_ff // 4
    early_pieces = []

    def widen_piece(which, at, *others):
        return lax.dynamic_slice_in_dim(after(widen, *others), (which * 2 + at) * part_ff, part_ff, 1)

    def tie(value, pieces, at):
        value, pieces[at] = lax.optimization_barrier((value, pieces[at]))
        return value

    def hop_tie(hop, value):
        if hop == 1:
            value, *sent = lax.optimization_barrier((value, early_sent, final_sent))
            early_pieces.extend([swap(piece) for piece in sent])
        return value

    x_own = incoming_sequence[0]
    label_rows = jnp.zeros((16, width), BF16).at[0, :row_count].set(document_labels[0].astype(BF16))
    blocks = line_gather(jnp.concatenate([x_own, label_rows], axis=0), "z", GROUPS, hop_tie)
    x_all = jnp.concatenate([piece[:row_count] for piece in blocks], axis=0)
    labels = jnp.concatenate([piece[row_count, :row_count] for piece in blocks], axis=0)

    widen_near = [swap(widen_piece(1 - f_at, at, *early_pieces)) for at in range(2)]
    widen_far = [swap(widen_piece(f_at, 0, *early_pieces))]
    widen_last = widen_piece(f_at, 1, *early_pieces)
    early_full = pair_order(early_own, both_cores(early_pieces[0]), f_at)
    maps_group, gain_in, gain_mid, router, embed = (
        early_full[:, begin:end] for begin, end in zip(edges[:-1], edges[1:])
    )
    gain_in, gain_mid = gain_in[:, 0].astype(F32), gain_mid[:, 0].astype(F32)
    embed = embed.reshape(fsdp_count, share, experts)[:, :embed_share].reshape(route, experts).astype(F32)
    final_map = roll_blocks(
        pair_order(mixer_final_map, both_cores(early_pieces[1]), f_at).reshape(GROUPS, group_width, width), z_at
    ).reshape(width, width)

    picked = piece_specialist_choice[0, :, 0]
    hits = (picked[:, None] == jnp.arange(ctx_count, dtype=jnp.int32)[None, :]).astype(jnp.int32)
    slot_rank = jnp.sum(jnp.cumsum(hits, axis=0) * hits, axis=1) - 1
    slot_index = picked * capacity + slot_rank
    place = (jnp.arange(slots, dtype=jnp.int32)[:, None] == slot_index[None, :]).astype(BF16)
    cotangent = result_cotangent_array[0]

    def to_slots(values):
        return jnp.dot(place, values, preferred_element_type=F32).astype(BF16)

    x_all = tie(x_all, widen_near, 0)
    x_all, final_map, grad_rows = lax.optimization_barrier((x_all, final_map, to_slots(cotangent)))
    unit_all, _ = norm_parts(x_all.astype(F32))
    normed_low = (unit_all * gain_in).astype(BF16)
    joined_t = dot32(maps_group, normed_low, (((0,), (1,)))).astype(BF16)
    aux_at = jnp.arange(AUX, dtype=jnp.int32)[:, None]
    same = labels.astype(jnp.int32)[None, :] == aux_at
    onehot = same.astype(BF16)
    key_aux = jnp.where(
        aux_at < DOCS, jnp.where(same, 0.0, NEG_LARGE), jnp.where(aux_at < DOCS + 3, 1.0, 0.0)
    ).astype(BF16)
    own_piece = jnp.concatenate([joined_t[group_width:], key_aux], axis=0)[None]
    even = own_piece
    for bit in range(bits - 1, 0, -1):
        even = jnp.stack([even, across(even, 1 << bit)], axis=1).reshape(-1, *own_piece.shape[1:])
    even = even[1:]
    last_sent = jnp.concatenate([widen_last, after(shrink_own, own_piece)[part_ff:]], axis=0)
    peer_piece, *shrink_sent = lax.optimization_barrier(
        (across(own_piece, 1), after(shrink_own, own_piece)[:part_ff], last_sent)
    )
    shrink_other = [swap(shrink_sent[0])]
    last_other = swap(shrink_sent[1])
    carry = attend(joined_t, onehot, own_piece, None, False, scale2, heads)
    carry = attend(joined_t, onehot, peer_piece, carry, False, scale2, heads)
    even = tie(tie(after(even, carry[0]), widen_near, 1), widen_far, 0)
    odd = across(even, 1)
    carry = attend(joined_t, onehot, even, carry, False, scale2, heads)
    grad_slots = exchange_slots(after(grad_rows, peer_piece))
    odd, grad_slots = lax.optimization_barrier((odd, grad_slots))
    out_heads, *out_low, lse = attend(joined_t, onehot, odd, carry, True, scale2, heads)
    context_t = jnp.concatenate(
        [out_low[0]] + [shift(out_low[k], "z", GROUPS, -k) for k in range(1, GROUPS)], axis=0
    )

    context_t = tie(context_t, shrink_other, 0)
    x32 = x_own.astype(F32)
    residual = x32 + dot32(context_t, final_map, (((0,), (0,))))
    unit_mid, scale_mid = norm_parts(residual)
    mid_low = (unit_mid * gain_mid).astype(BF16)
    def from_slots(values):
        return dot32(place, values, (((0,), (0,))))

    sent_rows = to_slots(mid_low)
    arrived = exchange_slots(sent_rows)
    arrived, far_pieces = lax.optimization_barrier((arrived, jnp.concatenate([odd, even], axis=0)))

    unit_columns, inverse_columns, share_columns = unit_of(embed, 0)
    routing = (
        jnp.pad(router, ((0, 0), (0, 128 - route))),
        jnp.pad(unit_columns, ((0, 128 - route), (0, 128 - experts))),
    )

    expert_info = jnp.stack([f_at, expert_at])
    hidden_own, hidden_third, *carry = run_expert(
        expert_info, arrived, grad_slots, widen, shrink_own, [*widen_near, *widen_far, *shrink_other], routing, None, experts
    )
    grad_made = carry[2]
    hidden_last, grad_pre, widen_sent, scaled, sent_back, routed_grad, columns_grad = run_expert(
        expert_info, arrived, grad_slots, widen, shrink_own, [last_other], routing, carry, experts
    )
    grad_back = exchange_slots(sent_back)

    arrived, hidden_own, hidden_third, hidden_last, grad_made, _ = lax.optimization_barrier(
        (arrived, hidden_own, hidden_third, hidden_last, grad_made, sent_back)
    )
    first, second = arrived[:, :share], arrived[:, share:]
    rows_own = jnp.where(f_at == 0, first, second)
    widen_back = swap(widen_sent)
    shrink_back = [
        dot32(value, grad_made, (((0,), (0,)))).astype(BF16)
        for value in (jnp.concatenate([hidden_third, hidden_last[:, :eighth]], axis=1), hidden_last[:, eighth:])
    ]
    grad_router_own, grad_columns = routed_grad[:route], columns_grad[:route, :experts]
    grad_embed_own = unit_back(unit_columns, inverse_columns, share_columns, grad_columns, 0)
    embed_rows = jnp.pad(
        grad_embed_own.reshape(fsdp_count, embed_share, experts), ((0, 0), (0, 0), (0, share - experts))
    )
    small = jnp.concatenate(
        [
            grad_router_own,
            jnp.concatenate([embed_rows[at] for at in range(fsdp_count)], axis=1),
            jnp.zeros((SMALL - route - embed_share, width), F32),
        ],
        axis=0,
    ).astype(BF16)
    grad_back, small, *shrink_back = lax.optimization_barrier((grad_back, small, *shrink_back))
    shrink_back[0] = swap(shrink_back[0])

    grad_mid = from_slots(grad_back)
    grad_residual = cotangent.astype(F32) + norm_back(unit_mid, scale_mid, grad_mid * gain_mid)
    grad_gain_mid = jnp.sum(grad_mid * unit_mid, axis=0)
    grad_res_low = grad_residual.astype(BF16)
    grad_context = dot32(final_map, grad_res_low, (((1,), (1,)))).astype(BF16).reshape(
        GROUPS, group_width, row_count
    )
    grad_parts = [grad_context[0]] + [shift(grad_context[k], "z", GROUPS, k) for k in range(1, GROUPS)]
    grad_t = jnp.stack(grad_parts)

    context_rows = roll_blocks(
        context_t.reshape(GROUPS, group_width, row_count), (GROUPS - z_at) % GROUPS
    ).reshape(width, row_count)
    def back(piece, running, last=False, ties=()):
        tied = lax.optimization_barrier((grad_t, *ties))
        rows = out_heads if running is None else delta
        result = attend_back(joined_t, onehot, tied[0], rows, lse, piece, running, last, scale2, heads)
        return (*result, *tied[1:])

    scaled_back = exchange_slots(after(scaled, grad_parts[1], grad_parts[3]))
    delta, running, far_both = back(far_pieces, None)
    far_odd, far_even = far_both[: odd.shape[0]], far_both[odd.shape[0] :]
    final_kept, final_sent = final_grads(core, after(grad_res_low, running), context_rows)
    final_got = across(final_sent, 1)
    finals = (final_kept.astype(F32) + final_got.astype(F32)).astype(BF16)
    finals = lax.all_to_all(finals, "z", split_axis=0, concat_axis=0, tiled=True)
    far_got = across(far_odd, 1)
    cut = far_even.shape[1] // 2

    def far_sum(part):
        return (far_even[:, part].astype(F32) + far_got[:, part].astype(F32)).astype(BF16)

    def add_far(value):
        if bits == 2:
            return across(value, 2)
        value = jnp.concatenate([jnp.zeros_like(value[:1]), value], axis=0)
        for bit in range(1, bits):
            halves = value.reshape(-1, 2, *value.shape[1:])
            value = (halves[:, 0].astype(F32) + across(halves[:, 1], 1 << bit).astype(F32)).astype(BF16)
        return value

    far, far_last = far_sum(slice(0, cut)), far_sum(slice(cut, None))
    running, near_peer, far, far_last = back(peer_piece, running, ties=(far, far_last))
    far = add_far(far)
    far_last = add_far(after(far_last, running))
    grad_query, near_own, far, scaled_back, widen_back = back(
        own_piece, running, True, ties=(far, scaled_back, widen_back)
    )

    joined, *grad_parts = gather_grads(grad_query, near_own, across(near_peer, 1), far, far_last, maps_group)
    second_part = shift(grad_parts[2], "z", GROUPS, -2)
    kept, sent = maps_product(core, joined, normed_low, small, grad_gain_mid, route + embed_share)
    grad_maps_part = (kept.astype(F32) + across(sent, 1).astype(F32)).astype(BF16)
    finals = after(finals, joined)
    final_rows = sum(finals[at].astype(F32) for at in range(GROUPS)).astype(BF16)
    grad_maps_part = jnp.concatenate([grad_maps_part, final_rows], axis=0)
    out = residual + from_slots(after(scaled_back, joined))
    x_at = (r_at >> 1) & 1
    if bits == 2:
        half_rows = grad_maps_part.shape[0] // 2

        def piece(x_bit, f_bit):
            return lax.dynamic_slice(grad_maps_part, (x_bit * half_rows, f_bit * share), (half_rows, share))

        corner = [
            (r * fsdp_count + f, (r ^ 2) * fsdp_count + (1 - f)) for r in range(ring) for f in range(fsdp_count)
        ]
        pieces = [
            piece(x_at, f_at),
            across(piece(1 - x_at, f_at), 2),
            swap(piece(x_at, 1 - f_at)),
            lax.ppermute(piece(1 - x_at, 1 - f_at), ("r", "fsdp"), corner),
        ]
        grad_maps_part = sum(value.astype(F32) for value in pieces).astype(BF16)
    else:
        for bit in range(1, bits):
            grad_maps_part = halve(grad_maps_part, 0, (r_at >> bit) & 1, lambda v: across(v, 1 << bit))
        grad_maps_part = halve(grad_maps_part, 1, f_at, swap)
    grad_maps_part, second_part, shrink_back[0] = lax.optimization_barrier((grad_maps_part, second_part, shrink_back[0]))
    shrink_back[1] = swap(after(shrink_back[1], grad_maps_part))
    groups = [grad_maps_part] + [shift(grad_maps_part, "z", GROUPS, -k) for k in (1, 2, 3)]
    first_part = shift(after(grad_parts[1], *groups), "z", GROUPS, -1)
    third_part = shift(after(grad_parts[3], *groups), "z", GROUPS, -3)
    if bits == 2:
        both = jnp.stack([*groups, *[across(value, 2) for value in groups]])
    else:
        both = jnp.stack(groups)
        for bit in range(bits - 1, 0, -1):
            got = across(both, 1 << bit)
            both = jnp.where(
                (r_at >> bit) & 1 == 0,
                jnp.concatenate([both, got], axis=1),
                jnp.concatenate([got, both], axis=1),
            )
        both = jnp.concatenate(jnp.split(both, 2, axis=1), axis=0)
        x_at = jnp.zeros_like(x_at)
    grad_up = dot32(rows_own, grad_pre, (((0,), (0,)))) + after(widen_back, grad_maps_part).astype(F32)
    grad_down = dot32(hidden_own, grad_made, (((0,), (0,)))) + jnp.concatenate(
        shrink_back, axis=0
    ).astype(F32)
    both, first_part, third_part, grad_up, grad_down = lax.optimization_barrier(
        (both, first_part, third_part, grad_up, grad_down)
    )
    grad_maps, grad_final, grad_router, grad_embed, grad_ln1, grad_ln2 = finish_shared(
        both, across(both, 1), asker_lookup_content_maps, mixer_scaling_factor, jnp.stack([z_at, core, x_at]),
        group_width, route, (embed_share, experts),
    )
    grad_router = grad_router.T

    grad_normed_in = sum(part.astype(F32) for part in (grad_parts[0], first_part, second_part, third_part))
    unit_in, scale_in = norm_parts(after(x_own, joined).astype(F32))
    grad_input = grad_residual + norm_back(unit_in, scale_in, grad_normed_in * gain_in)

    return (
        out[None].astype(BF16),
        grad_input[None],
        grad_ln1,
        grad_maps,
        grad_final,
        grad_ln2,
        grad_router,
        grad_embed,
        grad_up[None],
        grad_down[None],
    )


def solution(mesh):
    ctx_count, fsdp_count = mesh.shape["ctx"], mesh.shape["fsdp"]
    inner = Mesh(mesh.devices.reshape(GROUPS, ctx_count // GROUPS, fsdp_count), ("z", "r", "fsdp"))
    ctx = ("z", "r")
    tokens = P("fsdp", ctx, None)
    expert = P(ctx, "fsdp", None)
    halves, halves2 = P("fsdp"), P("fsdp", None)
    return jax.shard_map(
        functools.partial(body, ctx_count, fsdp_count),
        mesh=inner,
        in_specs=(
            tokens, halves, halves2, halves2, halves, halves2, halves2, expert, expert,
            P("fsdp", ctx), tokens, tokens,
        ),
        out_specs=(
            tokens, tokens, halves, halves2, halves2, halves, halves2, halves2, expert, expert,
        ),
        check_vma=False,
    )
```

```python
import functools
import math

import jax
import jax.numpy as jnp
from jax import lax
from jax.experimental import pallas as pl
from jax.experimental.pallas import tpu as pltpu
from jax.sharding import Mesh, PartitionSpec as P

HD = 64
SMALL = 64
DOCS = 8
AUX = 16
GROUPS = 4
EPSILON = 1e-05
FLOOR = 0.5
ROUTER_HEAT = 0.5
HIGHEST = lax.Precision.HIGHEST
ROOT_HALF = 0.7071067811865476
ROOT_TWO_PI = 2.5066282746310002
NEG_LARGE = -1e30
LOG2E = 1.4426950408889634
VMEM_BYTES = 62 * 1024 * 1024
VMEM_SHARED = 48 * 1024 * 1024
BF16 = jnp.bfloat16
F32 = jnp.float32


def dot32(left, right, dims):
    return lax.dot_general(left, right, (dims, ((), ())), preferred_element_type=F32)


def dot_high(left, right):
    return lax.dot_general(left, right, (((0,), (0,)), ((), ())), precision=HIGHEST)


def early_kernel(group_width, info, maps_ref, extra_ref, own_ref, sent_ref):
    width = GROUPS * group_width
    for group in range(GROUPS):

        @pl.when(info[0] == group)
        def _():
            begins = [part * width + group * group_width for part in range(3)]
            pieces = [maps_ref[:, begin : begin + group_width] for begin in begins]
            own_ref[...] = jnp.concatenate([*pieces, extra_ref[...]], axis=1)

    half = sent_ref.shape[0]
    sent_ref[...] = own_ref[pl.ds(pl.multiple_of(info[1] * half, 16), half)]


def early_rows(info, maps, extra, group_width):
    rows = maps.shape[0]
    columns = 3 * group_width + extra.shape[1]
    shapes = [(rows, columns), (rows // 2, columns)]
    return pl.pallas_call(
        functools.partial(early_kernel, group_width),
        grid_spec=pltpu.PrefetchScalarGridSpec(
            num_scalar_prefetch=1,
            grid=(1,),
            in_specs=[pl.BlockSpec(value.shape, lambda j, info: (0, 0)) for value in (maps, extra)],
            out_specs=[pl.BlockSpec(shape, lambda j, info: (0, 0)) for shape in shapes],
        ),
        out_shape=[jax.ShapeDtypeStruct(shape, BF16) for shape in shapes],
        compiler_params=pltpu.CompilerParams(vmem_limit_bytes=VMEM_BYTES),
    )(info.astype(jnp.int32), maps, extra)


def forward_kernel(scale2, first, last, q_ref, oh_ref, k_ref, v_ref, mk_ref, *rest):
    if not first:
        top_in, acc_in, *rest = rest
    if last:
        out_ref, *low_refs, lse_ref, top_sc, acc_sc = rest
    else:
        top_out, acc_out, top_sc, acc_sc = rest
    step = pl.program_id(1)
    width = k_ref.shape[-1]
    block = min(1024, width)
    pad = jnp.zeros((128 - HD - AUX, q_ref.shape[-1]), BF16)
    query = jnp.concatenate([q_ref[...], oh_ref[...], pad], axis=0)

    @pl.when(step == 0)
    def _():
        if first:
            top_sc[...] = jnp.full_like(top_sc, NEG_LARGE)
            acc_sc[...] = jnp.zeros_like(acc_sc)
        else:
            top_sc[...] = top_in[0]
            acc_sc[...] = acc_in[0]

    top, acc = top_sc[...], acc_sc[...]
    for at in range(0, width, block):
        cut = slice(at, at + block)
        aux = mk_ref[0, :, cut]
        keys = jnp.concatenate([k_ref[0, :, cut], aux, pad[:, :block]], axis=0).T
        scores = jnp.dot(keys, query, preferred_element_type=F32)
        new_top = jnp.maximum(top, jnp.max(scores, axis=0, keepdims=True))
        probs = jnp.exp2((scores - new_top) * scale2).astype(BF16)
        decay = jnp.exp2((top - new_top) * scale2)
        values = jnp.concatenate([v_ref[0, :, cut], aux], axis=0)
        acc = acc * decay + jnp.dot(values, probs, preferred_element_type=F32)
        top = new_top
    top_sc[...], acc_sc[...] = top, acc

    @pl.when(step == pl.num_programs(1) - 1)
    def _():
        if last:
            total = acc[HD + DOCS : HD + DOCS + 1]
            result = acc[:HD] / total
            out_ref[0] = result
            cut = low_refs[0].shape[-1]
            for at, low_ref in enumerate(low_refs):
                low_ref[...] = result[:, at * cut : (at + 1) * cut].astype(BF16)
            lse_ref[0] = top + jnp.log2(total) / scale2
        else:
            top_out[0] = top
            acc_out[0] = acc


def attend(query_t, onehot, pieces, carry, last, scale2, heads):
    count, _, width = pieces.shape
    rows = query_t.shape[1]
    cut = rows // GROUPS
    top_spec = pl.BlockSpec((1, 1, rows), lambda h, j: (h, 0, 0))
    acc_spec = pl.BlockSpec((1, HD + AUX, rows), lambda h, j: (h, 0, 0))
    in_specs = [
        pl.BlockSpec((HD, rows), lambda h, j: (h, 0)),
        pl.BlockSpec((AUX, rows), lambda h, j: (0, 0)),
        pl.BlockSpec((1, HD, width), lambda h, j: (j, h, 0)),
        pl.BlockSpec((1, HD, width), lambda h, j: (j, heads + h, 0)),
        pl.BlockSpec((1, AUX, width), lambda h, j: (j, 2 * heads * HD // AUX, 0)),
    ]
    if carry is not None:
        in_specs += [top_spec, acc_spec]
    top_shape = jax.ShapeDtypeStruct((heads, 1, rows), F32)
    if last:
        out_specs = [
            pl.BlockSpec((1, HD, rows), lambda h, j: (h, 0, 0)),
            *[pl.BlockSpec((HD, cut), lambda h, j: (h, 0))] * GROUPS,
            top_spec,
        ]
        out_shape = [
            jax.ShapeDtypeStruct((heads, HD, rows), F32),
            *[jax.ShapeDtypeStruct((heads * HD, cut), BF16)] * GROUPS,
            top_shape,
        ]
    else:
        out_specs = [top_spec, acc_spec]
        out_shape = [top_shape, jax.ShapeDtypeStruct((heads, HD + AUX, rows), F32)]
    return pl.pallas_call(
        functools.partial(forward_kernel, scale2, carry is None, last),
        grid=(heads, count),
        in_specs=in_specs,
        out_specs=out_specs,
        out_shape=out_shape,
        scratch_shapes=[pltpu.VMEM((1, rows), F32), pltpu.VMEM((HD + AUX, rows), F32)],
        compiler_params=pltpu.CompilerParams(vmem_limit_bytes=VMEM_SHARED),
        cost_estimate=pl.CostEstimate(
            flops=34 * heads * rows * count * width * HD, bytes_accessed=0, transcendentals=0
        ),
    )(query_t, onehot, pieces, pieces, pieces, *(carry or ()))


def split3(value):
    high = value.astype(BF16)
    rest = value - high.astype(F32)
    mid = rest.astype(BF16)
    return high, mid, (rest - mid.astype(F32)).astype(BF16)


def backward_kernel(scale2, first, last, q_ref, oh_ref, g_ref, o_ref, lse_ref, k_ref, v_ref, mk_ref, *rest):
    if not first:
        carry_ref, *rest = rest
    else:
        delta_ref, *rest = rest
    dq_ref, dkv_ref, qa_sc, ga_sc, nat_sc, dq_sc = rest
    step = pl.program_id(1)
    width = k_ref.shape[-1]
    block = width // GROUPS
    rows = q_ref.shape[-1]
    scale = 1.0 / math.sqrt(HD)
    pad = jnp.zeros((128 - HD - AUX, rows), BF16)

    @pl.when(step == 0)
    def _():
        query = q_ref[...]
        grad = jnp.concatenate([g_ref[at] for at in range(g_ref.shape[0])], axis=1)
        if first:
            delta = jnp.sum(grad.astype(F32) * o_ref[0], axis=0, keepdims=True)
            delta_ref[0] = delta
        else:
            delta = o_ref[0]
        place = lax.broadcasted_iota(jnp.int32, (AUX, rows), 0)

        def aux_rows(start, value):
            out = start
            for at, piece in enumerate(split3(-value)):
                out = jnp.where(place == DOCS + at, piece.astype(F32), out)
            return out.astype(BF16)

        qa_sc[...] = jnp.concatenate([query, aux_rows(oh_ref[...].astype(F32), lse_ref[0]), pad], axis=0)
        ga_sc[...] = jnp.concatenate([grad, aux_rows(jnp.zeros((AUX, rows), F32), delta), pad], axis=0)
        nat_sc[...] = jnp.concatenate([grad, query], axis=0).T
        if first:
            dq_sc[...] = jnp.zeros_like(dq_sc)
        else:
            dq_sc[...] = carry_ref[0]

    natural = nat_sc[...]
    for at in range(0, width, block):
        cut = slice(at, at + block)
        aux = mk_ref[0, :, cut]
        keys_t = k_ref[0, :, cut]
        keys = jnp.concatenate([keys_t, aux, pad[:, :block]], axis=0).T
        values = jnp.concatenate([v_ref[0, :, cut], aux, pad[:, :block]], axis=0).T
        probs = jnp.exp2(jnp.dot(keys, qa_sc[...], preferred_element_type=F32) * scale2)
        slopes = jnp.dot(values, ga_sc[...], preferred_element_type=F32)
        grad_scores = (probs * slopes).astype(BF16)
        from_probs = jnp.dot(probs.astype(BF16), natural, preferred_element_type=F32)
        from_scores = jnp.dot(grad_scores, natural, preferred_element_type=F32) * scale
        lane = lax.broadcasted_iota(jnp.int32, from_probs.shape, 1)
        both = jnp.where(lane < HD, from_probs, from_scores).T.astype(BF16)
        dkv_ref[0, at // block, 0] = both[HD:]
        dkv_ref[0, at // block, 1] = both[:HD]
        dq_sc[...] += jnp.dot(keys_t, grad_scores, preferred_element_type=F32)

    @pl.when(step == pl.num_programs(1) - 1)
    def _():
        if last:
            cut = dq_ref.shape[-1]
            for at in range(dq_ref.shape[0]):
                dq_ref[at] = (dq_sc[:, at * cut : (at + 1) * cut] * scale).astype(BF16)
        else:
            dq_ref[0] = dq_sc[...]


def attend_back(query_t, onehot, grad_t, out_heads, lse, pieces, carry, last, scale2, heads):
    count, _, width = pieces.shape
    rows = query_t.shape[1]
    cut = rows // GROUPS
    block = width // GROUPS
    blocks = width // block
    sum_spec = pl.BlockSpec((1, HD, rows), lambda h, j: (h, 0, 0))
    cut_spec = pl.BlockSpec((GROUPS, HD, cut), lambda h, j: (0, h, 0))
    row_spec = pl.BlockSpec((1, 1, rows), lambda h, j: (h, 0, 0))
    in_specs = [
        pl.BlockSpec((HD, rows), lambda h, j: (h, 0)),
        pl.BlockSpec((AUX, rows), lambda h, j: (0, 0)),
        cut_spec,
        sum_spec if carry is None else row_spec,
        row_spec,
        pl.BlockSpec((1, HD, width), lambda h, j: (j, h, 0)),
        pl.BlockSpec((1, HD, width), lambda h, j: (j, heads + h, 0)),
        pl.BlockSpec((1, AUX, width), lambda h, j: (j, 2 * heads * HD // AUX, 0)),
    ]
    if carry is not None:
        in_specs += [sum_spec]
    dq_shape = (GROUPS, heads * HD, cut) if last else (heads, HD, rows)
    return pl.pallas_call(
        functools.partial(backward_kernel, scale2, carry is None, last),
        grid=(heads, count),
        in_specs=in_specs,
        out_specs=([row_spec] if carry is None else [])
        + [
            cut_spec if last else sum_spec,
            pl.BlockSpec((1, blocks, 2, HD, block), lambda h, j: (j, 0, 0, h, 0)),
        ],
        out_shape=([jax.ShapeDtypeStruct((heads, 1, rows), F32)] if carry is None else [])
        + [
            jax.ShapeDtypeStruct(dq_shape, BF16 if last else F32),
            jax.ShapeDtypeStruct((count, blocks, 2, heads * HD, block), BF16),
        ],
        scratch_shapes=[
            pltpu.VMEM((128, rows), BF16),
            pltpu.VMEM((128, rows), BF16),
            pltpu.VMEM((rows, 128), BF16),
            pltpu.VMEM((HD, rows), F32),
        ],
        compiler_params=pltpu.CompilerParams(vmem_limit_bytes=VMEM_SHARED),
        cost_estimate=pl.CostEstimate(
            flops=15 * heads * rows * count * width * HD, bytes_accessed=0, transcendentals=0
        ),
    )(query_t, onehot, grad_t, out_heads, lse, pieces, pieces, pieces, *([] if carry is None else [carry]))


def route_parts(rows, router, columns, expert, expert_count):
    project = jnp.dot(rows, router, preferred_element_type=F32)
    size = jnp.sqrt(jnp.sum(project * project, axis=-1, keepdims=True))
    along = jnp.where(size > FLOOR, 1.0, jnp.where(size == FLOOR, 0.5, 0.0))
    inverse = 1.0 / jnp.maximum(size, FLOOR)
    unit = project * inverse
    logits = jnp.dot(unit, columns, precision=HIGHEST, preferred_element_type=F32) / ROUTER_HEAT
    lane = lax.broadcasted_iota(jnp.int32, logits.shape, 1)
    logits = jnp.where(lane < expert_count, logits, NEG_LARGE)
    raised = jnp.exp(logits - jnp.max(logits, axis=-1, keepdims=True))
    chances = raised / jnp.sum(raised, axis=-1, keepdims=True)
    mine = (lane == expert).astype(F32)
    gate = jnp.sum(chances * mine, axis=-1, keepdims=True)
    return unit, inverse, along, chances, mine, gate


def expert_kernel(first, expert_count, begin, info, x_ref, g_ref, uo_ref, so_ref, router_ref, columns_ref, *rest):
    steps = 3 if first else 1
    if first:
        *ux_refs, sx_ref = rest[: steps + 1]
        rest = rest[steps + 1 :]
    else:
        both_ref, *rest = rest
    if first:
        own_ref, hidden_ref, gp_ref, gw_ref, gm_ref, made_ref, gin_ref, up_sc, down_sc, turned_sc = rest
    else:
        gm_ref, made_in, gin_in, _, _, *rest = rest
        hidden_ref, gp_ref, gw_ref, scaled_ref, back_ref, routed_ref, columns_out, *rest = rest
        up_sc, down_sc, turned_sc, made_ref, gin_ref = rest
    step = pl.program_id(0)
    share, block = uo_ref.shape

    @pl.when(step == 0)
    def _():
        cut = pl.ds(pl.multiple_of((1 - info[0]) * share, 128), share)
        turned_sc[...] = x_ref[:, cut].T
        if first:
            gate = route_parts(x_ref[...], router_ref[...], columns_ref[...], info[1], expert_count)[-1]
            gm_ref[...] = (gate * g_ref[...].astype(F32)).astype(BF16)
            made_ref[...] = jnp.zeros_like(made_ref)
            gin_ref[...] = jnp.zeros_like(gin_ref)
        else:
            made_ref[...] = made_in[...]
            gin_ref[...] = gin_in[...]

    up_sc[pl.ds(pl.multiple_of(info[0] * share, 128), share)] = uo_ref[...]
    other = pl.ds(pl.multiple_of((1 - info[0]) * share, 128), share)
    for now in range(steps):

        @pl.when(step == now)
        def _():
            up_sc[other] = ux_refs[now][...] if first else both_ref[:share]
            if begin + now < 2:
                down_sc[...] = so_ref[...]
            else:
                down_sc[...] = sx_ref[...] if first else both_ref[share:]

    up, down = up_sc[...], down_sc[...]
    piece = x_ref.shape[0] // 2
    for begin_row in (0, piece):
        rows = slice(begin_row, begin_row + piece)
        pre_act = jnp.dot(x_ref[rows], up, preferred_element_type=F32)
        grad_hidden = dot32(gm_ref[rows], down, (((1,), (1,))))
        bell = 0.5 * (1.0 + lax.erf(pre_act * ROOT_HALF))
        hidden = (pre_act * bell).astype(BF16)
        hidden_ref[rows] = hidden
        made_ref[rows] += jnp.dot(hidden, down, preferred_element_type=F32)
        slope = bell + pre_act * (jnp.exp(-0.5 * pre_act * pre_act) * (1.0 / ROOT_TWO_PI))
        grad_pre = (grad_hidden * slope).astype(BF16)
        gp_ref[rows] = grad_pre
        gin_ref[rows] += dot32(grad_pre, up, (((1,), (1,))))
    if first:

        @pl.when(step < 2)
        def _():
            own_ref[...] = hidden_ref[...]

    gw_ref[...] = jnp.dot(turned_sc[...], gp_ref[...], preferred_element_type=F32).astype(BF16)

    if not first:
        router, columns = router_ref[...], columns_ref[...]
        unit, inverse, along, chances, mine, gate = route_parts(x_ref[...], router, columns, info[1], expert_count)
        made = made_ref[...].astype(BF16).astype(F32)
        scaled_ref[...] = (gate * made).astype(BF16)
        grad_gate = jnp.sum(g_ref[...].astype(F32) * made, axis=-1, keepdims=True)
        dlogit = grad_gate * gate * (mine - chances) / ROUTER_HEAT
        dunit = lax.dot_general(
            dlogit, columns, (((1,), (1,)), ((), ())), precision=HIGHEST, preferred_element_type=F32
        )
        dproj = inverse * (dunit - along * unit * jnp.sum(unit * dunit, axis=-1, keepdims=True))
        high = dproj.astype(BF16)
        low = (dproj - high.astype(F32)).astype(BF16)
        back = dot32(high, router, (((1,), (1,)))) + dot32(low, router, (((1,), (1,))))
        back_ref[...] = (gin_ref[...].astype(BF16).astype(F32) + back).astype(BF16)
        rows = x_ref[...]
        routed_ref[...] = jnp.dot(high.astype(F32).T.astype(BF16), rows, preferred_element_type=F32) + jnp.dot(
            low.astype(F32).T.astype(BF16), rows, preferred_element_type=F32
        )
        columns_out[...] = jnp.dot(unit.T, dlogit, precision=HIGHEST, preferred_element_type=F32)


def run_expert(info, rows, grads, widen, shrink, others, routing, carry, expert_count):
    slots, width = rows.shape
    share, units = widen.shape
    block = units // 4
    first = carry is None
    begin = 0 if first else 3

    def at(j, info):
        return lax.rem(2 * info[0] + begin + j, 4)

    whole = pl.BlockSpec((slots, width), lambda j, info: (0, 0))
    quarter = pl.BlockSpec((slots, block), lambda j, info: (0, 0))
    part = jax.ShapeDtypeStruct((slots, units), BF16)
    part_spec = pl.BlockSpec((slots, block), lambda j, info: (0, at(j, info)))
    low = jax.ShapeDtypeStruct((slots, width), BF16)
    full = jax.ShapeDtypeStruct((slots, width), F32)
    fixed = [*routing, *others]
    in_specs = [
        whole,
        whole,
        pl.BlockSpec((share, block), lambda j, info: (0, at(j, info))),
        pl.BlockSpec((block, width), lambda j, info: (jnp.minimum(j, 1), 0)),
        *[pl.BlockSpec(value.shape, lambda j, info: (0, 0)) for value in fixed],
    ]
    operands = [rows, grads, widen, shrink, *fixed]
    scratch = [pltpu.VMEM((width, block), BF16), pltpu.VMEM((block, width), BF16), pltpu.VMEM((share, slots), BF16)]
    sent = jax.ShapeDtypeStruct((share, units), BF16)
    sent_spec = pl.BlockSpec((share, block), lambda j, info: (0, at(j, info)))
    aliases = {}
    if first:
        own = jax.ShapeDtypeStruct((slots, 2 * block), BF16)
        out_specs = [
            pl.BlockSpec((slots, block), lambda j, info: (0, jnp.minimum(j, 1))), quarter, part_spec, sent_spec,
            whole, whole, whole,
        ]
        out_shape = [own, jax.ShapeDtypeStruct((slots, block), BF16), part, sent, low, full, full]
    else:
        grad_pre, widen_sent, grad_made, made, grad_inputs = carry
        in_specs += [whole, whole, whole] + [pl.BlockSpec(memory_space=pl.ANY)] * 2
        operands += [grad_made, made, grad_inputs, grad_pre, widen_sent]
        aliases = {len(operands) - 1: 1, len(operands): 2}
        tops = [jax.ShapeDtypeStruct((128, width), F32), jax.ShapeDtypeStruct((128, 128), F32)]
        out_specs = [quarter, part_spec, sent_spec, whole, whole]
        out_specs += [pl.BlockSpec(v.shape, lambda j, info: (0, 0)) for v in tops]
        out_shape = [jax.ShapeDtypeStruct((slots, block), BF16), part, sent, low, low, *tops]
        scratch += [pltpu.VMEM((slots, width), F32), pltpu.VMEM((slots, width), F32)]
    return pl.pallas_call(
        functools.partial(expert_kernel, first, expert_count, begin),
        grid_spec=pltpu.PrefetchScalarGridSpec(
            num_scalar_prefetch=1,
            grid=(3 if first else 1,),
            in_specs=in_specs,
            out_specs=out_specs,
            scratch_shapes=scratch,
        ),
        out_shape=out_shape,
        input_output_aliases=aliases,
        compiler_params=pltpu.CompilerParams(vmem_limit_bytes=VMEM_BYTES),
        cost_estimate=pl.CostEstimate(
            flops=(2 if first else 1) * slots * width * units, bytes_accessed=0, transcendentals=0
        ),
    )(info.astype(jnp.int32), *operands)


def final_kernel(info, g_ref, c_ref, kept_ref, sent_ref, all_sc):
    all_sc[...] = dot32(g_ref[...].T, c_ref[...], (((1,), (1,)))).astype(BF16)
    count, half = kept_ref.shape[:2]
    for at in range(count):
        for ref, core in ((kept_ref, info[0]), (sent_ref, 1 - info[0])):
            ref[at] = all_sc[pl.ds(pl.multiple_of((2 * at + core) * half, 16), half)]


def final_grads(core, grads, context):
    width = grads.shape[1]
    shape = (GROUPS, width // GROUPS // 2, context.shape[0])
    return pl.pallas_call(
        final_kernel,
        grid_spec=pltpu.PrefetchScalarGridSpec(
            num_scalar_prefetch=1,
            grid=(1,),
            in_specs=[pl.BlockSpec(value.shape, lambda j, info: (0, 0)) for value in (grads, context)],
            out_specs=[pl.BlockSpec(shape, lambda j, info: (0, 0, 0))] * 2,
            scratch_shapes=[pltpu.VMEM((width, context.shape[0]), BF16)],
        ),
        out_shape=[jax.ShapeDtypeStruct(shape, BF16)] * 2,
        compiler_params=pltpu.CompilerParams(vmem_limit_bytes=VMEM_BYTES),
    )(core[None].astype(jnp.int32), grads, context)


def gather_kernel(row, info, dq_ref, own_ref, got_ref, far0_ref, far1_ref, x_ref, w_ref, small_ref, gain_ref, *rest):
    *part_refs, kept_ref, sent_ref, acc_sc, all_sc = rest
    step = pl.program_id(0)
    far = jnp.where(step < GROUPS // 2, far0_ref[0, 0].astype(F32), far1_ref[0, 0].astype(F32))
    grad_kv = (own_ref[0, 0].astype(F32) + got_ref[0, 0].astype(F32) + far).astype(BF16)
    joined = jnp.concatenate([dq_ref[0], grad_kv[0], grad_kv[1]], axis=0)
    product = jnp.dot(joined, x_ref[...], preferred_element_type=F32)
    through = dot32(joined.T, w_ref[...], (((1,), (1,)))).astype(BF16)
    for at in range(GROUPS):

        @pl.when(step == at)
        def _():
            part_refs[at][...] = through
            if at == 0:
                acc_sc[...] = product
            else:
                acc_sc[...] += product

    @pl.when(step == pl.num_programs(0) - 1)
    def _():
        rows = acc_sc.shape[0]
        all_sc[:rows] = acc_sc[...].astype(BF16)
        place = lax.broadcasted_iota(jnp.int32, small_ref.shape, 0)
        all_sc[rows:] = jnp.where(place == row, gain_ref[...], small_ref[...].astype(F32)).astype(BF16)
        half = kept_ref.shape[0]
        kept_ref[...] = all_sc[pl.ds(pl.multiple_of(info[0] * half, 16), half)]
        sent_ref[...] = all_sc[pl.ds(pl.multiple_of((1 - info[0]) * half, 16), half)]


def gather_grads(core, grad_query, near_own, near_got, far, far_last, normed, maps, small, gain_grad, row):
    group_width, cut = grad_query.shape[1:]
    width = maps.shape[0]
    half = GROUPS // 2
    rows = 3 * group_width
    total = rows + small.shape[0]
    piece = (1, 1, 2, group_width, cut)

    def fixed(shape):
        return pl.BlockSpec(shape, lambda j, info: (0, 0))

    return pl.pallas_call(
        functools.partial(gather_kernel, row),
        grid_spec=pltpu.PrefetchScalarGridSpec(
            num_scalar_prefetch=1,
            grid=(GROUPS,),
            in_specs=[
                pl.BlockSpec((1, group_width, cut), lambda j, info: (j, 0, 0)),
                pl.BlockSpec(piece, lambda j, info: (0, j, 0, 0, 0)),
                pl.BlockSpec(piece, lambda j, info: (0, j, 0, 0, 0)),
                pl.BlockSpec(piece, lambda j, info: (0, jnp.minimum(j, half - 1), 0, 0, 0)),
                pl.BlockSpec(piece, lambda j, info: (0, jnp.maximum(j - half, 0), 0, 0, 0)),
                pl.BlockSpec((cut, width), lambda j, info: (j, 0)),
                fixed(maps.shape),
                fixed(small.shape),
                fixed((1, width)),
            ],
            out_specs=[fixed((cut, width))] * GROUPS + [fixed((total // 2, width))] * 2,
            scratch_shapes=[pltpu.VMEM((rows, width), F32), pltpu.VMEM((total, width), BF16)],
        ),
        out_shape=[jax.ShapeDtypeStruct((cut, width), BF16)] * GROUPS
        + [jax.ShapeDtypeStruct((total // 2, width), BF16)] * 2,
        compiler_params=pltpu.CompilerParams(vmem_limit_bytes=VMEM_BYTES),
        cost_estimate=pl.CostEstimate(flops=16 * group_width * GROUPS * cut * width, bytes_accessed=0, transcendentals=0),
    )(
        core[None].astype(jnp.int32), grad_query, near_own, near_got, far, far_last, normed, maps, small, gain_grad[None]
    )


def finish_kernel(
    group_width, info, own_ref, got_ref, w_ref, gain_ref, maps_ref, final_ref, router_ref, embed_ref, ln1_ref, ln2_ref,
    v_ref,
):
    final_half = group_width // 2
    part = own_ref.shape[1]
    half = 2 * part - final_half
    for ref, core in ((own_ref, info[1]), (got_ref, 1 - info[1])):
        low_rows = pl.ds(pl.multiple_of(core * half, 16), part)
        high_rows = pl.ds(pl.multiple_of(core * half + part, 16), half - part)
        final_rows = pl.ds(pl.multiple_of(2 * half + core * final_half, 16), final_half)
        for k in range(GROUPS):
            v_ref[k, low_rows] = ref[k + GROUPS * info[2]]
            high = ref[k + GROUPS * (1 - info[2])]
            v_ref[k, high_rows] = high[: half - part]
            v_ref[k, final_rows] = high[half - part :]

    def columns(pair, begin):
        rows = pl.ds(begin, group_width)
        halves = [v_ref[lax.rem(2 * pair + k + GROUPS - info[0], GROUPS), rows] for k in range(2)]
        return jnp.concatenate(halves, axis=0).astype(F32).T

    total = 0.0
    for part in range(3):
        for pair in range(GROUPS // 2):
            value = columns(pair, part * group_width)
            at = (part * GROUPS + 2 * pair) * group_width
            cut = slice(at, at + 2 * group_width)
            maps_ref[:, cut] = value
            total = total + jnp.sum(value * w_ref[:, cut].astype(F32), axis=1, keepdims=True)
    for pair in range(GROUPS // 2):
        at = 2 * pair * group_width
        final_ref[:, at : at + 2 * group_width] = columns(pair, 2 * half)
    small = sum(v_ref[k, 3 * group_width : 2 * half].astype(F32) for k in range(GROUPS))
    route, embed = router_ref.shape[0], embed_ref.shape[0]
    rows = small.shape[1]
    router_ref[...] = small[:route]
    embed_ref[...] = small[route : route + embed, : embed_ref.shape[1]]
    ln2_ref[...] = small[route + embed]
    ln1_ref[...] = (jnp.broadcast_to(total, (rows, 128)).T[:1] / gain_ref[...].astype(F32))[0]


def finish_shared(own, got, weights, gain, info, group_width, route, embed_shape):
    rows, columns = weights.shape
    shapes = [(rows, columns), (rows, GROUPS * group_width), (route, rows), embed_shape, (rows,), (rows,)]
    return pl.pallas_call(
        functools.partial(finish_kernel, group_width),
        grid_spec=pltpu.PrefetchScalarGridSpec(
            num_scalar_prefetch=1,
            grid=(1,),
            in_specs=[
                pl.BlockSpec(own.shape, lambda j, info: (0, 0, 0)),
                pl.BlockSpec(got.shape, lambda j, info: (0, 0, 0)),
                pl.BlockSpec(weights.shape, lambda j, info: (0, 0)),
                pl.BlockSpec((1, rows), lambda j, info: (0, 0)),
            ],
            out_specs=[pl.BlockSpec(shape, lambda j, info, rank=len(shape): (0,) * rank) for shape in shapes],
            scratch_shapes=[pltpu.VMEM((GROUPS, 4 * own.shape[1], rows), BF16)],
        ),
        out_shape=[jax.ShapeDtypeStruct(shape, F32) for shape in shapes],
        compiler_params=pltpu.CompilerParams(vmem_limit_bytes=VMEM_SHARED),
    )(info.astype(jnp.int32), own, got, weights, gain[None])


def norm_parts(values):
    center = values - jnp.mean(values, axis=-1, keepdims=True)
    scale = lax.rsqrt(jnp.mean(center * center, axis=-1, keepdims=True) + EPSILON)
    return center * scale, scale


def norm_back(unit, scale, scaled_grad):
    along = jnp.mean(scaled_grad * unit, axis=-1, keepdims=True)
    return scale * (scaled_grad - jnp.mean(scaled_grad, axis=-1, keepdims=True) - unit * along)


def unit_of(vectors, axis):
    size = jnp.sqrt(jnp.sum(vectors * vectors, axis=axis, keepdims=True))
    share = jnp.where(size > FLOOR, 1.0, jnp.where(size == FLOOR, 0.5, 0.0))
    inverse = 1.0 / jnp.maximum(size, FLOOR)
    return vectors * inverse, inverse, share


def unit_back(unit, inverse, share, grad, axis):
    return inverse * (grad - share * unit * jnp.sum(unit * grad, axis=axis, keepdims=True))


def shift(value, axis, size, by):
    return lax.ppermute(value, axis, [(at, (at + by) % size) for at in range(size)])


def flip(value, axis, size, bit):
    return lax.ppermute(value, axis, [(at, at ^ bit) for at in range(size)])


def after(value, *others):
    return lax.optimization_barrier((value, *others))[0]


def line_gather(value, axis, size, tied):
    upward, downward, from_low, from_high = value, value, [], []
    for hop in range(size - 1):
        upward = tied(hop, upward)
        upward = lax.ppermute(upward, axis, [(at, at + 1) for at in range(hop, size - 1)])
        downward = lax.ppermute(downward, axis, [(at, at - 1) for at in range(size - 1 - hop, 0, -1)])
        from_low.append(upward)
        from_high.append(downward)
    return [value] + [from_low[k] + from_high[size - 2 - k] for k in range(size - 1)]


def roll_blocks(blocks, start):
    return lax.dynamic_slice_in_dim(jnp.concatenate([blocks, blocks], axis=0), start, blocks.shape[0], 0)


def pair_order(own, other, at):
    return jnp.where(at == 0, jnp.concatenate([own, other], 0), jnp.concatenate([other, own], 0))


def body(
    ctx_count,
    fsdp_count,
    incoming_sequence,
    mixer_scaling_factor,
    asker_lookup_content_maps,
    mixer_final_map,
    specialist_scaling_factor,
    dispatch_space_map,
    specialist_dispatch_vectors,
    specialist_widen_weights_pair,
    specialist_shrink_weights_pair,
    document_labels,
    piece_specialist_choice,
    result_cotangent_array,
):
    row_count = incoming_sequence.shape[1]
    width = incoming_sequence.shape[2]
    head_count = width // HD
    heads = head_count // GROUPS
    group_width = heads * HD
    ring = ctx_count // GROUPS
    bits = ring.bit_length() - 1
    scale2 = LOG2E / math.sqrt(HD)
    z_at = lax.axis_index("z")
    r_at = lax.axis_index("r")
    f_at = lax.axis_index("fsdp")
    core = r_at & 1
    expert_at = z_at * ring + r_at
    share = width // fsdp_count
    capacity = max(2, 2 * row_count // ctx_count)
    slots = ctx_count * capacity

    def swap(value):
        return flip(value, "fsdp", fsdp_count, 1)

    def across(value, bit):
        return flip(value, "r", ring, bit)

    def exchange_slots(rows):
        return lax.all_to_all(
            rows.reshape(ctx_count, capacity, -1), ("z", "r"), split_axis=0, concat_axis=0, tiled=True
        ).reshape(slots, -1)

    def both_cores(got):
        return pair_order(got, across(got, 1), core)

    def halve(value, axis, flag, send):
        half = value.shape[axis] // 2
        kept = lax.dynamic_slice_in_dim(value, flag * half, half, axis)
        sent = lax.dynamic_slice_in_dim(value, (1 - flag) * half, half, axis)
        return (kept.astype(F32) + send(sent).astype(F32)).astype(BF16)

    def by_fsdp(own, other, axis):
        return jnp.where(
            f_at == 0,
            jnp.concatenate([own, other], axis=axis),
            jnp.concatenate([other, own], axis=axis),
        )

    route, experts = specialist_dispatch_vectors.shape[0] * fsdp_count, specialist_dispatch_vectors.shape[1]
    embed_share = route // fsdp_count
    extras = [
        mixer_scaling_factor[:, None],
        specialist_scaling_factor[:, None],
        dispatch_space_map,
        jnp.pad(specialist_dispatch_vectors, ((0, share - embed_share), (0, 0))),
    ]
    edges = [0, 3 * group_width]
    for value in extras:
        edges.append(edges[-1] + value.shape[1])
    extras.append(jnp.zeros((share, -edges[-1] % 128), BF16))
    early_own, early_sent = early_rows(
        jnp.stack([z_at, core]), asker_lookup_content_maps, jnp.concatenate(extras, axis=1), group_width
    )
    half = share // 2
    final_sent = lax.dynamic_slice_in_dim(mixer_final_map, core * half, half, 0)

    widen = specialist_widen_weights_pair[0]
    shrink_own = specialist_shrink_weights_pair[0]
    half_ff = shrink_own.shape[0]
    part_ff = half_ff // 2
    eighth = half_ff // 4
    early_pieces = []

    def widen_piece(which, at, *others):
        return lax.dynamic_slice_in_dim(after(widen, *others), (which * 2 + at) * part_ff, part_ff, 1)

    def tie(value, pieces, at):
        value, pieces[at] = lax.optimization_barrier((value, pieces[at]))
        return value

    def hop_tie(hop, value):
        if hop == 1:
            value, *sent = lax.optimization_barrier((value, early_sent, final_sent))
            early_pieces.extend([swap(piece) for piece in sent])
        return value

    x_own = incoming_sequence[0]
    label_rows = jnp.zeros((16, width), BF16).at[0, :row_count].set(document_labels[0].astype(BF16))
    blocks = line_gather(jnp.concatenate([x_own, label_rows], axis=0), "z", GROUPS, hop_tie)
    x_all = jnp.concatenate([piece[:row_count] for piece in blocks], axis=0)
    labels = jnp.concatenate([piece[row_count, :row_count] for piece in blocks], axis=0)

    widen_near = [swap(widen_piece(1 - f_at, at, *early_pieces)) for at in range(2)]
    widen_far = [swap(widen_piece(f_at, 0, *early_pieces))]
    widen_last = widen_piece(f_at, 1, *early_pieces)
    early_full = pair_order(early_own, both_cores(early_pieces[0]), f_at)
    maps_group, gain_in, gain_mid, router, embed = (
        early_full[:, begin:end] for begin, end in zip(edges[:-1], edges[1:])
    )
    gain_in, gain_mid = gain_in[:, 0].astype(F32), gain_mid[:, 0].astype(F32)
    embed = embed.reshape(fsdp_count, share, experts)[:, :embed_share].reshape(route, experts).astype(F32)
    final_map = roll_blocks(
        pair_order(mixer_final_map, both_cores(early_pieces[1]), f_at).reshape(GROUPS, group_width, width), z_at
    ).reshape(width, width)

    picked = piece_specialist_choice[0, :, 0]
    hits = (picked[:, None] == jnp.arange(ctx_count, dtype=jnp.int32)[None, :]).astype(jnp.int32)
    slot_rank = jnp.sum(jnp.cumsum(hits, axis=0) * hits, axis=1) - 1
    slot_index = picked * capacity + slot_rank
    place = (jnp.arange(slots, dtype=jnp.int32)[:, None] == slot_index[None, :]).astype(BF16)
    cotangent = result_cotangent_array[0]

    def to_slots(values):
        return jnp.dot(place, values, preferred_element_type=F32).astype(BF16)

    x_all = tie(x_all, widen_near, 0)
    x_all, final_map, grad_rows = lax.optimization_barrier((x_all, final_map, to_slots(cotangent)))
    unit_all, _ = norm_parts(x_all.astype(F32))
    normed_low = (unit_all * gain_in).astype(BF16)
    joined_t = dot32(maps_group, normed_low, (((0,), (1,)))).astype(BF16)
    aux_at = jnp.arange(AUX, dtype=jnp.int32)[:, None]
    same = labels.astype(jnp.int32)[None, :] == aux_at
    onehot = same.astype(BF16)
    key_aux = jnp.where(
        aux_at < DOCS, jnp.where(same, 0.0, NEG_LARGE), jnp.where(aux_at < DOCS + 3, 1.0, 0.0)
    ).astype(BF16)
    own_piece = jnp.concatenate([joined_t[group_width:], key_aux], axis=0)[None]
    even = own_piece
    for bit in range(bits - 1, 0, -1):
        even = jnp.stack([even, across(even, 1 << bit)], axis=1).reshape(-1, *own_piece.shape[1:])
    even = even[1:]
    last_sent = jnp.concatenate([widen_last, after(shrink_own, own_piece)[part_ff:]], axis=0)
    peer_piece, *shrink_sent = lax.optimization_barrier(
        (across(own_piece, 1), after(shrink_own, own_piece)[:part_ff], last_sent)
    )
    shrink_other = [swap(shrink_sent[0])]
    last_other = swap(shrink_sent[1])
    carry = attend(joined_t, onehot, own_piece, None, False, scale2, heads)
    carry = attend(joined_t, onehot, peer_piece, carry, False, scale2, heads)
    even = tie(tie(after(even, carry[0]), widen_near, 1), widen_far, 0)
    odd = across(even, 1)
    carry = attend(joined_t, onehot, even, carry, False, scale2, heads)
    grad_slots = exchange_slots(after(grad_rows, peer_piece))
    odd, grad_slots = lax.optimization_barrier((odd, grad_slots))
    out_heads, *out_low, lse = attend(joined_t, onehot, odd, carry, True, scale2, heads)
    context_t = jnp.concatenate(
        [out_low[0]] + [shift(out_low[k], "z", GROUPS, -k) for k in range(1, GROUPS)], axis=0
    )

    context_t = tie(context_t, shrink_other, 0)
    x32 = x_own.astype(F32)
    residual = x32 + dot32(context_t, final_map, (((0,), (0,))))
    unit_mid, scale_mid = norm_parts(residual)
    mid_low = (unit_mid * gain_mid).astype(BF16)
    def from_slots(values):
        return dot32(place, values, (((0,), (0,))))

    sent_rows = to_slots(mid_low)
    arrived = exchange_slots(sent_rows)
    arrived, far_pieces = lax.optimization_barrier((arrived, jnp.concatenate([odd, even], axis=0)))

    unit_columns, inverse_columns, share_columns = unit_of(embed, 0)
    routing = (
        jnp.pad(router, ((0, 0), (0, 128 - route))),
        jnp.pad(unit_columns, ((0, 128 - route), (0, 128 - experts))),
    )

    expert_info = jnp.stack([f_at, expert_at])
    hidden_own, hidden_third, *carry = run_expert(
        expert_info, arrived, grad_slots, widen, shrink_own, [*widen_near, *widen_far, *shrink_other], routing, None, experts
    )
    grad_made = carry[2]
    hidden_last, grad_pre, widen_sent, scaled, sent_back, routed_grad, columns_grad = run_expert(
        expert_info, arrived, grad_slots, widen, shrink_own, [last_other], routing, carry, experts
    )
    grad_back = exchange_slots(sent_back)

    arrived, hidden_own, hidden_third, hidden_last, grad_made, _ = lax.optimization_barrier(
        (arrived, hidden_own, hidden_third, hidden_last, grad_made, sent_back)
    )
    first, second = arrived[:, :share], arrived[:, share:]
    rows_own = jnp.where(f_at == 0, first, second)
    widen_back = swap(widen_sent)
    shrink_back = [
        dot32(value, grad_made, (((0,), (0,)))).astype(BF16)
        for value in (hidden_third, hidden_last)
    ]
    grad_router_own, grad_columns = routed_grad[:route], columns_grad[:route, :experts]
    grad_embed_own = unit_back(unit_columns, inverse_columns, share_columns, grad_columns, 0)
    embed_rows = jnp.pad(
        grad_embed_own.reshape(fsdp_count, embed_share, experts), ((0, 0), (0, 0), (0, share - experts))
    )
    small = jnp.concatenate(
        [
            grad_router_own,
            jnp.concatenate([embed_rows[at] for at in range(fsdp_count)], axis=1),
            jnp.zeros((SMALL - route - embed_share, width), F32),
        ],
        axis=0,
    ).astype(BF16)
    grad_back, small, *shrink_back = lax.optimization_barrier((grad_back, small, *shrink_back))
    shrink_back[0] = swap(shrink_back[0])

    grad_mid = from_slots(grad_back)
    grad_residual = cotangent.astype(F32) + norm_back(unit_mid, scale_mid, grad_mid * gain_mid)
    grad_gain_mid = jnp.sum(grad_mid * unit_mid, axis=0)
    grad_res_low = grad_residual.astype(BF16)
    grad_context = dot32(final_map, grad_res_low, (((1,), (1,)))).astype(BF16).reshape(
        GROUPS, group_width, row_count
    )
    grad_parts = [grad_context[0]] + [shift(grad_context[k], "z", GROUPS, k) for k in range(1, GROUPS)]
    grad_t = jnp.stack(grad_parts)

    context_rows = roll_blocks(
        context_t.reshape(GROUPS, group_width, row_count), (GROUPS - z_at) % GROUPS
    ).reshape(width, row_count)
    def back(piece, running, last=False, ties=()):
        tied = lax.optimization_barrier((grad_t, *ties))
        rows = out_heads if running is None else delta
        result = attend_back(joined_t, onehot, tied[0], rows, lse, piece, running, last, scale2, heads)
        return (*result, *tied[1:])

    scaled_back = exchange_slots(after(scaled, grad_parts[1], grad_parts[3]))
    delta, running, far_both = back(far_pieces, None)
    far_odd, far_even = far_both[: odd.shape[0]], far_both[odd.shape[0] :]
    final_kept, final_sent = final_grads(core, after(grad_res_low, running), context_rows)
    final_got = across(final_sent, 1)
    finals = (final_kept.astype(F32) + final_got.astype(F32)).astype(BF16)
    finals = lax.all_to_all(finals, "z", split_axis=0, concat_axis=0, tiled=True)
    far_got = across(far_odd, 1)
    cut = far_even.shape[1] // 2

    def far_sum(part):
        return (far_even[:, part].astype(F32) + far_got[:, part].astype(F32)).astype(BF16)

    def add_far(value):
        if bits == 2:
            return across(value, 2)
        value = jnp.concatenate([jnp.zeros_like(value[:1]), value], axis=0)
        for bit in range(1, bits):
            halves = value.reshape(-1, 2, *value.shape[1:])
            value = (halves[:, 0].astype(F32) + across(halves[:, 1], 1 << bit).astype(F32)).astype(BF16)
        return value

    far, far_last = far_sum(slice(0, cut)), far_sum(slice(cut, None))
    running, near_peer, far, far_last = back(peer_piece, running, ties=(far, far_last))
    far = add_far(far)
    far_last = add_far(after(far_last, running))
    grad_query, near_own, far, scaled_back, widen_back = back(
        own_piece, running, True, ties=(far, scaled_back, widen_back)
    )

    *grad_parts, kept, sent = gather_grads(
        core, grad_query, near_own, across(near_peer, 1), far, far_last, normed_low, maps_group, small, grad_gain_mid,
        route + embed_share,
    )
    second_part = shift(grad_parts[2], "z", GROUPS, -2)
    grad_maps_part = (kept.astype(F32) + across(sent, 1).astype(F32)).astype(BF16)
    finals = after(finals, kept)
    final_rows = sum(finals[at].astype(F32) for at in range(GROUPS)).astype(BF16)
    grad_maps_part = jnp.concatenate([grad_maps_part, final_rows], axis=0)
    out = residual + from_slots(after(scaled_back, kept))
    x_at = (r_at >> 1) & 1
    if bits == 2:
        half_rows = grad_maps_part.shape[0] // 2

        def piece(x_bit, f_bit):
            return lax.dynamic_slice(grad_maps_part, (x_bit * half_rows, f_bit * share), (half_rows, share))

        corner = [
            (r * fsdp_count + f, (r ^ 2) * fsdp_count + (1 - f)) for r in range(ring) for f in range(fsdp_count)
        ]
        pieces = [
            piece(x_at, f_at),
            across(piece(1 - x_at, f_at), 2),
            swap(piece(x_at, 1 - f_at)),
            lax.ppermute(piece(1 - x_at, 1 - f_at), ("r", "fsdp"), corner),
        ]
        grad_maps_part = sum(value.astype(F32) for value in pieces).astype(BF16)
    else:
        for bit in range(1, bits):
            grad_maps_part = halve(grad_maps_part, 0, (r_at >> bit) & 1, lambda v: across(v, 1 << bit))
        grad_maps_part = halve(grad_maps_part, 1, f_at, swap)
    grad_maps_part, second_part, shrink_back[0] = lax.optimization_barrier((grad_maps_part, second_part, shrink_back[0]))
    shrink_back[1] = swap(after(shrink_back[1], grad_maps_part))
    groups = [grad_maps_part] + [shift(grad_maps_part, "z", GROUPS, -k) for k in (1, 2, 3)]
    first_part = shift(after(grad_parts[1], *groups), "z", GROUPS, -1)
    third_part = shift(after(grad_parts[3], *groups), "z", GROUPS, -3)
    if bits == 2:
        both = jnp.stack([*groups, *[across(value, 2) for value in groups]])
    else:
        both = jnp.stack(groups)
        for bit in range(bits - 1, 0, -1):
            got = across(both, 1 << bit)
            both = jnp.where(
                (r_at >> bit) & 1 == 0,
                jnp.concatenate([both, got], axis=1),
                jnp.concatenate([got, both], axis=1),
            )
        both = jnp.concatenate(jnp.split(both, 2, axis=1), axis=0)
        x_at = jnp.zeros_like(x_at)
    grad_up = dot32(rows_own, grad_pre, (((0,), (0,)))) + after(widen_back, grad_maps_part).astype(F32)
    grad_down = dot32(hidden_own, grad_made, (((0,), (0,)))) + jnp.concatenate(
        shrink_back, axis=0
    ).astype(F32)
    both, first_part, third_part, grad_up, grad_down = lax.optimization_barrier(
        (both, first_part, third_part, grad_up, grad_down)
    )
    grad_maps, grad_final, grad_router, grad_embed, grad_ln1, grad_ln2 = finish_shared(
        both, across(both, 1), asker_lookup_content_maps, mixer_scaling_factor, jnp.stack([z_at, core, x_at]),
        group_width, route, (embed_share, experts),
    )
    grad_router = grad_router.T

    grad_normed_in = sum(part.astype(F32) for part in (grad_parts[0], first_part, second_part, third_part))
    unit_in, scale_in = norm_parts(after(x_own, kept).astype(F32))
    grad_input = grad_residual + norm_back(unit_in, scale_in, grad_normed_in * gain_in)

    return (
        out[None].astype(BF16),
        grad_input[None],
        grad_ln1,
        grad_maps,
        grad_final,
        grad_ln2,
        grad_router,
        grad_embed,
        grad_up[None],
        grad_down[None],
    )


def solution(mesh):
    ctx_count, fsdp_count = mesh.shape["ctx"], mesh.shape["fsdp"]
    inner = Mesh(mesh.devices.reshape(GROUPS, ctx_count // GROUPS, fsdp_count), ("z", "r", "fsdp"))
    ctx = ("z", "r")
    tokens = P("fsdp", ctx, None)
    expert = P(ctx, "fsdp", None)
    halves, halves2 = P("fsdp"), P("fsdp", None)
    return jax.shard_map(
        functools.partial(body, ctx_count, fsdp_count),
        mesh=inner,
        in_specs=(
            tokens, halves, halves2, halves2, halves, halves2, halves2, expert, expert,
            P("fsdp", ctx), tokens, tokens,
        ),
        out_specs=(
            tokens, tokens, halves, halves2, halves2, halves, halves2, halves2, expert, expert,
        ),
        check_vma=False,
    )
```

```python
import functools
import math

import jax
import jax.numpy as jnp
from jax import lax
from jax.experimental import pallas as pl
from jax.experimental.pallas import tpu as pltpu
from jax.sharding import Mesh, PartitionSpec as P

HD = 64
SMALL = 64
DOCS = 8
AUX = 16
GROUPS = 4
EPSILON = 1e-05
FLOOR = 0.5
ROUTER_HEAT = 0.5
HIGHEST = lax.Precision.HIGHEST
ROOT_HALF = 0.7071067811865476
ROOT_TWO_PI = 2.5066282746310002
NEG_LARGE = -1e30
LOG2E = 1.4426950408889634
VMEM_BYTES = 62 * 1024 * 1024
VMEM_SHARED = 48 * 1024 * 1024
BF16 = jnp.bfloat16
F32 = jnp.float32


def dot32(left, right, dims):
    return lax.dot_general(left, right, (dims, ((), ())), preferred_element_type=F32)


def dot_high(left, right):
    return lax.dot_general(left, right, (((0,), (0,)), ((), ())), precision=HIGHEST)


def early_kernel(group_width, info, maps_ref, extra_ref, own_ref, sent_ref):
    width = GROUPS * group_width
    for group in range(GROUPS):

        @pl.when(info[0] == group)
        def _():
            begins = [part * width + group * group_width for part in range(3)]
            pieces = [maps_ref[:, begin : begin + group_width] for begin in begins]
            own_ref[...] = jnp.concatenate([*pieces, extra_ref[...]], axis=1)

    half = sent_ref.shape[0]
    sent_ref[...] = own_ref[pl.ds(pl.multiple_of(info[1] * half, 16), half)]


def early_rows(info, maps, extra, group_width):
    rows = maps.shape[0]
    columns = 3 * group_width + extra.shape[1]
    shapes = [(rows, columns), (rows // 2, columns)]
    return pl.pallas_call(
        functools.partial(early_kernel, group_width),
        grid_spec=pltpu.PrefetchScalarGridSpec(
            num_scalar_prefetch=1,
            grid=(1,),
            in_specs=[pl.BlockSpec(value.shape, lambda j, info: (0, 0)) for value in (maps, extra)],
            out_specs=[pl.BlockSpec(shape, lambda j, info: (0, 0)) for shape in shapes],
        ),
        out_shape=[jax.ShapeDtypeStruct(shape, BF16) for shape in shapes],
        compiler_params=pltpu.CompilerParams(vmem_limit_bytes=VMEM_BYTES),
    )(info.astype(jnp.int32), maps, extra)


def forward_kernel(scale2, first, last, q_ref, oh_ref, k_ref, v_ref, mk_ref, *rest):
    if not first:
        top_in, acc_in, *rest = rest
    if last:
        out_ref, *low_refs, lse_ref, top_sc, acc_sc = rest
    else:
        top_out, acc_out, top_sc, acc_sc = rest
    step = pl.program_id(1)
    width = k_ref.shape[-1]
    block = min(1024, width)
    pad = jnp.zeros((128 - HD - AUX, q_ref.shape[-1]), BF16)
    query = jnp.concatenate([q_ref[...], oh_ref[...], pad], axis=0)

    @pl.when(step == 0)
    def _():
        if first:
            top_sc[...] = jnp.full_like(top_sc, NEG_LARGE)
            acc_sc[...] = jnp.zeros_like(acc_sc)
        else:
            top_sc[...] = top_in[0]
            acc_sc[...] = acc_in[0]

    top, acc = top_sc[...], acc_sc[...]
    for at in range(0, width, block):
        cut = slice(at, at + block)
        aux = mk_ref[0, :, cut]
        keys = jnp.concatenate([k_ref[0, :, cut], aux, pad[:, :block]], axis=0).T
        scores = jnp.dot(keys, query, preferred_element_type=F32)
        new_top = jnp.maximum(top, jnp.max(scores, axis=0, keepdims=True))
        probs = jnp.exp2((scores - new_top) * scale2).astype(BF16)
        decay = jnp.exp2((top - new_top) * scale2)
        values = jnp.concatenate([v_ref[0, :, cut], aux], axis=0)
        acc = acc * decay + jnp.dot(values, probs, preferred_element_type=F32)
        top = new_top
    top_sc[...], acc_sc[...] = top, acc

    @pl.when(step == pl.num_programs(1) - 1)
    def _():
        if last:
            total = acc[HD + DOCS : HD + DOCS + 1]
            result = acc[:HD] / total
            out_ref[0] = result
            cut = low_refs[0].shape[-1]
            for at, low_ref in enumerate(low_refs):
                low_ref[...] = result[:, at * cut : (at + 1) * cut].astype(BF16)
            lse_ref[0] = top + jnp.log2(total) / scale2
        else:
            top_out[0] = top
            acc_out[0] = acc


def attend(query_t, onehot, pieces, carry, last, scale2, heads):
    count, _, width = pieces.shape
    rows = query_t.shape[1]
    cut = rows // GROUPS
    top_spec = pl.BlockSpec((1, 1, rows), lambda h, j: (h, 0, 0))
    acc_spec = pl.BlockSpec((1, HD + AUX, rows), lambda h, j: (h, 0, 0))
    in_specs = [
        pl.BlockSpec((HD, rows), lambda h, j: (h, 0)),
        pl.BlockSpec((AUX, rows), lambda h, j: (0, 0)),
        pl.BlockSpec((1, HD, width), lambda h, j: (j, h, 0)),
        pl.BlockSpec((1, HD, width), lambda h, j: (j, heads + h, 0)),
        pl.BlockSpec((1, AUX, width), lambda h, j: (j, 2 * heads * HD // AUX, 0)),
    ]
    if carry is not None:
        in_specs += [top_spec, acc_spec]
    top_shape = jax.ShapeDtypeStruct((heads, 1, rows), F32)
    if last:
        out_specs = [
            pl.BlockSpec((1, HD, rows), lambda h, j: (h, 0, 0)),
            *[pl.BlockSpec((HD, cut), lambda h, j: (h, 0))] * GROUPS,
            top_spec,
        ]
        out_shape = [
            jax.ShapeDtypeStruct((heads, HD, rows), F32),
            *[jax.ShapeDtypeStruct((heads * HD, cut), BF16)] * GROUPS,
            top_shape,
        ]
    else:
        out_specs = [top_spec, acc_spec]
        out_shape = [top_shape, jax.ShapeDtypeStruct((heads, HD + AUX, rows), F32)]
    return pl.pallas_call(
        functools.partial(forward_kernel, scale2, carry is None, last),
        grid=(heads, count),
        in_specs=in_specs,
        out_specs=out_specs,
        out_shape=out_shape,
        scratch_shapes=[pltpu.VMEM((1, rows), F32), pltpu.VMEM((HD + AUX, rows), F32)],
        compiler_params=pltpu.CompilerParams(vmem_limit_bytes=VMEM_SHARED),
        cost_estimate=pl.CostEstimate(
            flops=34 * heads * rows * count * width * HD, bytes_accessed=0, transcendentals=0
        ),
    )(query_t, onehot, pieces, pieces, pieces, *(carry or ()))


def split3(value):
    high = value.astype(BF16)
    rest = value - high.astype(F32)
    mid = rest.astype(BF16)
    return high, mid, (rest - mid.astype(F32)).astype(BF16)


def backward_kernel(scale2, first, last, q_ref, oh_ref, g_ref, o_ref, lse_ref, k_ref, v_ref, mk_ref, *rest):
    if not first:
        carry_ref, *rest = rest
    else:
        delta_ref, *rest = rest
    dq_ref, dkv_ref, qa_sc, ga_sc, nat_sc, dq_sc = rest
    step = pl.program_id(1)
    width = k_ref.shape[-1]
    block = width // GROUPS
    rows = q_ref.shape[-1]
    scale = 1.0 / math.sqrt(HD)
    pad = jnp.zeros((128 - HD - AUX, rows), BF16)

    @pl.when(step == 0)
    def _():
        query = q_ref[...]
        grad = jnp.concatenate([g_ref[at] for at in range(g_ref.shape[0])], axis=1)
        if first:
            delta = jnp.sum(grad.astype(F32) * o_ref[0], axis=0, keepdims=True)
            delta_ref[0] = delta
        else:
            delta = o_ref[0]
        place = lax.broadcasted_iota(jnp.int32, (AUX, rows), 0)

        def aux_rows(start, value):
            out = start
            for at, piece in enumerate(split3(-value)):
                out = jnp.where(place == DOCS + at, piece.astype(F32), out)
            return out.astype(BF16)

        qa_sc[...] = jnp.concatenate([query, aux_rows(oh_ref[...].astype(F32), lse_ref[0]), pad], axis=0)
        ga_sc[...] = jnp.concatenate([grad, aux_rows(jnp.zeros((AUX, rows), F32), delta), pad], axis=0)
        nat_sc[...] = jnp.concatenate([grad, query], axis=0).T
        if first:
            dq_sc[...] = jnp.zeros_like(dq_sc)
        else:
            dq_sc[...] = carry_ref[0]

    natural = nat_sc[...]
    for at in range(0, width, block):
        cut = slice(at, at + block)
        aux = mk_ref[0, :, cut]
        keys_t = k_ref[0, :, cut]
        keys = jnp.concatenate([keys_t, aux, pad[:, :block]], axis=0).T
        values = jnp.concatenate([v_ref[0, :, cut], aux, pad[:, :block]], axis=0).T
        probs = jnp.exp2(jnp.dot(keys, qa_sc[...], preferred_element_type=F32) * scale2)
        slopes = jnp.dot(values, ga_sc[...], preferred_element_type=F32)
        grad_scores = (probs * slopes).astype(BF16)
        from_probs = jnp.dot(probs.astype(BF16), natural, preferred_element_type=F32)
        from_scores = jnp.dot(grad_scores, natural, preferred_element_type=F32) * scale
        lane = lax.broadcasted_iota(jnp.int32, from_probs.shape, 1)
        both = jnp.where(lane < HD, from_probs, from_scores).T.astype(BF16)
        dkv_ref[0, at // block, 0] = both[HD:]
        dkv_ref[0, at // block, 1] = both[:HD]
        dq_sc[...] += jnp.dot(keys_t, grad_scores, preferred_element_type=F32)

    @pl.when(step == pl.num_programs(1) - 1)
    def _():
        if last:
            cut = dq_ref.shape[-1]
            for at in range(dq_ref.shape[0]):
                dq_ref[at] = (dq_sc[:, at * cut : (at + 1) * cut] * scale).astype(BF16)
        else:
            dq_ref[0] = dq_sc[...]


def attend_back(query_t, onehot, grad_t, out_heads, lse, pieces, carry, last, scale2, heads):
    count, _, width = pieces.shape
    rows = query_t.shape[1]
    cut = rows // GROUPS
    block = width // GROUPS
    blocks = width // block
    sum_spec = pl.BlockSpec((1, HD, rows), lambda h, j: (h, 0, 0))
    cut_spec = pl.BlockSpec((GROUPS, HD, cut), lambda h, j: (0, h, 0))
    row_spec = pl.BlockSpec((1, 1, rows), lambda h, j: (h, 0, 0))
    in_specs = [
        pl.BlockSpec((HD, rows), lambda h, j: (h, 0)),
        pl.BlockSpec((AUX, rows), lambda h, j: (0, 0)),
        cut_spec,
        sum_spec if carry is None else row_spec,
        row_spec,
        pl.BlockSpec((1, HD, width), lambda h, j: (j, h, 0)),
        pl.BlockSpec((1, HD, width), lambda h, j: (j, heads + h, 0)),
        pl.BlockSpec((1, AUX, width), lambda h, j: (j, 2 * heads * HD // AUX, 0)),
    ]
    if carry is not None:
        in_specs += [sum_spec]
    dq_shape = (GROUPS, heads * HD, cut) if last else (heads, HD, rows)
    return pl.pallas_call(
        functools.partial(backward_kernel, scale2, carry is None, last),
        grid=(heads, count),
        in_specs=in_specs,
        out_specs=([row_spec] if carry is None else [])
        + [
            cut_spec if last else sum_spec,
            pl.BlockSpec((1, blocks, 2, HD, block), lambda h, j: (j, 0, 0, h, 0)),
        ],
        out_shape=([jax.ShapeDtypeStruct((heads, 1, rows), F32)] if carry is None else [])
        + [
            jax.ShapeDtypeStruct(dq_shape, BF16 if last else F32),
            jax.ShapeDtypeStruct((count, blocks, 2, heads * HD, block), BF16),
        ],
        scratch_shapes=[
            pltpu.VMEM((128, rows), BF16),
            pltpu.VMEM((128, rows), BF16),
            pltpu.VMEM((rows, 128), BF16),
            pltpu.VMEM((HD, rows), F32),
        ],
        compiler_params=pltpu.CompilerParams(vmem_limit_bytes=VMEM_SHARED),
        cost_estimate=pl.CostEstimate(
            flops=15 * heads * rows * count * width * HD, bytes_accessed=0, transcendentals=0
        ),
    )(query_t, onehot, grad_t, out_heads, lse, pieces, pieces, pieces, *([] if carry is None else [carry]))


def route_parts(rows, router, columns, expert, expert_count):
    project = jnp.dot(rows, router, preferred_element_type=F32)
    size = jnp.sqrt(jnp.sum(project * project, axis=-1, keepdims=True))
    along = jnp.where(size > FLOOR, 1.0, jnp.where(size == FLOOR, 0.5, 0.0))
    inverse = 1.0 / jnp.maximum(size, FLOOR)
    unit = project * inverse
    logits = jnp.dot(unit, columns, precision=HIGHEST, preferred_element_type=F32) / ROUTER_HEAT
    lane = lax.broadcasted_iota(jnp.int32, logits.shape, 1)
    logits = jnp.where(lane < expert_count, logits, NEG_LARGE)
    raised = jnp.exp(logits - jnp.max(logits, axis=-1, keepdims=True))
    chances = raised / jnp.sum(raised, axis=-1, keepdims=True)
    mine = (lane == expert).astype(F32)
    gate = jnp.sum(chances * mine, axis=-1, keepdims=True)
    return unit, inverse, along, chances, mine, gate


def expert_kernel(first, expert_count, begin, info, x_ref, g_ref, uo_ref, so_ref, router_ref, columns_ref, *rest):
    steps = 3 if first else 1
    if first:
        *ux_refs, sx_ref = rest[: steps + 1]
        rest = rest[steps + 1 :]
    else:
        both_ref, *rest = rest
    if first:
        own_ref, hidden_ref, gp_ref, gw_ref, gm_ref, made_ref, gin_ref, up_sc, down_sc, turned_sc = rest
    else:
        gm_ref, made_in, gin_in, _, _, *rest = rest
        hidden_ref, gp_ref, gw_ref, scaled_ref, back_ref, routed_ref, columns_out, *rest = rest
        up_sc, down_sc, turned_sc, made_ref, gin_ref = rest
    step = pl.program_id(0)
    share, block = uo_ref.shape

    @pl.when(step == 0)
    def _():
        cut = pl.ds(pl.multiple_of((1 - info[0]) * share, 128), share)
        turned_sc[...] = x_ref[:, cut].T
        if first:
            gate = route_parts(x_ref[...], router_ref[...], columns_ref[...], info[1], expert_count)[-1]
            gm_ref[...] = (gate * g_ref[...].astype(F32)).astype(BF16)
            made_ref[...] = jnp.zeros_like(made_ref)
            gin_ref[...] = jnp.zeros_like(gin_ref)
        else:
            made_ref[...] = made_in[...]
            gin_ref[...] = gin_in[...]

    up_sc[pl.ds(pl.multiple_of(info[0] * share, 128), share)] = uo_ref[...]
    other = pl.ds(pl.multiple_of((1 - info[0]) * share, 128), share)
    for now in range(steps):

        @pl.when(step == now)
        def _():
            up_sc[other] = ux_refs[now][...] if first else both_ref[:share]
            if begin + now < 2:
                down_sc[...] = so_ref[...]
            else:
                down_sc[...] = sx_ref[...] if first else both_ref[share:]

    up, down = up_sc[...], down_sc[...]
    piece = x_ref.shape[0] // 2
    for begin_row in (0, piece):
        rows = slice(begin_row, begin_row + piece)
        pre_act = jnp.dot(x_ref[rows], up, preferred_element_type=F32)
        grad_hidden = dot32(gm_ref[rows], down, (((1,), (1,))))
        bell = 0.5 * (1.0 + lax.erf(pre_act * ROOT_HALF))
        hidden = (pre_act * bell).astype(BF16)
        hidden_ref[rows] = hidden
        made_ref[rows] += jnp.dot(hidden, down, preferred_element_type=F32)
        slope = bell + pre_act * (jnp.exp(-0.5 * pre_act * pre_act) * (1.0 / ROOT_TWO_PI))
        grad_pre = (grad_hidden * slope).astype(BF16)
        gp_ref[rows] = grad_pre
        gin_ref[rows] += dot32(grad_pre, up, (((1,), (1,))))
    if first:

        @pl.when(step < 2)
        def _():
            own_ref[...] = hidden_ref[...]

    gw_ref[...] = jnp.dot(turned_sc[...], gp_ref[...], preferred_element_type=F32).astype(BF16)

    if not first:
        router, columns = router_ref[...], columns_ref[...]
        unit, inverse, along, chances, mine, gate = route_parts(x_ref[...], router, columns, info[1], expert_count)
        made = made_ref[...].astype(BF16).astype(F32)
        scaled_ref[...] = (gate * made).astype(BF16)
        grad_gate = jnp.sum(g_ref[...].astype(F32) * made, axis=-1, keepdims=True)
        dlogit = grad_gate * gate * (mine - chances) / ROUTER_HEAT
        dunit = lax.dot_general(
            dlogit, columns, (((1,), (1,)), ((), ())), precision=HIGHEST, preferred_element_type=F32
        )
        dproj = inverse * (dunit - along * unit * jnp.sum(unit * dunit, axis=-1, keepdims=True))
        high = dproj.astype(BF16)
        low = (dproj - high.astype(F32)).astype(BF16)
        back = dot32(high, router, (((1,), (1,)))) + dot32(low, router, (((1,), (1,))))
        back_ref[...] = (gin_ref[...].astype(BF16).astype(F32) + back).astype(BF16)
        rows = x_ref[...]
        routed_ref[...] = jnp.dot(high.astype(F32).T.astype(BF16), rows, preferred_element_type=F32) + jnp.dot(
            low.astype(F32).T.astype(BF16), rows, preferred_element_type=F32
        )
        columns_out[...] = jnp.dot(unit.T, dlogit, precision=HIGHEST, preferred_element_type=F32)


def run_expert(info, rows, grads, widen, shrink, others, routing, carry, expert_count):
    slots, width = rows.shape
    share, units = widen.shape
    block = units // 4
    first = carry is None
    begin = 0 if first else 3

    def at(j, info):
        return lax.rem(2 * info[0] + begin + j, 4)

    whole = pl.BlockSpec((slots, width), lambda j, info: (0, 0))
    quarter = pl.BlockSpec((slots, block), lambda j, info: (0, 0))
    part = jax.ShapeDtypeStruct((slots, units), BF16)
    part_spec = pl.BlockSpec((slots, block), lambda j, info: (0, at(j, info)))
    low = jax.ShapeDtypeStruct((slots, width), BF16)
    full = jax.ShapeDtypeStruct((slots, width), F32)
    fixed = [*routing, *others]
    in_specs = [
        whole,
        whole,
        pl.BlockSpec((share, block), lambda j, info: (0, at(j, info))),
        pl.BlockSpec((block, width), lambda j, info: (jnp.minimum(j, 1), 0)),
        *[pl.BlockSpec(value.shape, lambda j, info: (0, 0)) for value in fixed],
    ]
    operands = [rows, grads, widen, shrink, *fixed]
    scratch = [pltpu.VMEM((width, block), BF16), pltpu.VMEM((block, width), BF16), pltpu.VMEM((share, slots), BF16)]
    sent = jax.ShapeDtypeStruct((share, units), BF16)
    sent_spec = pl.BlockSpec((share, block), lambda j, info: (0, at(j, info)))
    aliases = {}
    if first:
        own = jax.ShapeDtypeStruct((slots, 2 * block), BF16)
        out_specs = [
            pl.BlockSpec((slots, block), lambda j, info: (0, jnp.minimum(j, 1))), quarter, part_spec, sent_spec,
            whole, whole, whole,
        ]
        out_shape = [own, jax.ShapeDtypeStruct((slots, block), BF16), part, sent, low, full, full]
    else:
        grad_pre, widen_sent, grad_made, made, grad_inputs = carry
        in_specs += [whole, whole, whole] + [pl.BlockSpec(memory_space=pl.ANY)] * 2
        operands += [grad_made, made, grad_inputs, grad_pre, widen_sent]
        aliases = {len(operands) - 1: 1, len(operands): 2}
        tops = [jax.ShapeDtypeStruct((128, width), F32), jax.ShapeDtypeStruct((128, 128), F32)]
        out_specs = [quarter, part_spec, sent_spec, whole, whole]
        out_specs += [pl.BlockSpec(v.shape, lambda j, info: (0, 0)) for v in tops]
        out_shape = [jax.ShapeDtypeStruct((slots, block), BF16), part, sent, low, low, *tops]
        scratch += [pltpu.VMEM((slots, width), F32), pltpu.VMEM((slots, width), F32)]
    return pl.pallas_call(
        functools.partial(expert_kernel, first, expert_count, begin),
        grid_spec=pltpu.PrefetchScalarGridSpec(
            num_scalar_prefetch=1,
            grid=(3 if first else 1,),
            in_specs=in_specs,
            out_specs=out_specs,
            scratch_shapes=scratch,
        ),
        out_shape=out_shape,
        input_output_aliases=aliases,
        compiler_params=pltpu.CompilerParams(vmem_limit_bytes=VMEM_BYTES),
        cost_estimate=pl.CostEstimate(
            flops=(2 if first else 1) * slots * width * units, bytes_accessed=0, transcendentals=0
        ),
    )(info.astype(jnp.int32), *operands)


def final_kernel(info, g_ref, c_ref, kept_ref, sent_ref, all_sc):
    all_sc[...] = dot32(g_ref[...].T, c_ref[...], (((1,), (1,)))).astype(BF16)
    count, half = kept_ref.shape[:2]
    for at in range(count):
        for ref, core in ((kept_ref, info[0]), (sent_ref, 1 - info[0])):
            ref[at] = all_sc[pl.ds(pl.multiple_of((2 * at + core) * half, 16), half)]


def final_grads(core, grads, context):
    width = grads.shape[1]
    shape = (GROUPS, width // GROUPS // 2, context.shape[0])
    return pl.pallas_call(
        final_kernel,
        grid_spec=pltpu.PrefetchScalarGridSpec(
            num_scalar_prefetch=1,
            grid=(1,),
            in_specs=[pl.BlockSpec(value.shape, lambda j, info: (0, 0)) for value in (grads, context)],
            out_specs=[pl.BlockSpec(shape, lambda j, info: (0, 0, 0))] * 2,
            scratch_shapes=[pltpu.VMEM((width, context.shape[0]), BF16)],
        ),
        out_shape=[jax.ShapeDtypeStruct(shape, BF16)] * 2,
        compiler_params=pltpu.CompilerParams(vmem_limit_bytes=VMEM_BYTES),
    )(core[None].astype(jnp.int32), grads, context)


def gather_kernel(row, info, dq_ref, own_ref, got_ref, far0_ref, far1_ref, x_ref, w_ref, small_ref, gain_ref, *rest):
    *part_refs, kept_ref, sent_ref, acc_sc, all_sc = rest
    step = pl.program_id(0)
    far = jnp.where(step < GROUPS // 2, far0_ref[0, 0].astype(F32), far1_ref[0, 0].astype(F32))
    grad_kv = (own_ref[0, 0].astype(F32) + got_ref[0, 0].astype(F32) + far).astype(BF16)
    joined = jnp.concatenate([dq_ref[0], grad_kv[0], grad_kv[1]], axis=0)
    product = jnp.dot(joined, x_ref[...], preferred_element_type=F32)
    through = dot32(joined.T, w_ref[...], (((1,), (1,)))).astype(BF16)
    for at in range(GROUPS):

        @pl.when(step == at)
        def _():
            part_refs[at][...] = through
            if at == 0:
                acc_sc[...] = product
            else:
                acc_sc[...] += product

    @pl.when(step == pl.num_programs(0) - 1)
    def _():
        rows = acc_sc.shape[0]
        all_sc[:rows] = acc_sc[...].astype(BF16)
        place = lax.broadcasted_iota(jnp.int32, small_ref.shape, 0)
        all_sc[rows:] = jnp.where(place == row, gain_ref[...], small_ref[...].astype(F32)).astype(BF16)
        half = kept_ref.shape[0]
        kept_ref[...] = all_sc[pl.ds(pl.multiple_of(info[0] * half, 16), half)]
        sent_ref[...] = all_sc[pl.ds(pl.multiple_of((1 - info[0]) * half, 16), half)]


def gather_grads(core, grad_query, near_own, near_got, far, far_last, normed, maps, small, gain_grad, row):
    group_width, cut = grad_query.shape[1:]
    width = maps.shape[0]
    half = GROUPS // 2
    rows = 3 * group_width
    total = rows + small.shape[0]
    piece = (1, 1, 2, group_width, cut)

    def fixed(shape):
        return pl.BlockSpec(shape, lambda j, info: (0, 0))

    return pl.pallas_call(
        functools.partial(gather_kernel, row),
        grid_spec=pltpu.PrefetchScalarGridSpec(
            num_scalar_prefetch=1,
            grid=(GROUPS,),
            in_specs=[
                pl.BlockSpec((1, group_width, cut), lambda j, info: (j, 0, 0)),
                pl.BlockSpec(piece, lambda j, info: (0, j, 0, 0, 0)),
                pl.BlockSpec(piece, lambda j, info: (0, j, 0, 0, 0)),
                pl.BlockSpec(piece, lambda j, info: (0, jnp.minimum(j, half - 1), 0, 0, 0)),
                pl.BlockSpec(piece, lambda j, info: (0, jnp.maximum(j - half, 0), 0, 0, 0)),
                pl.BlockSpec((cut, width), lambda j, info: (j, 0)),
                fixed(maps.shape),
                fixed(small.shape),
                fixed((1, width)),
            ],
            out_specs=[fixed((cut, width))] * GROUPS + [fixed((total // 2, width))] * 2,
            scratch_shapes=[pltpu.VMEM((rows, width), F32), pltpu.VMEM((total, width), BF16)],
        ),
        out_shape=[jax.ShapeDtypeStruct((cut, width), BF16)] * GROUPS
        + [jax.ShapeDtypeStruct((total // 2, width), BF16)] * 2,
        compiler_params=pltpu.CompilerParams(vmem_limit_bytes=VMEM_SHARED),
        cost_estimate=pl.CostEstimate(flops=16 * group_width * GROUPS * cut * width, bytes_accessed=0, transcendentals=0),
    )(
        core[None].astype(jnp.int32), grad_query, near_own, near_got, far, far_last, normed, maps, small, gain_grad[None]
    )


def finish_kernel(
    group_width, info, own_ref, got_ref, w_ref, gain_ref, maps_ref, final_ref, router_ref, embed_ref, ln1_ref, ln2_ref,
    v_ref,
):
    final_half = group_width // 2
    part = own_ref.shape[1]
    half = 2 * part - final_half
    for ref, core in ((own_ref, info[1]), (got_ref, 1 - info[1])):
        low_rows = pl.ds(pl.multiple_of(core * half, 16), part)
        high_rows = pl.ds(pl.multiple_of(core * half + part, 16), half - part)
        final_rows = pl.ds(pl.multiple_of(2 * half + core * final_half, 16), final_half)
        for k in range(GROUPS):
            v_ref[k, low_rows] = ref[k + GROUPS * info[2]]
            high = ref[k + GROUPS * (1 - info[2])]
            v_ref[k, high_rows] = high[: half - part]
            v_ref[k, final_rows] = high[half - part :]

    def columns(pair, begin):
        rows = pl.ds(begin, group_width)
        halves = [v_ref[lax.rem(2 * pair + k + GROUPS - info[0], GROUPS), rows] for k in range(2)]
        return jnp.concatenate(halves, axis=0).astype(F32).T

    total = 0.0
    for part in range(3):
        for pair in range(GROUPS // 2):
            value = columns(pair, part * group_width)
            at = (part * GROUPS + 2 * pair) * group_width
            cut = slice(at, at + 2 * group_width)
            maps_ref[:, cut] = value
            total = total + jnp.sum(value * w_ref[:, cut].astype(F32), axis=1, keepdims=True)
    for pair in range(GROUPS // 2):
        at = 2 * pair * group_width
        final_ref[:, at : at + 2 * group_width] = columns(pair, 2 * half)
    small = sum(v_ref[k, 3 * group_width : 2 * half].astype(F32) for k in range(GROUPS))
    route, embed = router_ref.shape[0], embed_ref.shape[0]
    rows = small.shape[1]
    router_ref[...] = small[:route]
    embed_ref[...] = small[route : route + embed, : embed_ref.shape[1]]
    ln2_ref[...] = small[route + embed]
    ln1_ref[...] = (jnp.broadcast_to(total, (rows, 128)).T[:1] / gain_ref[...].astype(F32))[0]


def finish_shared(own, got, weights, gain, info, group_width, route, embed_shape):
    rows, columns = weights.shape
    shapes = [(rows, columns), (rows, GROUPS * group_width), (route, rows), embed_shape, (rows,), (rows,)]
    return pl.pallas_call(
        functools.partial(finish_kernel, group_width),
        grid_spec=pltpu.PrefetchScalarGridSpec(
            num_scalar_prefetch=1,
            grid=(1,),
            in_specs=[
                pl.BlockSpec(own.shape, lambda j, info: (0, 0, 0)),
                pl.BlockSpec(got.shape, lambda j, info: (0, 0, 0)),
                pl.BlockSpec(weights.shape, lambda j, info: (0, 0)),
                pl.BlockSpec((1, rows), lambda j, info: (0, 0)),
            ],
            out_specs=[pl.BlockSpec(shape, lambda j, info, rank=len(shape): (0,) * rank) for shape in shapes],
            scratch_shapes=[pltpu.VMEM((GROUPS, 4 * own.shape[1], rows), BF16)],
        ),
        out_shape=[jax.ShapeDtypeStruct(shape, F32) for shape in shapes],
        compiler_params=pltpu.CompilerParams(vmem_limit_bytes=VMEM_SHARED),
    )(info.astype(jnp.int32), own, got, weights, gain[None])


def norm_parts(values):
    center = values - jnp.mean(values, axis=-1, keepdims=True)
    scale = lax.rsqrt(jnp.mean(center * center, axis=-1, keepdims=True) + EPSILON)
    return center * scale, scale


def norm_back(unit, scale, scaled_grad):
    along = jnp.mean(scaled_grad * unit, axis=-1, keepdims=True)
    return scale * (scaled_grad - jnp.mean(scaled_grad, axis=-1, keepdims=True) - unit * along)


def unit_of(vectors, axis):
    size = jnp.sqrt(jnp.sum(vectors * vectors, axis=axis, keepdims=True))
    share = jnp.where(size > FLOOR, 1.0, jnp.where(size == FLOOR, 0.5, 0.0))
    inverse = 1.0 / jnp.maximum(size, FLOOR)
    return vectors * inverse, inverse, share


def unit_back(unit, inverse, share, grad, axis):
    return inverse * (grad - share * unit * jnp.sum(unit * grad, axis=axis, keepdims=True))


def shift(value, axis, size, by):
    return lax.ppermute(value, axis, [(at, (at + by) % size) for at in range(size)])


def flip(value, axis, size, bit):
    return lax.ppermute(value, axis, [(at, at ^ bit) for at in range(size)])


def after(value, *others):
    return lax.optimization_barrier((value, *others))[0]


def line_gather(value, axis, size, tied):
    upward, downward, from_low, from_high = value, value, [], []
    for hop in range(size - 1):
        upward = tied(hop, upward)
        upward = lax.ppermute(upward, axis, [(at, at + 1) for at in range(hop, size - 1)])
        downward = lax.ppermute(downward, axis, [(at, at - 1) for at in range(size - 1 - hop, 0, -1)])
        from_low.append(upward)
        from_high.append(downward)
    return [value] + [from_low[k] + from_high[size - 2 - k] for k in range(size - 1)]


def roll_blocks(blocks, start):
    return lax.dynamic_slice_in_dim(jnp.concatenate([blocks, blocks], axis=0), start, blocks.shape[0], 0)


def pair_order(own, other, at):
    return jnp.where(at == 0, jnp.concatenate([own, other], 0), jnp.concatenate([other, own], 0))


def body(
    ctx_count,
    fsdp_count,
    incoming_sequence,
    mixer_scaling_factor,
    asker_lookup_content_maps,
    mixer_final_map,
    specialist_scaling_factor,
    dispatch_space_map,
    specialist_dispatch_vectors,
    specialist_widen_weights_pair,
    specialist_shrink_weights_pair,
    document_labels,
    piece_specialist_choice,
    result_cotangent_array,
):
    row_count = incoming_sequence.shape[1]
    width = incoming_sequence.shape[2]
    head_count = width // HD
    heads = head_count // GROUPS
    group_width = heads * HD
    ring = ctx_count // GROUPS
    bits = ring.bit_length() - 1
    scale2 = LOG2E / math.sqrt(HD)
    z_at = lax.axis_index("z")
    r_at = lax.axis_index("r")
    f_at = lax.axis_index("fsdp")
    core = r_at & 1
    expert_at = z_at * ring + r_at
    share = width // fsdp_count
    capacity = max(2, 2 * row_count // ctx_count)
    slots = ctx_count * capacity

    def swap(value):
        return flip(value, "fsdp", fsdp_count, 1)

    def across(value, bit):
        return flip(value, "r", ring, bit)

    def exchange_slots(rows):
        return lax.all_to_all(
            rows.reshape(ctx_count, capacity, -1), ("z", "r"), split_axis=0, concat_axis=0, tiled=True
        ).reshape(slots, -1)

    def both_cores(got):
        return pair_order(got, across(got, 1), core)

    def halve(value, axis, flag, send):
        half = value.shape[axis] // 2
        kept = lax.dynamic_slice_in_dim(value, flag * half, half, axis)
        sent = lax.dynamic_slice_in_dim(value, (1 - flag) * half, half, axis)
        return (kept.astype(F32) + send(sent).astype(F32)).astype(BF16)

    def by_fsdp(own, other, axis):
        return jnp.where(
            f_at == 0,
            jnp.concatenate([own, other], axis=axis),
            jnp.concatenate([other, own], axis=axis),
        )

    route, experts = specialist_dispatch_vectors.shape[0] * fsdp_count, specialist_dispatch_vectors.shape[1]
    embed_share = route // fsdp_count
    extras = [
        mixer_scaling_factor[:, None],
        specialist_scaling_factor[:, None],
        dispatch_space_map,
        jnp.pad(specialist_dispatch_vectors, ((0, share - embed_share), (0, 0))),
    ]
    edges = [0, 3 * group_width]
    for value in extras:
        edges.append(edges[-1] + value.shape[1])
    extras.append(jnp.zeros((share, -edges[-1] % 128), BF16))
    early_own, early_sent = early_rows(
        jnp.stack([z_at, core]), asker_lookup_content_maps, jnp.concatenate(extras, axis=1), group_width
    )
    half = share // 2
    final_sent = lax.dynamic_slice_in_dim(mixer_final_map, core * half, half, 0)

    widen = specialist_widen_weights_pair[0]
    shrink_own = specialist_shrink_weights_pair[0]
    half_ff = shrink_own.shape[0]
    part_ff = half_ff // 2
    eighth = half_ff // 4
    early_pieces = []

    def widen_piece(which, at, *others):
        return lax.dynamic_slice_in_dim(after(widen, *others), (which * 2 + at) * part_ff, part_ff, 1)

    def tie(value, pieces, at):
        value, pieces[at] = lax.optimization_barrier((value, pieces[at]))
        return value

    def hop_tie(hop, value):
        if hop == 1:
            value, *sent = lax.optimization_barrier((value, early_sent, final_sent))
            early_pieces.extend([swap(piece) for piece in sent])
        return value

    x_own = incoming_sequence[0]
    label_rows = jnp.zeros((16, width), BF16).at[0, :row_count].set(document_labels[0].astype(BF16))
    blocks = line_gather(jnp.concatenate([x_own, label_rows], axis=0), "z", GROUPS, hop_tie)
    x_all = jnp.concatenate([piece[:row_count] for piece in blocks], axis=0)
    labels = jnp.concatenate([piece[row_count, :row_count] for piece in blocks], axis=0)

    widen_near = [swap(widen_piece(1 - f_at, at, *early_pieces)) for at in range(2)]
    widen_far = [swap(widen_piece(f_at, 0, *early_pieces))]
    widen_last = widen_piece(f_at, 1, *early_pieces)
    early_full = pair_order(early_own, both_cores(early_pieces[0]), f_at)
    maps_group, gain_in, gain_mid, router, embed = (
        early_full[:, begin:end] for begin, end in zip(edges[:-1], edges[1:])
    )
    gain_in, gain_mid = gain_in[:, 0].astype(F32), gain_mid[:, 0].astype(F32)
    embed = embed.reshape(fsdp_count, share, experts)[:, :embed_share].reshape(route, experts).astype(F32)
    final_map = roll_blocks(
        pair_order(mixer_final_map, both_cores(early_pieces[1]), f_at).reshape(GROUPS, group_width, width), z_at
    ).reshape(width, width)

    picked = piece_specialist_choice[0, :, 0]
    hits = (picked[:, None] == jnp.arange(ctx_count, dtype=jnp.int32)[None, :]).astype(jnp.int32)
    slot_rank = jnp.sum(jnp.cumsum(hits, axis=0) * hits, axis=1) - 1
    slot_index = picked * capacity + slot_rank
    place = (jnp.arange(slots, dtype=jnp.int32)[:, None] == slot_index[None, :]).astype(BF16)
    cotangent = result_cotangent_array[0]

    def to_slots(values):
        return jnp.dot(place, values, preferred_element_type=F32).astype(BF16)

    x_all = tie(x_all, widen_near, 0)
    x_all, final_map, grad_rows = lax.optimization_barrier((x_all, final_map, to_slots(cotangent)))
    unit_all, _ = norm_parts(x_all.astype(F32))
    normed_low = (unit_all * gain_in).astype(BF16)
    joined_t = dot32(maps_group, normed_low, (((0,), (1,)))).astype(BF16)
    aux_at = jnp.arange(AUX, dtype=jnp.int32)[:, None]
    same = labels.astype(jnp.int32)[None, :] == aux_at
    onehot = same.astype(BF16)
    key_aux = jnp.where(
        aux_at < DOCS, jnp.where(same, 0.0, NEG_LARGE), jnp.where(aux_at < DOCS + 3, 1.0, 0.0)
    ).astype(BF16)
    own_piece = jnp.concatenate([joined_t[group_width:], key_aux], axis=0)[None]
    even = own_piece
    for bit in range(bits - 1, 0, -1):
        even = jnp.stack([even, across(even, 1 << bit)], axis=1).reshape(-1, *own_piece.shape[1:])
    even = even[1:]
    last_sent = jnp.concatenate([widen_last, after(shrink_own, own_piece)[part_ff:]], axis=0)
    peer_piece, *shrink_sent = lax.optimization_barrier(
        (across(own_piece, 1), after(shrink_own, own_piece)[:part_ff], last_sent)
    )
    shrink_other = [swap(shrink_sent[0])]
    last_other = swap(shrink_sent[1])
    carry = attend(joined_t, onehot, own_piece, None, False, scale2, heads)
    carry = attend(joined_t, onehot, peer_piece, carry, False, scale2, heads)
    even = tie(tie(after(even, carry[0]), widen_near, 1), widen_far, 0)
    odd = across(even, 1)
    carry = attend(joined_t, onehot, even, carry, False, scale2, heads)
    grad_slots = exchange_slots(after(grad_rows, peer_piece))
    odd, grad_slots = lax.optimization_barrier((odd, grad_slots))
    out_heads, *out_low, lse = attend(joined_t, onehot, odd, carry, True, scale2, heads)
    context_t = jnp.concatenate(
        [out_low[0]] + [shift(out_low[k], "z", GROUPS, -k) for k in range(1, GROUPS)], axis=0
    )

    context_t = tie(context_t, shrink_other, 0)
    x32 = x_own.astype(F32)
    residual = x32 + dot32(context_t, final_map, (((0,), (0,))))
    unit_mid, scale_mid = norm_parts(residual)
    mid_low = (unit_mid * gain_mid).astype(BF16)
    def from_slots(values):
        return dot32(place, values, (((0,), (0,))))

    sent_rows = to_slots(mid_low)
    arrived = exchange_slots(sent_rows)
    context_rows = roll_blocks(
        context_t.reshape(GROUPS, group_width, row_count), (GROUPS - z_at) % GROUPS
    ).reshape(width, row_count)
    arrived, far_pieces, context_rows = lax.optimization_barrier(
        (arrived, jnp.concatenate([odd, even], axis=0), context_rows)
    )

    unit_columns, inverse_columns, share_columns = unit_of(embed, 0)
    routing = (
        jnp.pad(router, ((0, 0), (0, 128 - route))),
        jnp.pad(unit_columns, ((0, 128 - route), (0, 128 - experts))),
    )

    expert_info = jnp.stack([f_at, expert_at])
    hidden_own, hidden_third, *carry = run_expert(
        expert_info, arrived, grad_slots, widen, shrink_own, [*widen_near, *widen_far, *shrink_other], routing, None, experts
    )
    grad_made = carry[2]
    hidden_last, grad_pre, widen_sent, scaled, sent_back, routed_grad, columns_grad = run_expert(
        expert_info, arrived, grad_slots, widen, shrink_own, [last_other], routing, carry, experts
    )
    grad_back = exchange_slots(sent_back)

    arrived, hidden_own, hidden_third, hidden_last, grad_made, _ = lax.optimization_barrier(
        (arrived, hidden_own, hidden_third, hidden_last, grad_made, sent_back)
    )
    first, second = arrived[:, :share], arrived[:, share:]
    rows_own = jnp.where(f_at == 0, first, second)
    widen_back = swap(widen_sent)
    shrink_back = [
        dot32(value, grad_made, (((0,), (0,)))).astype(BF16)
        for value in (hidden_third, hidden_last)
    ]
    grad_router_own, grad_columns = routed_grad[:route], columns_grad[:route, :experts]
    grad_embed_own = unit_back(unit_columns, inverse_columns, share_columns, grad_columns, 0)
    embed_rows = jnp.pad(
        grad_embed_own.reshape(fsdp_count, embed_share, experts), ((0, 0), (0, 0), (0, share - experts))
    )
    small = jnp.concatenate(
        [
            grad_router_own,
            jnp.concatenate([embed_rows[at] for at in range(fsdp_count)], axis=1),
            jnp.zeros((SMALL - route - embed_share, width), F32),
        ],
        axis=0,
    ).astype(BF16)
    grad_back, small, *shrink_back = lax.optimization_barrier((grad_back, small, *shrink_back))
    shrink_back[0] = swap(shrink_back[0])

    grad_mid = from_slots(grad_back)
    grad_residual = cotangent.astype(F32) + norm_back(unit_mid, scale_mid, grad_mid * gain_mid)
    grad_gain_mid = jnp.sum(grad_mid * unit_mid, axis=0)
    grad_res_low = grad_residual.astype(BF16)
    grad_context = dot32(final_map, grad_res_low, (((1,), (1,)))).astype(BF16).reshape(
        GROUPS, group_width, row_count
    )
    grad_parts = [grad_context[0]] + [shift(grad_context[k], "z", GROUPS, k) for k in range(1, GROUPS)]
    grad_t = jnp.stack(grad_parts)

    def back(piece, running, last=False, ties=()):
        tied = lax.optimization_barrier((grad_t, *ties))
        rows = out_heads if running is None else delta
        result = attend_back(joined_t, onehot, tied[0], rows, lse, piece, running, last, scale2, heads)
        return (*result, *tied[1:])

    scaled_back = exchange_slots(after(scaled, grad_parts[1], grad_parts[3]))
    delta, running, far_both = back(far_pieces, None)
    far_odd, far_even = far_both[: odd.shape[0]], far_both[odd.shape[0] :]
    final_kept, final_sent = final_grads(core, after(grad_res_low, running), context_rows)
    final_got = across(final_sent, 1)
    finals = (final_kept.astype(F32) + final_got.astype(F32)).astype(BF16)
    finals = lax.all_to_all(finals, "z", split_axis=0, concat_axis=0, tiled=True)
    far_got = across(far_odd, 1)
    cut = far_even.shape[1] // 2

    def far_sum(part):
        return (far_even[:, part].astype(F32) + far_got[:, part].astype(F32)).astype(BF16)

    def add_far(value):
        if bits == 2:
            return across(value, 2)
        value = jnp.concatenate([jnp.zeros_like(value[:1]), value], axis=0)
        for bit in range(1, bits):
            halves = value.reshape(-1, 2, *value.shape[1:])
            value = (halves[:, 0].astype(F32) + across(halves[:, 1], 1 << bit).astype(F32)).astype(BF16)
        return value

    far, far_last = far_sum(slice(0, cut)), far_sum(slice(cut, None))
    running, near_peer, far, far_last = back(peer_piece, running, ties=(far, far_last))
    far = add_far(far)
    far_last = add_far(after(far_last, running))
    grad_query, near_own, far, scaled_back, widen_back = back(
        own_piece, running, True, ties=(far, scaled_back, widen_back)
    )

    *grad_parts, kept, sent = gather_grads(
        core, grad_query, near_own, across(near_peer, 1), far, far_last, normed_low, maps_group, small, grad_gain_mid,
        route + embed_share,
    )
    second_part = shift(grad_parts[2], "z", GROUPS, -2)
    grad_maps_part = (kept.astype(F32) + across(sent, 1).astype(F32)).astype(BF16)
    finals = after(finals, kept)
    final_rows = sum(finals[at].astype(F32) for at in range(GROUPS)).astype(BF16)
    grad_maps_part = jnp.concatenate([grad_maps_part, final_rows], axis=0)
    out = residual + from_slots(after(scaled_back, kept))
    x_at = (r_at >> 1) & 1
    if bits == 2:
        half_rows = grad_maps_part.shape[0] // 2

        def piece(x_bit, f_bit):
            return lax.dynamic_slice(grad_maps_part, (x_bit * half_rows, f_bit * share), (half_rows, share))

        corner = [
            (r * fsdp_count + f, (r ^ 2) * fsdp_count + (1 - f)) for r in range(ring) for f in range(fsdp_count)
        ]
        pieces = [
            piece(x_at, f_at),
            across(piece(1 - x_at, f_at), 2),
            swap(piece(x_at, 1 - f_at)),
            lax.ppermute(piece(1 - x_at, 1 - f_at), ("r", "fsdp"), corner),
        ]
        grad_maps_part = sum(value.astype(F32) for value in pieces).astype(BF16)
    else:
        for bit in range(1, bits):
            grad_maps_part = halve(grad_maps_part, 0, (r_at >> bit) & 1, lambda v: across(v, 1 << bit))
        grad_maps_part = halve(grad_maps_part, 1, f_at, swap)
    grad_maps_part, second_part, shrink_back[0] = lax.optimization_barrier((grad_maps_part, second_part, shrink_back[0]))
    shrink_back[1] = swap(after(shrink_back[1], grad_maps_part))
    groups = [grad_maps_part] + [shift(grad_maps_part, "z", GROUPS, -k) for k in (1, 2, 3)]
    first_part = shift(after(grad_parts[1], *groups), "z", GROUPS, -1)
    third_part = shift(after(grad_parts[3], *groups), "z", GROUPS, -3)
    if bits == 2:
        both = jnp.stack([*groups, *[across(value, 2) for value in groups]])
    else:
        both = jnp.stack(groups)
        for bit in range(bits - 1, 0, -1):
            got = across(both, 1 << bit)
            both = jnp.where(
                (r_at >> bit) & 1 == 0,
                jnp.concatenate([both, got], axis=1),
                jnp.concatenate([got, both], axis=1),
            )
        both = jnp.concatenate(jnp.split(both, 2, axis=1), axis=0)
        x_at = jnp.zeros_like(x_at)
    grad_up = dot32(rows_own, grad_pre, (((0,), (0,)))) + after(widen_back, grad_maps_part).astype(F32)
    grad_down = dot32(hidden_own, grad_made, (((0,), (0,)))) + jnp.concatenate(
        shrink_back, axis=0
    ).astype(F32)
    both, first_part, third_part, grad_up, grad_down = lax.optimization_barrier(
        (both, first_part, third_part, grad_up, grad_down)
    )
    grad_maps, grad_final, grad_router, grad_embed, grad_ln1, grad_ln2 = finish_shared(
        both, across(both, 1), asker_lookup_content_maps, mixer_scaling_factor, jnp.stack([z_at, core, x_at]),
        group_width, route, (embed_share, experts),
    )
    grad_router = grad_router.T

    grad_normed_in = sum(part.astype(F32) for part in (grad_parts[0], first_part, second_part, third_part))
    unit_in, scale_in = norm_parts(after(x_own, kept).astype(F32))
    grad_input = grad_residual + norm_back(unit_in, scale_in, grad_normed_in * gain_in)

    return (
        out[None].astype(BF16),
        grad_input[None],
        grad_ln1,
        grad_maps,
        grad_final,
        grad_ln2,
        grad_router,
        grad_embed,
        grad_up[None],
        grad_down[None],
    )


def solution(mesh):
    ctx_count, fsdp_count = mesh.shape["ctx"], mesh.shape["fsdp"]
    inner = Mesh(mesh.devices.reshape(GROUPS, ctx_count // GROUPS, fsdp_count), ("z", "r", "fsdp"))
    ctx = ("z", "r")
    tokens = P("fsdp", ctx, None)
    expert = P(ctx, "fsdp", None)
    halves, halves2 = P("fsdp"), P("fsdp", None)
    return jax.shard_map(
        functools.partial(body, ctx_count, fsdp_count),
        mesh=inner,
        in_specs=(
            tokens, halves, halves2, halves2, halves, halves2, halves2, expert, expert,
            P("fsdp", ctx), tokens, tokens,
        ),
        out_specs=(
            tokens, tokens, halves, halves2, halves2, halves, halves2, halves2, expert, expert,
        ),
        check_vma=False,
    )
```

```python
import functools
import math

import jax
import jax.numpy as jnp
from jax import lax
from jax.experimental import pallas as pl
from jax.experimental.pallas import tpu as pltpu
from jax.sharding import Mesh, PartitionSpec as P

HD = 64
SMALL = 64
DOCS = 8
AUX = 16
GROUPS = 4
EPSILON = 1e-05
FLOOR = 0.5
ROUTER_HEAT = 0.5
HIGHEST = lax.Precision.HIGHEST
ROOT_HALF = 0.7071067811865476
ROOT_TWO_PI = 2.5066282746310002
NEG_LARGE = -1e30
LOG2E = 1.4426950408889634
VMEM_BYTES = 62 * 1024 * 1024
VMEM_SHARED = 48 * 1024 * 1024
BF16 = jnp.bfloat16
F32 = jnp.float32


def dot32(left, right, dims):
    return lax.dot_general(left, right, (dims, ((), ())), preferred_element_type=F32)


def dot_high(left, right):
    return lax.dot_general(left, right, (((0,), (0,)), ((), ())), precision=HIGHEST)


def early_kernel(group_width, info, maps_ref, extra_ref, own_ref, sent_ref):
    width = GROUPS * group_width
    for group in range(GROUPS):

        @pl.when(info[0] == group)
        def _():
            begins = [part * width + group * group_width for part in range(3)]
            pieces = [maps_ref[:, begin : begin + group_width] for begin in begins]
            own_ref[...] = jnp.concatenate([*pieces, extra_ref[...]], axis=1)

    half = sent_ref.shape[0]
    sent_ref[...] = own_ref[pl.ds(pl.multiple_of(info[1] * half, 16), half)]


def early_rows(info, maps, extra, group_width):
    rows = maps.shape[0]
    columns = 3 * group_width + extra.shape[1]
    shapes = [(rows, columns), (rows // 2, columns)]
    return pl.pallas_call(
        functools.partial(early_kernel, group_width),
        grid_spec=pltpu.PrefetchScalarGridSpec(
            num_scalar_prefetch=1,
            grid=(1,),
            in_specs=[pl.BlockSpec(value.shape, lambda j, info: (0, 0)) for value in (maps, extra)],
            out_specs=[pl.BlockSpec(shape, lambda j, info: (0, 0)) for shape in shapes],
        ),
        out_shape=[jax.ShapeDtypeStruct(shape, BF16) for shape in shapes],
        compiler_params=pltpu.CompilerParams(vmem_limit_bytes=VMEM_BYTES),
    )(info.astype(jnp.int32), maps, extra)


def forward_kernel(scale2, first, last, q_ref, oh_ref, k_ref, v_ref, mk_ref, *rest):
    if not first:
        top_in, acc_in, *rest = rest
    if last:
        out_ref, *low_refs, lse_ref, top_sc, acc_sc = rest
    else:
        top_out, acc_out, top_sc, acc_sc = rest
    step = pl.program_id(1)
    width = k_ref.shape[-1]
    block = min(1024, width)
    pad = jnp.zeros((128 - HD - AUX, q_ref.shape[-1]), BF16)
    query = jnp.concatenate([q_ref[...], oh_ref[...], pad], axis=0)

    @pl.when(step == 0)
    def _():
        if first:
            top_sc[...] = jnp.full_like(top_sc, NEG_LARGE)
            acc_sc[...] = jnp.zeros_like(acc_sc)
        else:
            top_sc[...] = top_in[0]
            acc_sc[...] = acc_in[0]

    top, acc = top_sc[...], acc_sc[...]
    for at in range(0, width, block):
        cut = slice(at, at + block)
        aux = mk_ref[0, :, cut]
        keys = jnp.concatenate([k_ref[0, :, cut], aux, pad[:, :block]], axis=0).T
        scores = jnp.dot(keys, query, preferred_element_type=F32)
        new_top = jnp.maximum(top, jnp.max(scores, axis=0, keepdims=True))
        probs = jnp.exp2((scores - new_top) * scale2).astype(BF16)
        decay = jnp.exp2((top - new_top) * scale2)
        values = jnp.concatenate([v_ref[0, :, cut], aux], axis=0)
        acc = acc * decay + jnp.dot(values, probs, preferred_element_type=F32)
        top = new_top
    top_sc[...], acc_sc[...] = top, acc

    @pl.when(step == pl.num_programs(1) - 1)
    def _():
        if last:
            total = acc[HD + DOCS : HD + DOCS + 1]
            result = acc[:HD] / total
            out_ref[0] = result
            cut = low_refs[0].shape[-1]
            for at, low_ref in enumerate(low_refs):
                low_ref[...] = result[:, at * cut : (at + 1) * cut].astype(BF16)
            lse_ref[0] = top + jnp.log2(total) / scale2
        else:
            top_out[0] = top
            acc_out[0] = acc


def attend(query_t, onehot, pieces, carry, last, scale2, heads):
    count, _, width = pieces.shape
    rows = query_t.shape[1]
    cut = rows // GROUPS
    top_spec = pl.BlockSpec((1, 1, rows), lambda h, j: (h, 0, 0))
    acc_spec = pl.BlockSpec((1, HD + AUX, rows), lambda h, j: (h, 0, 0))
    in_specs = [
        pl.BlockSpec((HD, rows), lambda h, j: (h, 0)),
        pl.BlockSpec((AUX, rows), lambda h, j: (0, 0)),
        pl.BlockSpec((1, HD, width), lambda h, j: (j, h, 0)),
        pl.BlockSpec((1, HD, width), lambda h, j: (j, heads + h, 0)),
        pl.BlockSpec((1, AUX, width), lambda h, j: (j, 2 * heads * HD // AUX, 0)),
    ]
    if carry is not None:
        in_specs += [top_spec, acc_spec]
    top_shape = jax.ShapeDtypeStruct((heads, 1, rows), F32)
    if last:
        out_specs = [
            pl.BlockSpec((1, HD, rows), lambda h, j: (h, 0, 0)),
            *[pl.BlockSpec((HD, cut), lambda h, j: (h, 0))] * GROUPS,
            top_spec,
        ]
        out_shape = [
            jax.ShapeDtypeStruct((heads, HD, rows), F32),
            *[jax.ShapeDtypeStruct((heads * HD, cut), BF16)] * GROUPS,
            top_shape,
        ]
    else:
        out_specs = [top_spec, acc_spec]
        out_shape = [top_shape, jax.ShapeDtypeStruct((heads, HD + AUX, rows), F32)]
    return pl.pallas_call(
        functools.partial(forward_kernel, scale2, carry is None, last),
        grid=(heads, count),
        in_specs=in_specs,
        out_specs=out_specs,
        out_shape=out_shape,
        scratch_shapes=[pltpu.VMEM((1, rows), F32), pltpu.VMEM((HD + AUX, rows), F32)],
        compiler_params=pltpu.CompilerParams(vmem_limit_bytes=VMEM_SHARED),
        cost_estimate=pl.CostEstimate(
            flops=34 * heads * rows * count * width * HD, bytes_accessed=0, transcendentals=0
        ),
    )(query_t, onehot, pieces, pieces, pieces, *(carry or ()))


def split3(value):
    high = value.astype(BF16)
    rest = value - high.astype(F32)
    mid = rest.astype(BF16)
    return high, mid, (rest - mid.astype(F32)).astype(BF16)


def backward_kernel(scale2, first, last, q_ref, oh_ref, g_ref, o_ref, lse_ref, k_ref, v_ref, mk_ref, *rest):
    if not first:
        carry_ref, *rest = rest
    else:
        delta_ref, *rest = rest
    dq_ref, dkv_ref, qa_sc, ga_sc, nat_sc, dq_sc = rest
    step = pl.program_id(1)
    width = k_ref.shape[-1]
    block = width // GROUPS
    rows = q_ref.shape[-1]
    scale = 1.0 / math.sqrt(HD)
    pad = jnp.zeros((128 - HD - AUX, rows), BF16)

    @pl.when(step == 0)
    def _():
        query = q_ref[...]
        grad = jnp.concatenate([g_ref[at] for at in range(g_ref.shape[0])], axis=1)
        if first:
            delta = jnp.sum(grad.astype(F32) * o_ref[0], axis=0, keepdims=True)
            delta_ref[0] = delta
        else:
            delta = o_ref[0]
        place = lax.broadcasted_iota(jnp.int32, (AUX, rows), 0)

        def aux_rows(start, value):
            out = start
            for at, piece in enumerate(split3(-value)):
                out = jnp.where(place == DOCS + at, piece.astype(F32), out)
            return out.astype(BF16)

        qa_sc[...] = jnp.concatenate([query, aux_rows(oh_ref[...].astype(F32), lse_ref[0]), pad], axis=0)
        ga_sc[...] = jnp.concatenate([grad, aux_rows(jnp.zeros((AUX, rows), F32), delta), pad], axis=0)
        nat_sc[...] = jnp.concatenate([grad, query], axis=0).T
        if first:
            dq_sc[...] = jnp.zeros_like(dq_sc)
        else:
            dq_sc[...] = carry_ref[0]

    natural = nat_sc[...]
    for at in range(0, width, block):
        cut = slice(at, at + block)
        aux = mk_ref[0, :, cut]
        keys_t = k_ref[0, :, cut]
        keys = jnp.concatenate([keys_t, aux, pad[:, :block]], axis=0).T
        values = jnp.concatenate([v_ref[0, :, cut], aux, pad[:, :block]], axis=0).T
        probs = jnp.exp2(jnp.dot(keys, qa_sc[...], preferred_element_type=F32) * scale2)
        slopes = jnp.dot(values, ga_sc[...], preferred_element_type=F32)
        grad_scores = (probs * slopes).astype(BF16)
        from_probs = jnp.dot(probs.astype(BF16), natural, preferred_element_type=F32)
        from_scores = jnp.dot(grad_scores, natural, preferred_element_type=F32) * scale
        lane = lax.broadcasted_iota(jnp.int32, from_probs.shape, 1)
        both = jnp.where(lane < HD, from_probs, from_scores).T.astype(BF16)
        dkv_ref[0, at // block, 0] = both[HD:]
        dkv_ref[0, at // block, 1] = both[:HD]
        dq_sc[...] += jnp.dot(keys_t, grad_scores, preferred_element_type=F32)

    @pl.when(step == pl.num_programs(1) - 1)
    def _():
        if last:
            cut = dq_ref.shape[-1]
            for at in range(dq_ref.shape[0]):
                dq_ref[at] = (dq_sc[:, at * cut : (at + 1) * cut] * scale).astype(BF16)
        else:
            dq_ref[0] = dq_sc[...]


def attend_back(query_t, onehot, grad_t, out_heads, lse, pieces, carry, last, scale2, heads):
    count, _, width = pieces.shape
    rows = query_t.shape[1]
    cut = rows // GROUPS
    block = width // GROUPS
    blocks = width // block
    sum_spec = pl.BlockSpec((1, HD, rows), lambda h, j: (h, 0, 0))
    cut_spec = pl.BlockSpec((GROUPS, HD, cut), lambda h, j: (0, h, 0))
    row_spec = pl.BlockSpec((1, 1, rows), lambda h, j: (h, 0, 0))
    in_specs = [
        pl.BlockSpec((HD, rows), lambda h, j: (h, 0)),
        pl.BlockSpec((AUX, rows), lambda h, j: (0, 0)),
        cut_spec,
        sum_spec if carry is None else row_spec,
        row_spec,
        pl.BlockSpec((1, HD, width), lambda h, j: (j, h, 0)),
        pl.BlockSpec((1, HD, width), lambda h, j: (j, heads + h, 0)),
        pl.BlockSpec((1, AUX, width), lambda h, j: (j, 2 * heads * HD // AUX, 0)),
    ]
    if carry is not None:
        in_specs += [sum_spec]
    dq_shape = (GROUPS, heads * HD, cut) if last else (heads, HD, rows)
    return pl.pallas_call(
        functools.partial(backward_kernel, scale2, carry is None, last),
        grid=(heads, count),
        in_specs=in_specs,
        out_specs=([row_spec] if carry is None else [])
        + [
            cut_spec if last else sum_spec,
            pl.BlockSpec((1, blocks, 2, HD, block), lambda h, j: (j, 0, 0, h, 0)),
        ],
        out_shape=([jax.ShapeDtypeStruct((heads, 1, rows), F32)] if carry is None else [])
        + [
            jax.ShapeDtypeStruct(dq_shape, BF16 if last else F32),
            jax.ShapeDtypeStruct((count, blocks, 2, heads * HD, block), BF16),
        ],
        scratch_shapes=[
            pltpu.VMEM((128, rows), BF16),
            pltpu.VMEM((128, rows), BF16),
            pltpu.VMEM((rows, 128), BF16),
            pltpu.VMEM((HD, rows), F32),
        ],
        compiler_params=pltpu.CompilerParams(vmem_limit_bytes=VMEM_SHARED),
        cost_estimate=pl.CostEstimate(
            flops=15 * heads * rows * count * width * HD, bytes_accessed=0, transcendentals=0
        ),
    )(query_t, onehot, grad_t, out_heads, lse, pieces, pieces, pieces, *([] if carry is None else [carry]))


def route_parts(rows, router, columns, expert, expert_count):
    project = jnp.dot(rows, router, preferred_element_type=F32)
    size = jnp.sqrt(jnp.sum(project * project, axis=-1, keepdims=True))
    along = jnp.where(size > FLOOR, 1.0, jnp.where(size == FLOOR, 0.5, 0.0))
    inverse = 1.0 / jnp.maximum(size, FLOOR)
    unit = project * inverse
    logits = jnp.dot(unit, columns, precision=HIGHEST, preferred_element_type=F32) / ROUTER_HEAT
    lane = lax.broadcasted_iota(jnp.int32, logits.shape, 1)
    logits = jnp.where(lane < expert_count, logits, NEG_LARGE)
    raised = jnp.exp(logits - jnp.max(logits, axis=-1, keepdims=True))
    chances = raised / jnp.sum(raised, axis=-1, keepdims=True)
    mine = (lane == expert).astype(F32)
    gate = jnp.sum(chances * mine, axis=-1, keepdims=True)
    return unit, inverse, along, chances, mine, gate


def expert_kernel(first, expert_count, begin, info, x_ref, g_ref, uo_ref, so_ref, router_ref, columns_ref, *rest):
    steps = 3 if first else 1
    if first:
        *ux_refs, sx_ref = rest[: steps + 1]
        rest = rest[steps + 1 :]
    else:
        both_ref, *rest = rest
    if first:
        own_ref, hidden_ref, gp_ref, gw_ref, gm_ref, made_ref, gin_ref, up_sc, down_sc, turned_sc = rest
    else:
        gm_ref, made_in, gin_in, _, _, *rest = rest
        hidden_ref, gp_ref, gw_ref, scaled_ref, back_ref, routed_ref, columns_out, *rest = rest
        up_sc, down_sc, turned_sc, made_ref, gin_ref = rest
    step = pl.program_id(0)
    share, block = uo_ref.shape

    @pl.when(step == 0)
    def _():
        cut = pl.ds(pl.multiple_of((1 - info[0]) * share, 128), share)
        turned_sc[...] = x_ref[:, cut].T
        if first:
            gate = route_parts(x_ref[...], router_ref[...], columns_ref[...], info[1], expert_count)[-1]
            gm_ref[...] = (gate * g_ref[...].astype(F32)).astype(BF16)
            made_ref[...] = jnp.zeros_like(made_ref)
            gin_ref[...] = jnp.zeros_like(gin_ref)
        else:
            made_ref[...] = made_in[...]
            gin_ref[...] = gin_in[...]

    up_sc[pl.ds(pl.multiple_of(info[0] * share, 128), share)] = uo_ref[...]
    other = pl.ds(pl.multiple_of((1 - info[0]) * share, 128), share)
    for now in range(steps):

        @pl.when(step == now)
        def _():
            up_sc[other] = ux_refs[now][...] if first else both_ref[:share]
            if begin + now < 2:
                down_sc[...] = so_ref[...]
            else:
                down_sc[...] = sx_ref[...] if first else both_ref[share:]

    up, down = up_sc[...], down_sc[...]
    piece = x_ref.shape[0] // 2
    for begin_row in (0, piece):
        rows = slice(begin_row, begin_row + piece)
        pre_act = jnp.dot(x_ref[rows], up, preferred_element_type=F32)
        grad_hidden = dot32(gm_ref[rows], down, (((1,), (1,))))
        bell = 0.5 * (1.0 + lax.erf(pre_act * ROOT_HALF))
        hidden = (pre_act * bell).astype(BF16)
        hidden_ref[rows] = hidden
        made_ref[rows] += jnp.dot(hidden, down, preferred_element_type=F32)
        slope = bell + pre_act * (jnp.exp(-0.5 * pre_act * pre_act) * (1.0 / ROOT_TWO_PI))
        grad_pre = (grad_hidden * slope).astype(BF16)
        gp_ref[rows] = grad_pre
        gin_ref[rows] += dot32(grad_pre, up, (((1,), (1,))))
    if first:

        @pl.when(step < 2)
        def _():
            own_ref[...] = hidden_ref[...]

    gw_ref[...] = jnp.dot(turned_sc[...], gp_ref[...], preferred_element_type=F32).astype(BF16)

    if not first:
        router, columns = router_ref[...], columns_ref[...]
        unit, inverse, along, chances, mine, gate = route_parts(x_ref[...], router, columns, info[1], expert_count)
        made = made_ref[...].astype(BF16).astype(F32)
        scaled_ref[...] = (gate * made).astype(BF16)
        grad_gate = jnp.sum(g_ref[...].astype(F32) * made, axis=-1, keepdims=True)
        dlogit = grad_gate * gate * (mine - chances) / ROUTER_HEAT
        dunit = lax.dot_general(
            dlogit, columns, (((1,), (1,)), ((), ())), precision=HIGHEST, preferred_element_type=F32
        )
        dproj = inverse * (dunit - along * unit * jnp.sum(unit * dunit, axis=-1, keepdims=True))
        high = dproj.astype(BF16)
        low = (dproj - high.astype(F32)).astype(BF16)
        back = dot32(high, router, (((1,), (1,)))) + dot32(low, router, (((1,), (1,))))
        back_ref[...] = (gin_ref[...].astype(BF16).astype(F32) + back).astype(BF16)
        rows = x_ref[...]
        routed_ref[...] = jnp.dot(high.astype(F32).T.astype(BF16), rows, preferred_element_type=F32) + jnp.dot(
            low.astype(F32).T.astype(BF16), rows, preferred_element_type=F32
        )
        columns_out[...] = jnp.dot(unit.T, dlogit, precision=HIGHEST, preferred_element_type=F32)


def run_expert(info, rows, grads, widen, shrink, others, routing, carry, expert_count):
    slots, width = rows.shape
    share, units = widen.shape
    block = units // 4
    first = carry is None
    begin = 0 if first else 3

    def at(j, info):
        return lax.rem(2 * info[0] + begin + j, 4)

    whole = pl.BlockSpec((slots, width), lambda j, info: (0, 0))
    quarter = pl.BlockSpec((slots, block), lambda j, info: (0, 0))
    part = jax.ShapeDtypeStruct((slots, units), BF16)
    part_spec = pl.BlockSpec((slots, block), lambda j, info: (0, at(j, info)))
    low = jax.ShapeDtypeStruct((slots, width), BF16)
    full = jax.ShapeDtypeStruct((slots, width), F32)
    fixed = [*routing, *others]
    in_specs = [
        whole,
        whole,
        pl.BlockSpec((share, block), lambda j, info: (0, at(j, info))),
        pl.BlockSpec((block, width), lambda j, info: (jnp.minimum(j, 1), 0)),
        *[pl.BlockSpec(value.shape, lambda j, info: (0, 0)) for value in fixed],
    ]
    operands = [rows, grads, widen, shrink, *fixed]
    scratch = [pltpu.VMEM((width, block), BF16), pltpu.VMEM((block, width), BF16), pltpu.VMEM((share, slots), BF16)]
    sent = jax.ShapeDtypeStruct((share, units), BF16)
    sent_spec = pl.BlockSpec((share, block), lambda j, info: (0, at(j, info)))
    aliases = {}
    if first:
        own = jax.ShapeDtypeStruct((slots, 2 * block), BF16)
        out_specs = [
            pl.BlockSpec((slots, block), lambda j, info: (0, jnp.minimum(j, 1))), quarter, part_spec, sent_spec,
            whole, whole, whole,
        ]
        out_shape = [own, jax.ShapeDtypeStruct((slots, block), BF16), part, sent, low, full, full]
    else:
        grad_pre, widen_sent, grad_made, made, grad_inputs = carry
        in_specs += [whole, whole, whole] + [pl.BlockSpec(memory_space=pl.ANY)] * 2
        operands += [grad_made, made, grad_inputs, grad_pre, widen_sent]
        aliases = {len(operands) - 1: 1, len(operands): 2}
        tops = [jax.ShapeDtypeStruct((128, width), F32), jax.ShapeDtypeStruct((128, 128), F32)]
        out_specs = [quarter, part_spec, sent_spec, whole, whole]
        out_specs += [pl.BlockSpec(v.shape, lambda j, info: (0, 0)) for v in tops]
        out_shape = [jax.ShapeDtypeStruct((slots, block), BF16), part, sent, low, low, *tops]
        scratch += [pltpu.VMEM((slots, width), F32), pltpu.VMEM((slots, width), F32)]
    return pl.pallas_call(
        functools.partial(expert_kernel, first, expert_count, begin),
        grid_spec=pltpu.PrefetchScalarGridSpec(
            num_scalar_prefetch=1,
            grid=(3 if first else 1,),
            in_specs=in_specs,
            out_specs=out_specs,
            scratch_shapes=scratch,
        ),
        out_shape=out_shape,
        input_output_aliases=aliases,
        compiler_params=pltpu.CompilerParams(vmem_limit_bytes=VMEM_BYTES),
        cost_estimate=pl.CostEstimate(
            flops=(2 if first else 1) * slots * width * units, bytes_accessed=0, transcendentals=0
        ),
    )(info.astype(jnp.int32), *operands)


def final_kernel(info, g_ref, c_ref, kept_ref, sent_ref, all_sc):
    all_sc[...] = dot32(g_ref[...].T, c_ref[...], (((1,), (1,)))).astype(BF16)
    count, half = kept_ref.shape[:2]
    for at in range(count):
        for ref, core in ((kept_ref, info[0]), (sent_ref, 1 - info[0])):
            ref[at] = all_sc[pl.ds(pl.multiple_of((2 * at + core) * half, 16), half)]


def final_grads(core, grads, context):
    width = grads.shape[1]
    shape = (GROUPS, width // GROUPS // 2, context.shape[0])
    return pl.pallas_call(
        final_kernel,
        grid_spec=pltpu.PrefetchScalarGridSpec(
            num_scalar_prefetch=1,
            grid=(1,),
            in_specs=[pl.BlockSpec(value.shape, lambda j, info: (0, 0)) for value in (grads, context)],
            out_specs=[pl.BlockSpec(shape, lambda j, info: (0, 0, 0))] * 2,
            scratch_shapes=[pltpu.VMEM((width, context.shape[0]), BF16)],
        ),
        out_shape=[jax.ShapeDtypeStruct(shape, BF16)] * 2,
        compiler_params=pltpu.CompilerParams(vmem_limit_bytes=VMEM_BYTES),
    )(core[None].astype(jnp.int32), grads, context)


def gather_kernel(row, info, dq_ref, own_ref, got_ref, far0_ref, far1_ref, x_ref, w_ref, small_ref, gain_ref, *rest):
    *part_refs, kept_ref, sent_ref, acc_sc, all_sc = rest
    step = pl.program_id(0)
    far = jnp.where(step < GROUPS // 2, far0_ref[0, 0].astype(F32), far1_ref[0, 0].astype(F32))
    grad_kv = (own_ref[0, 0].astype(F32) + got_ref[0, 0].astype(F32) + far).astype(BF16)
    joined = jnp.concatenate([dq_ref[0], grad_kv[0], grad_kv[1]], axis=0)
    product = jnp.dot(joined, x_ref[...], preferred_element_type=F32)
    through = dot32(joined.T, w_ref[...], (((1,), (1,)))).astype(BF16)
    for at in range(GROUPS):

        @pl.when(step == at)
        def _():
            part_refs[at][...] = through
            if at == 0:
                acc_sc[...] = product
            else:
                acc_sc[...] += product

    @pl.when(step == pl.num_programs(0) - 1)
    def _():
        rows = acc_sc.shape[0]
        all_sc[:rows] = acc_sc[...].astype(BF16)
        place = lax.broadcasted_iota(jnp.int32, small_ref.shape, 0)
        all_sc[rows:] = jnp.where(place == row, gain_ref[...], small_ref[...].astype(F32)).astype(BF16)
        half = kept_ref.shape[0]
        kept_ref[...] = all_sc[pl.ds(pl.multiple_of(info[0] * half, 16), half)]
        sent_ref[...] = all_sc[pl.ds(pl.multiple_of((1 - info[0]) * half, 16), half)]


def gather_grads(core, grad_query, near_own, near_got, far, far_last, normed, maps, small, gain_grad, row):
    group_width, cut = grad_query.shape[1:]
    width = maps.shape[0]
    half = GROUPS // 2
    rows = 3 * group_width
    total = rows + small.shape[0]
    piece = (1, 1, 2, group_width, cut)

    def fixed(shape):
        return pl.BlockSpec(shape, lambda j, info: (0, 0))

    return pl.pallas_call(
        functools.partial(gather_kernel, row),
        grid_spec=pltpu.PrefetchScalarGridSpec(
            num_scalar_prefetch=1,
            grid=(GROUPS,),
            in_specs=[
                pl.BlockSpec((1, group_width, cut), lambda j, info: (j, 0, 0)),
                pl.BlockSpec(piece, lambda j, info: (0, j, 0, 0, 0)),
                pl.BlockSpec(piece, lambda j, info: (0, j, 0, 0, 0)),
                pl.BlockSpec(piece, lambda j, info: (0, jnp.minimum(j, half - 1), 0, 0, 0)),
                pl.BlockSpec(piece, lambda j, info: (0, jnp.maximum(j - half, 0), 0, 0, 0)),
                pl.BlockSpec((cut, width), lambda j, info: (j, 0)),
                fixed(maps.shape),
                fixed(small.shape),
                fixed((1, width)),
            ],
            out_specs=[fixed((cut, width))] * GROUPS + [fixed((total // 2, width))] * 2,
            scratch_shapes=[pltpu.VMEM((rows, width), F32), pltpu.VMEM((total, width), BF16)],
        ),
        out_shape=[jax.ShapeDtypeStruct((cut, width), BF16)] * GROUPS
        + [jax.ShapeDtypeStruct((total // 2, width), BF16)] * 2,
        compiler_params=pltpu.CompilerParams(vmem_limit_bytes=VMEM_SHARED),
        cost_estimate=pl.CostEstimate(flops=16 * group_width * GROUPS * cut * width, bytes_accessed=0, transcendentals=0),
    )(
        core[None].astype(jnp.int32), grad_query, near_own, near_got, far, far_last, normed, maps, small, gain_grad[None]
    )


def finish_kernel(
    group_width, info, own_ref, got_ref, w_ref, gain_ref, maps_ref, final_ref, router_ref, embed_ref, ln1_ref, ln2_ref,
    v_ref,
):
    final_half = group_width // 2
    part = own_ref.shape[1]
    half = 2 * part - final_half
    for ref, core in ((own_ref, info[1]), (got_ref, 1 - info[1])):
        low_rows = pl.ds(pl.multiple_of(core * half, 16), part)
        high_rows = pl.ds(pl.multiple_of(core * half + part, 16), half - part)
        final_rows = pl.ds(pl.multiple_of(2 * half + core * final_half, 16), final_half)
        for k in range(GROUPS):
            v_ref[k, low_rows] = ref[k + GROUPS * info[2]]
            high = ref[k + GROUPS * (1 - info[2])]
            v_ref[k, high_rows] = high[: half - part]
            v_ref[k, final_rows] = high[half - part :]

    def columns(pair, begin):
        rows = pl.ds(begin, group_width)
        halves = [v_ref[lax.rem(2 * pair + k + GROUPS - info[0], GROUPS), rows] for k in range(2)]
        return jnp.concatenate(halves, axis=0).astype(F32).T

    total = 0.0
    for part in range(3):
        for pair in range(GROUPS // 2):
            value = columns(pair, part * group_width)
            at = (part * GROUPS + 2 * pair) * group_width
            cut = slice(at, at + 2 * group_width)
            maps_ref[:, cut] = value
            total = total + jnp.sum(value * w_ref[:, cut].astype(F32), axis=1, keepdims=True)
    for pair in range(GROUPS // 2):
        at = 2 * pair * group_width
        final_ref[:, at : at + 2 * group_width] = columns(pair, 2 * half)
    small = sum(v_ref[k, 3 * group_width : 2 * half].astype(F32) for k in range(GROUPS))
    route, embed = router_ref.shape[0], embed_ref.shape[0]
    rows = small.shape[1]
    router_ref[...] = small[:route]
    embed_ref[...] = small[route : route + embed, : embed_ref.shape[1]]
    ln2_ref[...] = small[route + embed]
    ln1_ref[...] = (jnp.broadcast_to(total, (rows, 128)).T[:1] / gain_ref[...].astype(F32))[0]


def finish_shared(own, got, weights, gain, info, group_width, route, embed_shape):
    rows, columns = weights.shape
    shapes = [(rows, columns), (rows, GROUPS * group_width), (route, rows), embed_shape, (rows,), (rows,)]
    return pl.pallas_call(
        functools.partial(finish_kernel, group_width),
        grid_spec=pltpu.PrefetchScalarGridSpec(
            num_scalar_prefetch=1,
            grid=(1,),
            in_specs=[
                pl.BlockSpec(own.shape, lambda j, info: (0, 0, 0)),
                pl.BlockSpec(got.shape, lambda j, info: (0, 0, 0)),
                pl.BlockSpec(weights.shape, lambda j, info: (0, 0)),
                pl.BlockSpec((1, rows), lambda j, info: (0, 0)),
            ],
            out_specs=[pl.BlockSpec(shape, lambda j, info, rank=len(shape): (0,) * rank) for shape in shapes],
            scratch_shapes=[pltpu.VMEM((GROUPS, 4 * own.shape[1], rows), BF16)],
        ),
        out_shape=[jax.ShapeDtypeStruct(shape, F32) for shape in shapes],
        compiler_params=pltpu.CompilerParams(vmem_limit_bytes=VMEM_SHARED),
    )(info.astype(jnp.int32), own, got, weights, gain[None])


def norm_parts(values):
    center = values - jnp.mean(values, axis=-1, keepdims=True)
    scale = lax.rsqrt(jnp.mean(center * center, axis=-1, keepdims=True) + EPSILON)
    return center * scale, scale


def norm_back(unit, scale, scaled_grad):
    along = jnp.mean(scaled_grad * unit, axis=-1, keepdims=True)
    return scale * (scaled_grad - jnp.mean(scaled_grad, axis=-1, keepdims=True) - unit * along)


def unit_of(vectors, axis):
    size = jnp.sqrt(jnp.sum(vectors * vectors, axis=axis, keepdims=True))
    share = jnp.where(size > FLOOR, 1.0, jnp.where(size == FLOOR, 0.5, 0.0))
    inverse = 1.0 / jnp.maximum(size, FLOOR)
    return vectors * inverse, inverse, share


def unit_back(unit, inverse, share, grad, axis):
    return inverse * (grad - share * unit * jnp.sum(unit * grad, axis=axis, keepdims=True))


def shift(value, axis, size, by):
    return lax.ppermute(value, axis, [(at, (at + by) % size) for at in range(size)])


def flip(value, axis, size, bit):
    return lax.ppermute(value, axis, [(at, at ^ bit) for at in range(size)])


def after(value, *others):
    return lax.optimization_barrier((value, *others))[0]


def line_gather(value, axis, size, tied):
    upward, downward, from_low, from_high = value, value, [], []
    for hop in range(size - 1):
        upward = tied(hop, upward)
        upward = lax.ppermute(upward, axis, [(at, at + 1) for at in range(hop, size - 1)])
        downward = lax.ppermute(downward, axis, [(at, at - 1) for at in range(size - 1 - hop, 0, -1)])
        from_low.append(upward)
        from_high.append(downward)
    return [value] + [from_low[k] + from_high[size - 2 - k] for k in range(size - 1)]


def roll_blocks(blocks, start):
    return lax.dynamic_slice_in_dim(jnp.concatenate([blocks, blocks], axis=0), start, blocks.shape[0], 0)


def pair_order(own, other, at):
    return jnp.where(at == 0, jnp.concatenate([own, other], 0), jnp.concatenate([other, own], 0))


def body(
    ctx_count,
    fsdp_count,
    incoming_sequence,
    mixer_scaling_factor,
    asker_lookup_content_maps,
    mixer_final_map,
    specialist_scaling_factor,
    dispatch_space_map,
    specialist_dispatch_vectors,
    specialist_widen_weights_pair,
    specialist_shrink_weights_pair,
    document_labels,
    piece_specialist_choice,
    result_cotangent_array,
):
    row_count = incoming_sequence.shape[1]
    width = incoming_sequence.shape[2]
    head_count = width // HD
    heads = head_count // GROUPS
    group_width = heads * HD
    ring = ctx_count // GROUPS
    bits = ring.bit_length() - 1
    scale2 = LOG2E / math.sqrt(HD)
    z_at = lax.axis_index("z")
    r_at = lax.axis_index("r")
    f_at = lax.axis_index("fsdp")
    core = r_at & 1
    expert_at = z_at * ring + r_at
    share = width // fsdp_count
    capacity = max(2, 2 * row_count // ctx_count)
    slots = ctx_count * capacity

    def swap(value):
        return flip(value, "fsdp", fsdp_count, 1)

    def across(value, bit):
        return flip(value, "r", ring, bit)

    def exchange_slots(rows):
        return lax.all_to_all(
            rows.reshape(ctx_count, capacity, -1), ("z", "r"), split_axis=0, concat_axis=0, tiled=True
        ).reshape(slots, -1)

    def both_cores(got):
        return pair_order(got, across(got, 1), core)

    def halve(value, axis, flag, send):
        half = value.shape[axis] // 2
        kept = lax.dynamic_slice_in_dim(value, flag * half, half, axis)
        sent = lax.dynamic_slice_in_dim(value, (1 - flag) * half, half, axis)
        return (kept.astype(F32) + send(sent).astype(F32)).astype(BF16)

    def by_fsdp(own, other, axis):
        return jnp.where(
            f_at == 0,
            jnp.concatenate([own, other], axis=axis),
            jnp.concatenate([other, own], axis=axis),
        )

    route, experts = specialist_dispatch_vectors.shape[0] * fsdp_count, specialist_dispatch_vectors.shape[1]
    embed_share = route // fsdp_count
    extras = [
        mixer_scaling_factor[:, None],
        specialist_scaling_factor[:, None],
        dispatch_space_map,
        jnp.pad(specialist_dispatch_vectors, ((0, share - embed_share), (0, 0))),
    ]
    edges = [0, 3 * group_width]
    for value in extras:
        edges.append(edges[-1] + value.shape[1])
    extras.append(jnp.zeros((share, -edges[-1] % 128), BF16))
    early_own, early_sent = early_rows(
        jnp.stack([z_at, core]), asker_lookup_content_maps, jnp.concatenate(extras, axis=1), group_width
    )
    half = share // 2
    final_sent = lax.dynamic_slice_in_dim(mixer_final_map, core * half, half, 0)

    widen = specialist_widen_weights_pair[0]
    shrink_own = specialist_shrink_weights_pair[0]
    half_ff = shrink_own.shape[0]
    part_ff = half_ff // 2
    eighth = half_ff // 4
    early_pieces = []

    def widen_piece(which, at, *others):
        return lax.dynamic_slice_in_dim(after(widen, *others), (which * 2 + at) * part_ff, part_ff, 1)

    def tie(value, pieces, at):
        value, pieces[at] = lax.optimization_barrier((value, pieces[at]))
        return value

    def hop_tie(hop, value):
        if hop == 1:
            value, *sent = lax.optimization_barrier((value, early_sent, final_sent))
            early_pieces.extend([swap(piece) for piece in sent])
        return value

    x_own = incoming_sequence[0]
    label_rows = jnp.zeros((8, width), BF16).at[0, :row_count].set(document_labels[0].astype(BF16))
    blocks = line_gather(jnp.concatenate([x_own, label_rows], axis=0), "z", GROUPS, hop_tie)
    x_all = jnp.concatenate([piece[:row_count] for piece in blocks], axis=0)
    labels = jnp.concatenate([piece[row_count, :row_count] for piece in blocks], axis=0)

    widen_near = [swap(widen_piece(1 - f_at, at, *early_pieces)) for at in range(2)]
    widen_far = [swap(widen_piece(f_at, 0, *early_pieces))]
    widen_last = widen_piece(f_at, 1, *early_pieces)
    early_full = pair_order(early_own, both_cores(early_pieces[0]), f_at)
    maps_group, gain_in, gain_mid, router, embed = (
        early_full[:, begin:end] for begin, end in zip(edges[:-1], edges[1:])
    )
    gain_in, gain_mid = gain_in[:, 0].astype(F32), gain_mid[:, 0].astype(F32)
    embed = embed.reshape(fsdp_count, share, experts)[:, :embed_share].reshape(route, experts).astype(F32)
    final_map = roll_blocks(
        pair_order(mixer_final_map, both_cores(early_pieces[1]), f_at).reshape(GROUPS, group_width, width), z_at
    ).reshape(width, width)

    picked = piece_specialist_choice[0, :, 0]
    hits = (picked[:, None] == jnp.arange(ctx_count, dtype=jnp.int32)[None, :]).astype(jnp.int32)
    slot_rank = jnp.sum(jnp.cumsum(hits, axis=0) * hits, axis=1) - 1
    slot_index = picked * capacity + slot_rank
    place = (jnp.arange(slots, dtype=jnp.int32)[:, None] == slot_index[None, :]).astype(BF16)
    cotangent = result_cotangent_array[0]

    def to_slots(values):
        return jnp.dot(place, values, preferred_element_type=F32).astype(BF16)

    x_all = tie(x_all, widen_near, 0)
    x_all, final_map, grad_rows = lax.optimization_barrier((x_all, final_map, to_slots(cotangent)))
    unit_all, _ = norm_parts(x_all.astype(F32))
    normed_low = (unit_all * gain_in).astype(BF16)
    joined_t = dot32(maps_group, normed_low, (((0,), (1,)))).astype(BF16)
    aux_at = jnp.arange(AUX, dtype=jnp.int32)[:, None]
    same = labels.astype(jnp.int32)[None, :] == aux_at
    onehot = same.astype(BF16)
    key_aux = jnp.where(
        aux_at < DOCS, jnp.where(same, 0.0, NEG_LARGE), jnp.where(aux_at < DOCS + 3, 1.0, 0.0)
    ).astype(BF16)
    own_piece = jnp.concatenate([joined_t[group_width:], key_aux], axis=0)[None]
    even = own_piece
    for bit in range(bits - 1, 0, -1):
        even = jnp.stack([even, across(even, 1 << bit)], axis=1).reshape(-1, *own_piece.shape[1:])
    even = even[1:]
    last_sent = jnp.concatenate([widen_last, after(shrink_own, own_piece)[part_ff:]], axis=0)
    peer_piece, *shrink_sent = lax.optimization_barrier(
        (across(own_piece, 1), after(shrink_own, own_piece)[:part_ff], last_sent)
    )
    shrink_other = [swap(shrink_sent[0])]
    last_other = swap(shrink_sent[1])
    carry = attend(joined_t, onehot, own_piece, None, False, scale2, heads)
    carry = attend(joined_t, onehot, peer_piece, carry, False, scale2, heads)
    even = tie(tie(after(even, carry[0]), widen_near, 1), widen_far, 0)
    odd = across(even, 1)
    carry = attend(joined_t, onehot, even, carry, False, scale2, heads)
    grad_slots = exchange_slots(after(grad_rows, peer_piece))
    odd, grad_slots = lax.optimization_barrier((odd, grad_slots))
    out_heads, *out_low, lse = attend(joined_t, onehot, odd, carry, True, scale2, heads)
    context_t = jnp.concatenate(
        [out_low[0]] + [shift(out_low[k], "z", GROUPS, -k) for k in range(1, GROUPS)], axis=0
    )

    context_t = tie(context_t, shrink_other, 0)
    x32 = x_own.astype(F32)
    residual = x32 + dot32(context_t, final_map, (((0,), (0,))))
    unit_mid, scale_mid = norm_parts(residual)
    mid_low = (unit_mid * gain_mid).astype(BF16)
    def from_slots(values):
        return dot32(place, values, (((0,), (0,))))

    sent_rows = to_slots(mid_low)
    arrived = exchange_slots(sent_rows)
    context_rows = roll_blocks(
        context_t.reshape(GROUPS, group_width, row_count), (GROUPS - z_at) % GROUPS
    ).reshape(width, row_count)
    arrived, far_pieces, context_rows = lax.optimization_barrier(
        (arrived, jnp.concatenate([odd, even], axis=0), context_rows)
    )

    unit_columns, inverse_columns, share_columns = unit_of(embed, 0)
    routing = (
        jnp.pad(router, ((0, 0), (0, 128 - route))),
        jnp.pad(unit_columns, ((0, 128 - route), (0, 128 - experts))),
    )

    expert_info = jnp.stack([f_at, expert_at])
    hidden_own, hidden_third, *carry = run_expert(
        expert_info, arrived, grad_slots, widen, shrink_own, [*widen_near, *widen_far, *shrink_other], routing, None, experts
    )
    grad_made = carry[2]
    hidden_last, grad_pre, widen_sent, scaled, sent_back, routed_grad, columns_grad = run_expert(
        expert_info, arrived, grad_slots, widen, shrink_own, [last_other], routing, carry, experts
    )
    grad_back = exchange_slots(sent_back)

    arrived, hidden_own, hidden_third, hidden_last, grad_made, _ = lax.optimization_barrier(
        (arrived, hidden_own, hidden_third, hidden_last, grad_made, sent_back)
    )
    first, second = arrived[:, :share], arrived[:, share:]
    rows_own = jnp.where(f_at == 0, first, second)
    widen_back = swap(widen_sent)
    shrink_back = [
        dot32(value, grad_made, (((0,), (0,)))).astype(BF16)
        for value in (hidden_third, hidden_last)
    ]
    grad_router_own, grad_columns = routed_grad[:route], columns_grad[:route, :experts]
    grad_embed_own = unit_back(unit_columns, inverse_columns, share_columns, grad_columns, 0)
    embed_rows = jnp.pad(
        grad_embed_own.reshape(fsdp_count, embed_share, experts), ((0, 0), (0, 0), (0, share - experts))
    )
    small = jnp.concatenate(
        [
            grad_router_own,
            jnp.concatenate([embed_rows[at] for at in range(fsdp_count)], axis=1),
            jnp.zeros((SMALL - route - embed_share, width), F32),
        ],
        axis=0,
    ).astype(BF16)
    grad_back, small, *shrink_back = lax.optimization_barrier((grad_back, small, *shrink_back))
    shrink_back[0] = swap(shrink_back[0])

    grad_mid = from_slots(grad_back)
    grad_residual = cotangent.astype(F32) + norm_back(unit_mid, scale_mid, grad_mid * gain_mid)
    grad_gain_mid = jnp.sum(grad_mid * unit_mid, axis=0)
    grad_res_low = grad_residual.astype(BF16)
    grad_context = dot32(final_map, grad_res_low, (((1,), (1,)))).astype(BF16).reshape(
        GROUPS, group_width, row_count
    )
    grad_parts = [grad_context[0]] + [shift(grad_context[k], "z", GROUPS, k) for k in range(1, GROUPS)]
    grad_t = jnp.stack(grad_parts)

    def back(piece, running, last=False, ties=()):
        tied = lax.optimization_barrier((grad_t, *ties))
        rows = out_heads if running is None else delta
        result = attend_back(joined_t, onehot, tied[0], rows, lse, piece, running, last, scale2, heads)
        return (*result, *tied[1:])

    scaled_back = exchange_slots(after(scaled, grad_parts[1], grad_parts[3]))
    delta, running, far_both = back(far_pieces, None)
    far_odd, far_even = far_both[: odd.shape[0]], far_both[odd.shape[0] :]
    final_kept, final_sent = final_grads(core, after(grad_res_low, running), context_rows)
    final_got = across(final_sent, 1)
    finals = (final_kept.astype(F32) + final_got.astype(F32)).astype(BF16)
    finals = lax.all_to_all(finals, "z", split_axis=0, concat_axis=0, tiled=True)
    far_got = across(far_odd, 1)
    cut = far_even.shape[1] // 2

    def far_sum(part):
        return (far_even[:, part].astype(F32) + far_got[:, part].astype(F32)).astype(BF16)

    def add_far(value):
        if bits == 2:
            return across(value, 2)
        value = jnp.concatenate([jnp.zeros_like(value[:1]), value], axis=0)
        for bit in range(1, bits):
            halves = value.reshape(-1, 2, *value.shape[1:])
            value = (halves[:, 0].astype(F32) + across(halves[:, 1], 1 << bit).astype(F32)).astype(BF16)
        return value

    far, far_last = far_sum(slice(0, cut)), far_sum(slice(cut, None))
    running, near_peer, far, far_last = back(peer_piece, running, ties=(far, far_last))
    far = add_far(far)
    far_last = add_far(after(far_last, running))
    grad_query, near_own, far, scaled_back, widen_back = back(
        own_piece, running, True, ties=(far, scaled_back, widen_back)
    )

    *grad_parts, kept, sent = gather_grads(
        core, grad_query, near_own, across(near_peer, 1), far, far_last, normed_low, maps_group, small, grad_gain_mid,
        route + embed_share,
    )
    second_part = shift(grad_parts[2], "z", GROUPS, -2)
    grad_maps_part = (kept.astype(F32) + across(sent, 1).astype(F32)).astype(BF16)
    finals = after(finals, kept)
    final_rows = sum(finals[at].astype(F32) for at in range(GROUPS)).astype(BF16)
    grad_maps_part = jnp.concatenate([grad_maps_part, final_rows], axis=0)
    out = residual + from_slots(after(scaled_back, kept))
    x_at = (r_at >> 1) & 1
    if bits == 2:
        half_rows = grad_maps_part.shape[0] // 2

        def piece(x_bit, f_bit):
            return lax.dynamic_slice(grad_maps_part, (x_bit * half_rows, f_bit * share), (half_rows, share))

        corner = [
            (r * fsdp_count + f, (r ^ 2) * fsdp_count + (1 - f)) for r in range(ring) for f in range(fsdp_count)
        ]
        pieces = [
            piece(x_at, f_at),
            across(piece(1 - x_at, f_at), 2),
            swap(piece(x_at, 1 - f_at)),
            lax.ppermute(piece(1 - x_at, 1 - f_at), ("r", "fsdp"), corner),
        ]
        grad_maps_part = sum(value.astype(F32) for value in pieces).astype(BF16)
    else:
        for bit in range(1, bits):
            grad_maps_part = halve(grad_maps_part, 0, (r_at >> bit) & 1, lambda v: across(v, 1 << bit))
        grad_maps_part = halve(grad_maps_part, 1, f_at, swap)
    grad_maps_part, second_part, shrink_back[0] = lax.optimization_barrier((grad_maps_part, second_part, shrink_back[0]))
    shrink_back[1] = swap(after(shrink_back[1], grad_maps_part))
    groups = [grad_maps_part] + [shift(grad_maps_part, "z", GROUPS, -k) for k in (1, 2, 3)]
    first_part = shift(after(grad_parts[1], *groups), "z", GROUPS, -1)
    third_part = shift(after(grad_parts[3], *groups), "z", GROUPS, -3)
    if bits == 2:
        both = jnp.stack([*groups, *[across(value, 2) for value in groups]])
    else:
        both = jnp.stack(groups)
        for bit in range(bits - 1, 0, -1):
            got = across(both, 1 << bit)
            both = jnp.where(
                (r_at >> bit) & 1 == 0,
                jnp.concatenate([both, got], axis=1),
                jnp.concatenate([got, both], axis=1),
            )
        both = jnp.concatenate(jnp.split(both, 2, axis=1), axis=0)
        x_at = jnp.zeros_like(x_at)
    grad_up = dot32(rows_own, grad_pre, (((0,), (0,)))) + after(widen_back, grad_maps_part).astype(F32)
    grad_down = dot32(hidden_own, grad_made, (((0,), (0,)))) + jnp.concatenate(
        shrink_back, axis=0
    ).astype(F32)
    both, first_part, third_part, grad_up, grad_down = lax.optimization_barrier(
        (both, first_part, third_part, grad_up, grad_down)
    )
    grad_maps, grad_final, grad_router, grad_embed, grad_ln1, grad_ln2 = finish_shared(
        both, across(both, 1), asker_lookup_content_maps, mixer_scaling_factor, jnp.stack([z_at, core, x_at]),
        group_width, route, (embed_share, experts),
    )
    grad_router = grad_router.T

    grad_normed_in = sum(part.astype(F32) for part in (grad_parts[0], first_part, second_part, third_part))
    unit_in, scale_in = norm_parts(after(x_own, kept).astype(F32))
    grad_input = grad_residual + norm_back(unit_in, scale_in, grad_normed_in * gain_in)

    return (
        out[None].astype(BF16),
        grad_input[None],
        grad_ln1,
        grad_maps,
        grad_final,
        grad_ln2,
        grad_router,
        grad_embed,
        grad_up[None],
        grad_down[None],
    )


def solution(mesh):
    ctx_count, fsdp_count = mesh.shape["ctx"], mesh.shape["fsdp"]
    inner = Mesh(mesh.devices.reshape(GROUPS, ctx_count // GROUPS, fsdp_count), ("z", "r", "fsdp"))
    ctx = ("z", "r")
    tokens = P("fsdp", ctx, None)
    expert = P(ctx, "fsdp", None)
    halves, halves2 = P("fsdp"), P("fsdp", None)
    return jax.shard_map(
        functools.partial(body, ctx_count, fsdp_count),
        mesh=inner,
        in_specs=(
            tokens, halves, halves2, halves2, halves, halves2, halves2, expert, expert,
            P("fsdp", ctx), tokens, tokens,
        ),
        out_specs=(
            tokens, tokens, halves, halves2, halves2, halves, halves2, halves2, expert, expert,
        ),
        check_vma=False,
    )
```
